32 devices in a mesh: dp: 8 (over z, x), seq: 4 (over y, core).
Axes of the slice: x: 2, y: 2, z: 4, core: 2. Of those that a mesh axis runs over, the one named last changes fastest.
Arguments:
- passages: bfloat16 [32, 512, 768], P('dp', 'seq'), may hold values from -6 to 6
- lengths: int32 [32], P('dp'), may hold values from 32 to 512, as said below
- attn_gain: float32 [768], replicated, may hold values from 0.5 to 1.5
- w_query: bfloat16 [768, 768], P('dp'), may hold values from -0.0546875 to 0.0546875
- w_key: bfloat16 [768, 768], P('dp'), may hold values from -0.21875 to 0.21875
- w_value: bfloat16 [768, 768], P('dp'), may hold values from -0.21875 to 0.21875
- w_attn_out: bfloat16 [768, 768], P('dp'), may hold values from -0.625 to 0.625
- bias_table: float32 [32, 12], replicated, may hold values from -4 to 4
- ffn_gain: float32 [768], replicated, may hold values from 0.5 to 1.5
- w_in: bfloat16 [768, 3072], P('dp'), may hold values from -0.21875 to 0.21875
- w_ff_out: bfloat16 [3072, 768], P('dp'), may hold values from -0.109375 to 0.109375
- cotangent: bfloat16 [32, 512, 768], P('dp', 'seq'), may hold values from -6 to 6
Outputs:
- layer_out: bfloat16 [32, 512, 768], P('dp', 'seq')
- pooled: float32 [32, 768], P('dp')
- grad_passages: bfloat16 [32, 512, 768], P('dp', 'seq')
- grad_attn_gain: float32 [768], replicated
- grad_w_query: float32 [768, 768], P('dp')
- grad_w_key: float32 [768, 768], P('dp')
- grad_w_value: float32 [768, 768], P('dp')
- grad_w_attn_out: float32 [768, 768], P('dp')
- grad_bias_table: float32 [32, 12], replicated
- grad_ffn_gain: float32 [768], replicated
- grad_w_in: float32 [768, 3072], P('dp')
- grad_w_ff_out: float32 [3072, 768], P('dp')
The draws below stay inside these ranges and needn't reach their ends.
Inputs may be any that keep to these rules, and one draw needn't show every extreme that they name: `lengths`: among the 4 passages of each index of dp (aligned blocks of 4 passages) one has exactly 512 tokens.
All inputs are finite; a program needn't handle non-finite values.
Results may differ from the reference program's by a relative error of at most 0.018.
Values may be sent and summed in bfloat16 or wider, within the bound.
A program may use at most 192 MiB of HBM per device.

```python
import math
import jax
import jax.numpy as jnp
from jax import lax

D = 768
HEADS = 12
FF = 3072
BUCKETS = 32
MAXDIST = 128
LENGTH = 512
PAS_DEV = 4
PASSAGES = 32


def draw_lengths(key, part):
    key = jax.random.fold_in(key, 11)
    first_key, second_key = jax.random.split(key)
    drawn = jax.random.randint(first_key, (PASSAGES // PAS_DEV, PAS_DEV), LENGTH // 16, LENGTH + 1, dtype=jnp.int32)
    chosen = jax.random.randint(second_key, (PASSAGES // PAS_DEV, 1), 0, PAS_DEV, dtype=jnp.int32)
    slots = jnp.arange(PAS_DEV, dtype=jnp.int32)[None, :] == chosen
    return jnp.where(slots, LENGTH, drawn).reshape(PASSAGES).astype(jnp.int32)


def levels(stream_key, extent, cuts, smallest, largest):
    def one(axis_at, blocks):
        draws = jax.random.uniform(jax.random.fold_in(jax.random.fold_in(stream_key, 6), axis_at), (blocks,), jnp.float32, smallest / len(cuts), largest / len(cuts))
        return jnp.repeat(jnp.exp(draws), extent[axis_at] // blocks).reshape((-1,) + (1,) * (len(extent) - axis_at - 1))

    gain = one(*cuts[0])
    for cut in cuts[1:]:
        gain = gain * one(*cut)
    return gain


def gaussian(rng, shape, deviation, most, cuts=(), kind=jnp.bfloat16):
    values = deviation * jax.random.normal(rng, shape, jnp.float32)
    if cuts:
        values = values * levels(rng, shape, cuts, -0.22, 0.18)
    return jnp.clip(values, -most, most).astype(kind)


def setup_inputs(seed: int = 0) -> dict:
    key_of = jax.random.split(jax.random.key(seed), 13)
    passages = gaussian(key_of[0], (PASSAGES, LENGTH, D), 1.0, 6.0, ((0, 8), (1, 4)))
    lengths = draw_lengths(jax.random.fold_in(key_of[12], 71), 0)
    attn_gain = jnp.clip(1.0 + 0.1 * jax.random.normal(key_of[2], (D,), jnp.float32), 0.5, 1.5)
    w_query = gaussian(key_of[3], (D, D), (D * 16) ** -0.5, 0.0546875, ((0, 8),))
    w_key = gaussian(key_of[4], (D, D), D ** -0.5, 0.21875, ((0, 8),))
    w_value = gaussian(key_of[5], (D, D), D ** -0.5, 0.21875, ((0, 8),))
    w_attn_out = gaussian(key_of[6], (D, D), (D // 8) ** -0.5, 0.625, ((0, 8),))
    bias_table = gaussian(key_of[7], (BUCKETS, HEADS), 1.0, 4.0, (), jnp.float32)
    ffn_gain = jnp.clip(1.0 + 0.1 * jax.random.normal(key_of[8], (D,), jnp.float32), 0.5, 1.5)
    w_in = gaussian(key_of[9], (D, FF), D ** -0.5, 0.21875, ((0, 8),))
    w_ff_out = gaussian(key_of[10], (FF, D), FF ** -0.5, 0.109375, ((0, 8),))
    cotangent = gaussian(key_of[11], (PASSAGES, LENGTH, D), 1.0, 6.0, ((0, 8), (1, 4)))
    return dict(passages=passages, lengths=lengths, attn_gain=attn_gain, w_query=w_query, w_key=w_key, w_value=w_value, w_attn_out=w_attn_out, bias_table=bias_table, ffn_gain=ffn_gain, w_in=w_in, w_ff_out=w_ff_out, cotangent=cotangent)


EPS = 1e-06
HIGH = lax.Precision.HIGHEST
FLOOR = -1e+30

@jax.custom_vjp
def low(v):
    return lax.optimization_barrier(v.astype(jnp.bfloat16)).astype(jnp.float32)

@jax.custom_vjp
def low_back(v):
    return v

def low_keep(v):
    return (low(v), None)

def low_pass(kept, grad):
    return (grad,)

def back_keep(v):
    return (v, None)

def back_low(kept, grad):
    return (low(grad),)
low.defvjp(low_keep, low_pass)
low_back.defvjp(back_keep, back_low)

def bucket_index(relative, buckets, reach):
    half_count = buckets // 2
    exact_count = half_count // 2
    distance = jnp.abs(relative)
    result = jnp.minimum(distance, exact_count)
    for power in range(1, half_count - exact_count):
        bound_at = math.ceil(exact_count * (reach / exact_count) ** (power / (half_count - exact_count)) - 1e-06)
        result = result + (distance >= bound_at).astype(jnp.int32)
    return result + (relative > 0).astype(jnp.int32) * half_count

def rms_norm(values, gain_vec):
    return values * lax.rsqrt(lax.optimization_barrier(jnp.mean(values * values, axis=-1, keepdims=True)) + EPS) * gain_vec

def forward(values, weights, mask, index):
    attn_gain, w_query, w_key, w_value, w_attn_out, bias_table, ffn_gain, w_in, w_ff_out = weights
    groups, length, model_width = values.shape
    head_count = bias_table.shape[1]
    normed = low(rms_norm(values, attn_gain))

    def project(matrix):
        rows = jnp.einsum('gld,de->gle', normed, matrix, precision=HIGH)
        return low_back(low(rows)).reshape(groups, length, head_count, -1)
    query_rows = project(w_query)
    key_rows = project(w_key)
    value_rows = project(w_value)
    bias_rows = jnp.transpose(bias_table[index], (2, 0, 1))
    scores = low_back(jnp.einsum('gqhe,gkhe->ghqk', query_rows, key_rows, precision=HIGH) + bias_rows[None])
    masked = jnp.where(mask[:, None, None, :], scores, FLOOR)
    attn_probs = jax.nn.softmax(masked, axis=-1)
    mixed_rows = jnp.einsum('ghqk,gkhe->gqhe', low(attn_probs), value_rows, precision=HIGH)
    mixed_rows = low_back(low(mixed_rows)).reshape(groups, length, model_width)
    hidden = values + low_back(jnp.einsum('gle,ed->gld', mixed_rows, w_attn_out, precision=HIGH))
    normed_ffn = low(rms_norm(hidden, ffn_gain))
    up_rows = low_back(jnp.einsum('gld,df->glf', normed_ffn, w_in, precision=HIGH))
    activated = low(jax.nn.gelu(up_rows))
    return hidden + low_back(jnp.einsum('glf,fd->gld', activated, w_ff_out, precision=HIGH))

def reference(passages, lengths, attn_gain, w_query, w_key, w_value, w_attn_out, bias_table, ffn_gain, w_in, w_ff_out, cotangent):
    group_size = math.gcd(PASSAGES, max(1, 4096 // LENGTH))
    group_count = PASSAGES // group_size
    params = tuple((item.astype(jnp.float32) for item in (attn_gain, w_query, w_key, w_value, w_attn_out, bias_table, ffn_gain, w_in, w_ff_out)))
    inputs = passages.astype(jnp.float32).reshape(group_count, group_size, LENGTH, D)
    grad_in = cotangent.astype(jnp.float32).reshape(group_count, group_size, LENGTH, D)
    positions = jnp.arange(LENGTH, dtype=jnp.int32)
    valid = (positions[None, :] < lengths[:, None]).reshape(group_count, group_size, LENGTH)
    index = bucket_index(positions[None, :] - positions[:, None], BUCKETS, MAXDIST)

    def one_group(totals, pieces):
        block, grad_block, mask = pieces

        def run(values, *weights):
            return forward(values, weights, mask, index)
        output_rows, pull = jax.vjp(run, block, *params)
        grads = pull(grad_block)
        totals = tuple((left + right for left, right in zip(totals, grads[1:])))
        return (totals, (output_rows, grads[0]))
    zeros = tuple((jnp.zeros_like(item) for item in params))
    totals, (outputs, grad_inputs) = lax.scan(one_group, zeros, (inputs, grad_in, valid))
    outputs = outputs.reshape(PASSAGES, LENGTH, D)
    keep = (positions[None, :] < lengths[:, None]).astype(jnp.float32)
    pooled = lax.optimization_barrier(jnp.sum(outputs * keep[:, :, None], axis=1)) / lengths[:, None].astype(jnp.float32)
    grad_passages = grad_inputs.reshape(PASSAGES, LENGTH, D).astype(jnp.bfloat16)
    return (outputs.astype(jnp.bfloat16), pooled, grad_passages, totals[0], totals[1], totals[2], totals[3], totals[4], totals[5], totals[6], totals[7], totals[8])
```

```python
import math

import jax
import jax.numpy as jnp
from jax import lax
from jax.experimental import pallas as pl
from jax.experimental.pallas import tpu as pltpu
from jax.sharding import PartitionSpec as P

MAXDIST = 128


EPS = 1e-06
HIGH = lax.Precision.HIGHEST
FLOOR = -1e30


def bucket_index(relative, buckets, reach):
    half_count = buckets // 2
    exact_count = half_count // 2
    distance = jnp.abs(relative)
    result = jnp.minimum(distance, exact_count)
    for power in range(1, half_count - exact_count):
        bound_at = math.ceil(
            exact_count * (reach / exact_count) ** (power / (half_count - exact_count)) - 1e-06
        )
        result = result + (distance >= bound_at).astype(jnp.int32)
    return result + (relative > 0).astype(jnp.int32) * half_count


def rms_norm(values, gain_vec):
    return values * lax.rsqrt(jnp.mean(values * values, axis=-1, keepdims=True) + EPS) * gain_vec


def attend_forward(query_four, key_four, value_four, bias_rows, key_valid):
    scores = (
        jnp.einsum("pqhe,pkhe->phqk", query_four, key_four, preferred_element_type=jnp.float32)
        + bias_rows[None]
    )
    scores = jnp.where(key_valid[:, None, None, :], scores, FLOOR)
    row_top = jnp.max(scores, axis=-1, keepdims=True)
    expo = jnp.exp(scores - row_top)
    row_total = jnp.sum(expo, axis=-1, keepdims=True)
    log_total = row_top + jnp.log(row_total)
    attn_probs = (expo / row_total).astype(jnp.bfloat16)
    mixed_rows = jnp.einsum(
        "phqk,pkhe->pqhe", attn_probs, value_four, preferred_element_type=jnp.float32
    )
    return (mixed_rows.astype(jnp.bfloat16), log_total)


def attend_backward(query_four, key_four, value_four, grad_mixed, log_total, key_valid, bias_rows):

    def one_passage(score_sum, pieces):
        query_p, key_p, value_p, grad_p, log_p, valid_p = pieces
        score_p = (
            jnp.einsum("qhe,khe->hqk", query_p, key_p, preferred_element_type=jnp.float32)
            + bias_rows
        )
        score_p = jnp.where(valid_p[None, None, :], score_p, FLOOR)
        prob_p = jnp.exp(score_p - log_p)
        grad_prob = jnp.einsum("qhe,khe->hqk", grad_p, value_p, preferred_element_type=jnp.float32)
        grad_score = (
            prob_p * (grad_prob - jnp.sum(prob_p * grad_prob, axis=-1, keepdims=True))
        ).astype(jnp.bfloat16)
        grad_query_p = jnp.einsum(
            "hqk,khe->qhe", grad_score, key_p, preferred_element_type=jnp.float32
        ).astype(jnp.bfloat16)
        grad_key_p = jnp.einsum(
            "hqk,qhe->khe", grad_score, query_p, preferred_element_type=jnp.float32
        )
        grad_value_p = jnp.einsum(
            "hqk,qhe->khe", prob_p.astype(jnp.bfloat16), grad_p, preferred_element_type=jnp.float32
        )
        return (
            score_sum + grad_score.astype(jnp.float32),
            (grad_query_p, grad_key_p, grad_value_p),
        )

    start_sum = jnp.zeros(bias_rows.shape, jnp.float32)
    return lax.scan(
        one_passage, start_sum, (query_four, key_four, value_four, grad_mixed, log_total, key_valid)
    )


def shards(
    passages,
    lengths,
    attn_gain,
    w_query,
    w_key,
    w_value,
    w_attn_out,
    bias_table,
    ffn_gain,
    w_in,
    w_ff_out,
    cotangent,
):
    n_pass, local_rows, width = passages.shape
    n_buckets, n_heads = bias_table.shape
    head_dim = width // n_heads
    seq_count = lax.axis_size("seq")
    full_len = local_rows * seq_count
    row_count = n_pass * local_rows
    first_row = lax.axis_index("seq") * local_rows
    gathered = (
        lax.all_gather(w_query, "dp", axis=0, tiled=True),
        lax.all_gather(w_key, "dp", axis=0, tiled=True),
        lax.all_gather(w_value, "dp", axis=0, tiled=True),
        lax.all_gather(w_attn_out, "dp", axis=0, tiled=True),
        lax.all_gather(w_in, "dp", axis=0, tiled=True),
        lax.all_gather(w_ff_out, "dp", axis=0, tiled=True),
    )
    wq_full, wk_full, wv_full, wo_full, win_full, wff_full = gathered
    key_pos = jnp.arange(full_len, dtype=jnp.int32)
    query_pos = first_row + jnp.arange(local_rows, dtype=jnp.int32)
    key_valid = key_pos[None, :] < lengths[:, None]
    query_valid = query_pos[None, :] < lengths[:, None]
    inputs = passages.astype(jnp.float32).reshape(row_count, width)
    normed = rms_norm(inputs, attn_gain).astype(jnp.bfloat16)
    query_rows = jnp.dot(normed, wq_full, preferred_element_type=jnp.float32).astype(jnp.bfloat16)
    key_rows = jnp.dot(normed, wk_full, preferred_element_type=jnp.float32).astype(jnp.bfloat16)
    value_rows = jnp.dot(normed, wv_full, preferred_element_type=jnp.float32).astype(jnp.bfloat16)
    query_local = query_rows.reshape(n_pass, local_rows, n_heads, head_dim)
    relative = key_pos[None, :] - query_pos[:, None]
    one_hot = (
        bucket_index(relative, n_buckets, MAXDIST)[:, :, None]
        == jnp.arange(n_buckets, dtype=jnp.int32)
    ).astype(jnp.float32)
    bias_rows = jnp.einsum("qkb,bh->hqk", one_hot, bias_table, precision=HIGH)
    key_all, value_all = (
        lax.all_gather(key_rows.reshape(n_pass, local_rows, width), "seq", axis=1, tiled=True),
        lax.all_gather(value_rows.reshape(n_pass, local_rows, width), "seq", axis=1, tiled=True),
    )
    key_four = key_all.reshape(n_pass, full_len, n_heads, head_dim)
    value_four = value_all.reshape(n_pass, full_len, n_heads, head_dim)
    mixed_four, log_total = attend_forward(query_local, key_four, value_four, bias_rows, key_valid)
    mixed_rows = mixed_four.reshape(row_count, width)
    hidden = inputs + jnp.dot(mixed_rows, wo_full, preferred_element_type=jnp.float32)
    normed_ffn = rms_norm(hidden, ffn_gain).astype(jnp.bfloat16)
    up_rows = jnp.dot(normed_ffn, win_full, preferred_element_type=jnp.float32)
    activated = jax.nn.gelu(up_rows).astype(jnp.bfloat16)
    output_rows = hidden + jnp.dot(activated, wff_full, preferred_element_type=jnp.float32)
    pool_part = jnp.sum(
        output_rows.reshape(n_pass, local_rows, width)
        * query_valid[:, :, None].astype(jnp.float32),
        axis=1,
    )
    pooled = lax.psum(pool_part, "seq") / lengths[:, None].astype(jnp.float32)
    gathered = (
        lax.all_gather(w_query, "dp", axis=0, tiled=True),
        lax.all_gather(w_key, "dp", axis=0, tiled=True),
        lax.all_gather(w_value, "dp", axis=0, tiled=True),
        lax.all_gather(w_attn_out, "dp", axis=0, tiled=True),
        lax.all_gather(w_in, "dp", axis=0, tiled=True),
        lax.all_gather(w_ff_out, "dp", axis=0, tiled=True),
    )
    wq_full, wk_full, wv_full, wo_full, win_full, wff_full = gathered
    grad_out = cotangent.astype(jnp.float32).reshape(row_count, width)
    grad_branch = grad_out.astype(jnp.bfloat16)
    g_ff_out = jnp.einsum("rf,rd->fd", activated, grad_branch, preferred_element_type=jnp.float32)
    grad_act = jnp.einsum("rd,fd->rf", grad_branch, wff_full, preferred_element_type=jnp.float32)
    _, gelu_pull = jax.vjp(jax.nn.gelu, up_rows)
    grad_up = gelu_pull(grad_act)[0].astype(jnp.bfloat16)
    g_in = jnp.einsum("rd,rf->df", normed_ffn, grad_up, preferred_element_type=jnp.float32)
    grad_normed_ffn = jnp.einsum("rf,df->rd", grad_up, win_full, preferred_element_type=jnp.float32)
    _, ffn_pull = jax.vjp(rms_norm, hidden, ffn_gain)
    grad_hidden_norm, g_ffn_gain = ffn_pull(grad_normed_ffn)
    grad_hidden = grad_out + grad_hidden_norm
    grad_attn = grad_hidden.astype(jnp.bfloat16)
    g_attn_out = jnp.einsum("rd,re->de", mixed_rows, grad_attn, preferred_element_type=jnp.float32)
    grad_mixed = jnp.einsum("re,de->rd", grad_attn, wo_full, preferred_element_type=jnp.float32)
    grad_mixed = grad_mixed.astype(jnp.bfloat16).reshape(n_pass, local_rows, n_heads, head_dim)
    score_sum, (grad_query, grad_key, grad_value) = attend_backward(
        query_local, key_four, value_four, grad_mixed, log_total, key_valid, bias_rows
    )
    grad_key, grad_value = (
        lax.psum_scatter(
            grad_key.reshape(n_pass, full_len, width).astype(jnp.bfloat16),
            "seq",
            scatter_dimension=1,
            tiled=True,
        ).astype(jnp.float32),
        lax.psum_scatter(
            grad_value.reshape(n_pass, full_len, width).astype(jnp.bfloat16),
            "seq",
            scatter_dimension=1,
            tiled=True,
        ).astype(jnp.float32),
    )
    grad_query = grad_query.reshape(row_count, width)
    grad_key = grad_key.astype(jnp.bfloat16).reshape(row_count, width)
    grad_value = grad_value.astype(jnp.bfloat16).reshape(row_count, width)
    g_table = jnp.einsum("qkb,hqk->bh", one_hot, score_sum, precision=HIGH)
    g_query = jnp.einsum("rd,re->de", normed, grad_query, preferred_element_type=jnp.float32)
    g_key = jnp.einsum("rd,re->de", normed, grad_key, preferred_element_type=jnp.float32)
    g_value = jnp.einsum("rd,re->de", normed, grad_value, preferred_element_type=jnp.float32)
    grad_normed = jnp.einsum("re,de->rd", grad_query, wq_full, preferred_element_type=jnp.float32)
    grad_normed = grad_normed + jnp.einsum(
        "re,de->rd", grad_key, wk_full, preferred_element_type=jnp.float32
    )
    grad_normed = grad_normed + jnp.einsum(
        "re,de->rd", grad_value, wv_full, preferred_element_type=jnp.float32
    )
    _, attn_pull = jax.vjp(rms_norm, inputs, attn_gain)
    grad_inputs_norm, g_attn_gain = attn_pull(grad_normed)
    grad_input = (
        (grad_hidden + grad_inputs_norm).astype(jnp.bfloat16).reshape(n_pass, local_rows, width)
    )
    row_grads = (
        lax.psum_scatter(g_query, "dp", scatter_dimension=0, tiled=True),
        lax.psum_scatter(g_key, "dp", scatter_dimension=0, tiled=True),
        lax.psum_scatter(g_value, "dp", scatter_dimension=0, tiled=True),
        lax.psum_scatter(g_attn_out, "dp", scatter_dimension=0, tiled=True),
        lax.psum_scatter(g_in, "dp", scatter_dimension=0, tiled=True),
        lax.psum_scatter(g_ff_out, "dp", scatter_dimension=0, tiled=True),
    )
    row_grads = (
        lax.psum(row_grads[0].astype(jnp.bfloat16), "seq").astype(jnp.float32),
        lax.psum(row_grads[1].astype(jnp.bfloat16), "seq").astype(jnp.float32),
        lax.psum(row_grads[2].astype(jnp.bfloat16), "seq").astype(jnp.float32),
        lax.psum(row_grads[3].astype(jnp.bfloat16), "seq").astype(jnp.float32),
        lax.psum(row_grads[4].astype(jnp.bfloat16), "seq").astype(jnp.float32),
        lax.psum(row_grads[5].astype(jnp.bfloat16), "seq").astype(jnp.float32),
    )
    small_sums = lax.psum((g_attn_gain, g_ffn_gain, g_table), ("dp", "seq"))
    layer_out = output_rows.astype(jnp.bfloat16).reshape(n_pass, local_rows, width)
    return (
        layer_out,
        pooled,
        grad_input,
        small_sums[0],
        row_grads[0],
        row_grads[1],
        row_grads[2],
        row_grads[3],
        small_sums[2],
        small_sums[1],
        row_grads[4],
        row_grads[5],
    )


DP, SEQ = 8, 4
LAST = DP - 1
BF, F32 = jnp.bfloat16, jnp.float32
MESH_ID = pl.DeviceIdType.MESH
TOKENS, WIDTH, HIDDEN, HEAD_N = 512, 768, 3072, 12
PAIRS = HEAD_N // 2
GELU_A, GELU_B = math.sqrt(2 / math.pi), 0.044715


def dg(left, right, on_left, on_right):
    return lax.dot_general(
        left, right, (((on_left,), (on_right,)), ((), ())), preferred_element_type=F32
    )


def ring_dp(place):
    high = place // 4
    return 2 * (place * (1 - high) + (7 - place) * high) + high


def times(start, size, step):
    return pl.ds(pl.multiple_of(start, step), size)


def band_bucket(n_buckets):
    lane = lax.broadcasted_iota(jnp.int32, (n_buckets, 512), 1)
    relative = jnp.where(lane < 384, lane - 128, lane - 640)
    row = lax.broadcasted_iota(jnp.int32, (n_buckets, 512), 0)
    return (bucket_index(relative, n_buckets, MAXDIST) == row).astype(F32)


def layer_kernel(
    x_hbm, cot_hbm, wq_hbm, wk_hbm, wv_hbm, wo_hbm, win_hbm, wff_hbm, lengths, attn_gain, ffn_gain, table,
    out_hbm, gx_hbm, gatt_hbm, gin_hbm, gff_hbm, pool_hbm, small_out,
    watt, win, wff, gin, gff, big, probs, xs, cot, normed, qkv, mixed, nf, lay, hid, acc, band, diag,
    sib_ff, y_ff, y_in, y_att, r_ffa, r_ffb, r_ina, r_inb, r_ata, r_atb, f_ff, f_in, f_att, sums, sums_in, pool,
    ag_s, ag_r, sb_s, sb_r, yf_s, yf_r, yb_s, yb_r, rr_s, rr_r, loc, a2_s, a2_r, hs_s, hs_r, yx_s, yx_r,
    fa_s, fa_r, fo_s, fo_r, fl, bf_s, bf_r, free_sem,
):
    dp, sq = lax.axis_index("dp"), lax.axis_index("seq")
    z, x, y, c = dp // 2, dp % 2, sq // 2, sq % 2
    place = x * (7 - z) + (1 - x) * z
    turn = 1 - 2 * c

    def owner(steps):
        return ring_dp((place + steps * turn + 16) % 8)

    nxt, prv = (owner(1), sq), (owner(-1), sq)
    sib, yp, ysib = (dp, 2 * y + 1 - c), (dp, 2 * (1 - y) + c), (dp, 2 * (1 - y) + 1 - c)
    xp = (2 * z + 1 - x, sq)
    z1 = (2 * (z + 1 - 2 * (z % 2)) + x, sq)
    z2 = (2 * ((z + 2) % 4) + x, sq)
    peers = (sib, yp, ysib)

    def send(src, dst, ss, rs, dev):
        return pltpu.make_async_remote_copy(
            src_ref=src, dst_ref=dst, send_sem=ss, recv_sem=rs, device_id=dev, device_id_type=MESH_ID
        )

    barrier = pltpu.get_barrier_semaphore()
    for dev in (sib, yp, ysib, nxt, prv, xp, z1, z2):
        pl.semaphore_signal(barrier, inc=1, device_id=dev, device_id_type=MESH_ID)

    r96 = times(96 * dp, 96, 96)
    own = [pltpu.make_async_copy(w, watt.at[i, r96], loc.at[i]) for i, w in enumerate((wq_hbm, wk_hbm, wv_hbm, wo_hbm))]
    own.append(pltpu.make_async_copy(win_hbm, win.at[r96], loc.at[4]))
    own.append(pltpu.make_async_copy(wff_hbm, wff.at[times(384 * dp, 384, 384)], loc.at[5]))
    mine = times(128 * sq, 128, 128)
    own.append(pltpu.make_async_copy(x_hbm.at[sq], xs.at[mine], loc.at[6]))
    own.append(pltpu.make_async_copy(cot_hbm.at[sq], cot.at[mine], loc.at[7]))
    for copy in own:
        copy.start()
    pl.semaphore_wait(barrier, 8)

    def swap(k, src_hbm, dst, at):
        dev = peers[k]
        return send(src_hbm.at[dev[1]], dst.at[mine], a2_s.at[at, k], a2_r.at[at, k], dev)

    def swap_wait(dst, at):
        for k in range(3):
            theirs = dst.at[times(128 * peers[k][1], 128, 128)]
            send(theirs, theirs, a2_s.at[at, k], a2_r.at[at, k], peers[k]).wait_recv()

    for k in range(3):
        swap(k, x_hbm, xs, 0).start()

    def piece(ch, d, cc, yy):
        if ch < 2:
            cols = pl.ds(256, 256) if ch == 0 else times(512 * yy, 256, 256)
            return watt.at[:, times(96 * d + 48 * cc, 48, 48), cols]
        if ch < 4:
            cols = pl.ds(1024, 1024) if ch == 2 else times(2048 * yy, 1024, 1024)
            return win.at[times(96 * d + 48 * cc, 48, 48), cols]
        cols = pl.ds(256, 256) if ch == 4 else times(512 * yy, 256, 256)
        return wff.at[times(384 * d + 192 * cc, 192, 192), cols]

    def ring_send(ch, s):
        part = piece(ch, owner(-s), c, y)
        return send(part, part, ag_s.at[ch, s], ag_r.at[ch, s], nxt)

    def hand_on(ch, s):
        part = piece(ch, owner(-s - 1), c, y)
        return send(part, part, sb_s.at[ch, s], sb_r.at[ch, s], sib)

    def cross(ch, s):
        part = piece(ch, owner(-s - 1), c, y)
        return send(part, part, yf_s.at[ch // 2, s], yf_r.at[ch // 2, s], yp)

    def cross_on(ch, s):
        part = piece(ch, owner(-s - 1), c, 1 - y)
        return send(part, part, yb_s.at[ch // 2, s], yb_r.at[ch // 2, s], sib)

    def tick(ch, s):
        part = piece(ch, owner(-s - 1), c, y)
        send(part, part, ag_s.at[ch, s], ag_r.at[ch, s], nxt).wait_recv()

        @pl.when(s < LAST - 1)
        def _():
            ring_send(ch, s + 1).start()

        hand_on(ch, s).start()
        if ch % 2:
            cross(ch, s).start()

    def cross_tick(ch, s):
        part = piece(ch, owner(-s - 1), c, 1 - y)
        send(part, part, yf_s.at[ch // 2, s], yf_r.at[ch // 2, s], yp).wait_recv()
        cross_on(ch, s).start()

    def gathered(group):
        def step(s, _):
            d = owner(s + 1)
            for ch in (2 * group, 2 * group + 1):
                part = piece(ch, d, 1 - c, y)
                send(part, part, sb_s.at[ch, s], sb_r.at[ch, s], sib).wait_recv()
            part = piece(2 * group + 1, d, 1 - c, 1 - y)
            send(part, part, yb_s.at[group, s], yb_r.at[group, s], sib).wait_recv()
            return 0

        lax.fori_loop(0, LAST, step, 0)

    def gather_sent():
        def step(s, _):
            for ch in range(6):
                ring_send(ch, s).wait_send()
                hand_on(ch, s).wait_send()
                if ch % 2:
                    cross(ch, s).wait_send()
                    cross_on(ch, s).wait_send()
            return 0

        lax.fori_loop(0, LAST, step, 0)

    for i in range(5):
        own[i].wait()
    for ch in (0, 1, 2):
        ring_send(ch, 0).start()
    own[5].wait()
    for k in range(3):
        swap(k, cot_hbm, cot, 1).start()

    one_hot = band_bucket(32)
    band[pl.ds(0, HEAD_N), :] = lax.dot_general(
        table[...], one_hot, (((0,), (0,)), ((), ())), precision=HIGH, preferred_element_type=F32
    )

    own[6].wait()
    swap_wait(xs, 0)

    def norm_rows(src, gain, dst):
        def step(b, _):
            rows = times(128 * b, 128, 128)
            v = src[rows, :].astype(F32)
            s = lax.rsqrt(jnp.mean(v * v, axis=-1, keepdims=True) + EPS)
            dst[rows, :] = (v * s * gain[...]).astype(BF)
            return 0

        lax.fori_loop(0, 4, step, 0)

    norm_rows(xs, attn_gain, normed)

    def first_steps(s, _):
        tick(1, s)
        tick(0, s)

        @pl.when(s > 0)
        def _():
            cross_tick(1, s - 1)

        tick(2, s)

        @pl.when(s == LAST - 2)
        def _():
            ring_send(3, 0).start()
            ring_send(5, 0).start()

        return 0

    lax.fori_loop(0, LAST, first_steps, 0)
    ring_send(4, 0).start()
    cross_tick(1, LAST - 1)
    gathered(0)

    def later_steps(s):
        tick(3, s)
        tick(5, s)

        @pl.when(s > 0)
        def _():
            cross_tick(3, s - 1)
            cross_tick(5, s - 1)

        tick(4, s)

    def project(m, _):
        qkv[m] = dg(normed[...], watt[m], 1, 0).astype(BF)
        return 0

    lax.fori_loop(0, 3, project, 0)
    later_steps(0)

    count = lengths[sq]
    valid = lax.broadcasted_iota(jnp.int32, (1, TOKENS), 1) < count
    lane = lax.broadcasted_iota(jnp.int32, (1, 128), 1)
    keep = (lane < 64, lane >= 64)

    def only(h, v):
        return jnp.where(keep[h], v, jnp.zeros_like(v))

    def attend(hp, _):
        cols = times(128 * hp, 128, 128)
        key, value = qkv[1, :, cols], qkv[2, :, cols]
        total = [None] * 4
        for h in range(2):
            row = band[pl.ds(2 * hp + h, 1), :]
            tilted = pltpu.roll(jnp.broadcast_to(row, (128, 512)), 0, 1, stride=1, stride_axis=0)
            before = jnp.broadcast_to(row[:, 384:], (128, 128))
            after = jnp.broadcast_to(row[:, 256:384], (128, 128))
            value_h = only(h, value)
            for ib in range(4):
                rows = pl.ds(128 * ib, 128)
                blocks = []
                for jb in range(4):
                    off = jb - ib
                    if off < -1:
                        blocks.append(before)
                    elif off > 1:
                        blocks.append(after)
                    else:
                        blocks.append(tilted[:, 128 * (off + 1) : 128 * (off + 2)])
                scores = dg(only(h, qkv[0, rows, cols]), key, 1, 1) + jnp.concatenate(blocks, axis=1)
                scores = jnp.where(valid, scores, FLOOR)
                top = jnp.max(scores, axis=-1, keepdims=True)
                expo = jnp.exp(scores - top)
                part = jnp.sum(expo, axis=-1, keepdims=True)
                low = (expo * (1.0 / part)).astype(BF)
                probs[2 * hp + h, rows, :] = low
                one = dg(low, value_h, 1, 0)
                total[ib] = one if h == 0 else total[ib] + one
        for ib in range(4):
            mixed[pl.ds(128 * ib, 128), cols] = total[ib].astype(BF)
        later_steps(hp + 1)
        return 0

    lax.fori_loop(0, PAIRS, attend, 0)
    cross_tick(3, LAST - 1)
    cross_tick(5, LAST - 1)

    def residual(b, _):
        rows = times(128 * b, 128, 128)
        v = xs[rows, :].astype(F32) + dg(mixed[rows, :], watt[3], 1, 0)
        hid[rows, :] = v
        s = lax.rsqrt(jnp.mean(v * v, axis=-1, keepdims=True) + EPS)
        nf[rows, :] = (v * s * ffn_gain[...]).astype(BF)
        return 0

    lax.fori_loop(0, 4, residual, 0)

    gathered(1)
    up_rows, down_rows = pl.ds(0, TOKENS), pl.ds(TOKENS, TOKENS)

    def block(j):
        return times(768 * j, 768, 768)

    def widen(j, _):
        v = dg(nf[...], win[:, block(j)], 1, 0)
        sq_v = v * v
        t = jnp.tanh(v * (GELU_A + (GELU_A * GELU_B) * sq_v))
        half = 0.5 + 0.5 * t
        big[j, up_rows, :] = (v * half).astype(BF)
        slope = half + (v * half) * (1.0 - t) * (GELU_A + (3 * GELU_A * GELU_B) * sq_v)
        big[j, down_rows, :] = slope.astype(BF)
        return 0

    lax.fori_loop(0, 4, widen, 0)
    own[7].wait()
    swap_wait(cot, 1)

    def half_ff(d2, cc):
        return gff.at[pl.ds(d2, 2), :, times(384 * cc, 384, 384)]

    def grad_ff(j, _):
        v = dg(big[j, up_rows, :], cot[...], 0, 0).astype(BF)
        gff[pl.ds(2 * j, 2)] = v.reshape(2, 384, 768)
        send(half_ff(2 * j, 1 - c), sib_ff.at[pl.ds(2 * j, 2)], hs_s.at[0, j], hs_r.at[0, j], sib).start()
        return 0

    lax.fori_loop(0, 4, grad_ff, 0)
    gathered(2)

    def grad_up(j, _):
        v = dg(cot[...], wff[block(j), :], 1, 1) * big[j, down_rows, :].astype(F32)
        big[j, down_rows, :] = v.astype(BF)
        return 0

    lax.fori_loop(0, 4, grad_up, 0)

    def merge_ff(j, _):
        send(half_ff(2 * j, 1 - c), sib_ff.at[pl.ds(2 * j, 2)], hs_s.at[0, j], hs_r.at[0, j], sib).wait()
        cols = times(384 * c, 384, 384)
        for i in range(2):
            gff[2 * j + i, :, cols] = (gff[2 * j + i, :, cols].astype(F32) + sib_ff[2 * j + i].astype(F32)).astype(BF)
        return 0

    lax.fori_loop(0, 4, merge_ff, 0)

    def cross_src(g, yy):
        if g == 0:
            return gff.at[:, times(320 * yy, 64, 64), times(384 * c, 384, 384)]
        if g == 1:
            return gin.at[:, times(1536 * c + 1280 * yy, 256, 256)]
        return big.at[:, pl.ds(0, 768), times(384 * c + 256 * yy, 128, 128)]

    cross_dst = (y_ff, y_in, y_att)

    def cross_sum(g):
        return send(cross_src(g, 1 - y), cross_dst[g], yx_s.at[g], yx_r.at[g], yp)

    def add_cross(g):
        cross_sum(g).wait()
        here, came = cross_src(g, y), cross_dst[g]
        here[...] = (here[...].astype(F32) + came[...].astype(F32)).astype(BF)

    def rs_piece(ch, d, yy):
        if ch < 2:
            rows = pl.ds(64, 256) if ch == 0 else times(320 * yy, 64, 64)
            return gff.at[d, rows, times(384 * c, 384, 384)]
        rows = times(96 * d, 96, 96)
        if ch < 4:
            cols = times(1536 * c + 256, 1024, 256) if ch == 2 else times(1536 * c + 1280 * yy, 256, 256)
            return gin.at[rows, cols]
        cols = times(384 * c + 128, 128, 128) if ch == 4 else times(384 * c + 256 * yy, 128, 128)
        return big.at[:, rows, cols]

    landing = (r_ffa, r_ffb, r_ina, r_inb, r_ata, r_atb)

    def rs_send(ch, s):
        return send(rs_piece(ch, owner(-s - 1), y), landing[ch].at[s], rr_s.at[ch, s], rr_r.at[ch, s], nxt)

    def rs_tick(ch, s):
        rs_send(ch, s).wait_recv()
        here = rs_piece(ch, owner(-s - 2), y)
        here[...] = (here[...].astype(F32) + landing[ch][s].astype(F32)).astype(BF)

        @pl.when(s < LAST - 1)
        def _():
            rs_send(ch, s + 1).start()

    def rs_sent(ch):
        def step(s, _):
            rs_send(ch, s).wait_send()
            return 0

        lax.fori_loop(0, LAST, step, 0)

    cross_sum(0).start()
    rs_send(0, 0).start()
    add_cross(0)
    rs_send(1, 0).start()

    acc[...] = hid[...]

    def narrow(j, _):
        acc[...] += dg(big[j, up_rows, :], wff[block(j), :], 1, 0)
        return 0

    lax.fori_loop(0, 4, narrow, 0)
    lay[...] = acc[...].astype(BF)

    def give(src, dst_hbm, at, k):
        dev = peers[k]
        return send(src.at[times(128 * dev[1], 128, 128)], dst_hbm.at[sq], a2_s.at[at, k], a2_r.at[at, k], dev)

    def give_wait(src, dst_hbm, at):
        for k in range(3):
            give(src, dst_hbm, at, k).wait_send()
            theirs = dst_hbm.at[peers[k][1]]
            send(theirs, theirs, a2_s.at[at, k], a2_r.at[at, k], peers[k]).wait_recv()

    for k in range(3):
        give(lay, out_hbm, 2, k).start()
    lay_own = pltpu.make_async_copy(lay.at[mine], out_hbm.at[sq], loc.at[0])
    lay_own.start()
    here_t = lax.broadcasted_iota(jnp.int32, (TOKENS, 1), 0) < count
    mean = jnp.sum(jnp.where(here_t, acc[...], 0.0), axis=0, keepdims=True) / count.astype(F32)
    pool[...] = jnp.broadcast_to(mean, (8, WIDTH))
    pool_own = pltpu.make_async_copy(pool, pool_hbm.at[sq], loc.at[1])
    pool_own.start()

    def pool_send(k):
        return send(pool, pool_hbm.at[sq], a2_s.at[4, k], a2_r.at[4, k], peers[k])

    for k in range(3):
        pool_send(k).start()

    gather_sent()
    pl.semaphore_signal(free_sem, inc=1, device_id=sib, device_id_type=MESH_ID)

    def grad_in(j, _):
        gin[:, block(j)] = dg(nf[...], big[j, down_rows, :], 0, 0).astype(BF)
        return 0

    lax.fori_loop(0, 4, grad_in, 0)
    pl.semaphore_wait(free_sem, 1)

    def half_in(k):
        src = gin.at[:, times(1536 * (1 - c) + 384 * k, 384, 384)]
        return send(src, wff.at[times(768 * k, 768, 768), pl.ds(384, 384)], hs_s.at[1, k], hs_r.at[1, k], sib)

    for k in range(4):
        half_in(k).start()

    acc[...] = jnp.zeros_like(acc)

    def grad_nf(j, _):
        acc[...] += dg(big[j, down_rows, :], win[:, block(j)], 1, 1)
        return 0

    lax.fori_loop(0, 4, grad_nf, 0)

    for k in range(4):
        half_in(k).wait()
        cols = times(1536 * c + 384 * k, 384, 384)
        gin[:, cols] = (gin[:, cols].astype(F32) + wff[pl.ds(768 * k, 768), pl.ds(384, 384)].astype(F32)).astype(BF)
    cross_sum(1).start()
    rs_send(2, 0).start()

    def norm_back(v, gain, grad):
        s = lax.rsqrt(jnp.mean(v * v, axis=-1, keepdims=True) + EPS)
        scaled = grad * gain
        back = s * scaled - v * (s * s * s) * jnp.mean(v * scaled, axis=-1, keepdims=True)
        return back, jnp.sum(grad * v * s, axis=0, keepdims=True)

    def ffn_norm_back(b, total):
        rows = times(128 * b, 128, 128)
        back, part = norm_back(hid[rows, :], ffn_gain[...], acc[rows, :])
        v = cot[rows, :].astype(F32) + back
        hid[rows, :] = v
        cot[rows, :] = v.astype(BF)
        return total + part

    g_ffn_gain = lax.fori_loop(0, 4, ffn_norm_back, jnp.zeros((1, WIDTH), F32))

    add_cross(1)
    rs_send(3, 0).start()

    big[3, pl.ds(0, 768), :] = dg(mixed[...], cot[...], 0, 0).astype(BF)
    nf[...] = dg(cot[...], watt[3], 1, 1).astype(BF)

    flip_sum = lax.broadcasted_iota(jnp.int32, (128, 128), 0) + lax.broadcasted_iota(jnp.int32, (128, 128), 1)
    flip = (flip_sum == 127).astype(F32)

    def attend_back(hp, _):
        cols = times(128 * hp, 128, 128)
        key, value = qkv[1, :, cols], qkv[2, :, cols]
        g_key = g_value = jnp.zeros((TOKENS, 128), F32)
        g_query = [None] * 4
        for h in range(2):
            key_h = only(h, key)
            before = after = jnp.zeros((128, 128), F32)
            near = [jnp.zeros((128, 128), F32) for _ in range(3)]
            for ib in range(4):
                rows = pl.ds(128 * ib, 128)
                grad_h = only(h, nf[rows, cols])
                low = probs[2 * hp + h, rows, :]
                wide = low.astype(F32)
                d_probs = dg(grad_h, value, 1, 1)
                mean_d = jnp.sum(wide * d_probs, axis=-1, keepdims=True)
                d_score = wide * (d_probs - mean_d)
                for jb in range(4):
                    off, part = jb - ib, d_score[:, 128 * jb : 128 * (jb + 1)]
                    if off < -1:
                        before = before + part
                    elif off > 1:
                        after = after + part
                    else:
                        near[off + 1] = near[off + 1] + part
                d_low = d_score.astype(BF)
                one = dg(d_low, key_h, 1, 0)
                g_query[ib] = one if h == 0 else g_query[ib] + one
                g_key = g_key + dg(d_low, only(h, qkv[0, rows, cols]), 0, 0)
                g_value = g_value + dg(low, grad_h, 0, 0)
            tilted = lax.dot_general(
                flip, jnp.concatenate(near, axis=1), (((1,), (0,)), ((), ())), precision=HIGH, preferred_element_type=F32
            )
            tilted = jnp.concatenate([tilted, jnp.zeros((128, 128), F32)], axis=1)
            flat = jnp.sum(pltpu.roll(tilted, 385, 1, stride=1, stride_axis=0), axis=0, keepdims=True)
            far = jnp.concatenate(
                [
                    jnp.zeros((1, 256), F32),
                    jnp.sum(after, axis=0, keepdims=True),
                    jnp.sum(before, axis=0, keepdims=True),
                ],
                axis=1,
            )
            diag[pl.ds(2 * hp + h, 1), :] = flat + far
        for ib in range(4):
            qkv[0, pl.ds(128 * ib, 128), cols] = g_query[ib].astype(BF)
        qkv[1, :, cols] = g_key.astype(BF)
        qkv[2, :, cols] = g_value.astype(BF)
        return 0

    lax.fori_loop(0, PAIRS, attend_back, 0)

    def grad_project(m, _):
        big[m, pl.ds(0, 768), :] = dg(normed[...], qkv[m], 0, 0).astype(BF)
        return 0

    lax.fori_loop(0, 3, grad_project, 0)

    def half_att(m):
        src = big.at[m, pl.ds(0, 768), times(384 * (1 - c), 384, 384)]
        return send(src, wff.at[times(768 * m, 768, 768), pl.ds(0, 384)], hs_s.at[2, m], hs_r.at[2, m], sib)

    for m in range(4):
        half_att(m).start()

    acc[...] = jnp.zeros_like(acc)

    def grad_normed(m, _):
        acc[...] += dg(qkv[m], watt[m], 1, 1)
        return 0

    lax.fori_loop(0, 3, grad_normed, 0)

    for m in range(4):
        half_att(m).wait()
        cols = times(384 * c, 384, 384)
        rows = pl.ds(0, 768)
        big[m, rows, cols] = (
            big[m, rows, cols].astype(F32) + wff[pl.ds(768 * m, 768), pl.ds(0, 384)].astype(F32)
        ).astype(BF)
    cross_sum(2).start()
    rs_send(4, 0).start()

    def attn_norm_back(b, total):
        rows = times(128 * b, 128, 128)
        back, part = norm_back(xs[rows, :].astype(F32), attn_gain[...], acc[rows, :])
        mixed[rows, :] = (hid[rows, :] + back).astype(BF)
        return total + part

    g_attn_gain = lax.fori_loop(0, 4, attn_norm_back, jnp.zeros((1, WIDTH), F32))
    for k in range(3):
        give(mixed, gx_hbm, 3, k).start()
    gx_own = pltpu.make_async_copy(mixed.at[mine], gx_hbm.at[sq], loc.at[2])
    gx_own.start()

    add_cross(2)
    rs_send(5, 0).start()

    sums[0] = jnp.zeros((48, 128), F32)
    diag_all = diag[...]
    sums[0, 0:32, 0:16] = lax.dot_general(
        band_bucket(32), diag_all, (((1,), (1,)), ((), ())), precision=HIGH, preferred_element_type=F32
    )
    for k in range(6):
        sums[0, 32 + k : 33 + k, :] = g_attn_gain[:, 128 * k : 128 * (k + 1)]
        sums[0, 38 + k : 39 + k, :] = g_ffn_gain[:, 128 * k : 128 * (k + 1)]
    for k, dev in enumerate((sib, yp, xp, z1, z2)):
        copy = send(sums.at[k], sums_in.at[k], bf_s.at[k], bf_r.at[k], dev)
        copy.start()
        copy.wait()
        sums[k + 1] = sums[k] + sums_in[k]
    small_out[...] = sums[5]

    def rounds(s, _):
        for ch in range(6):
            rs_tick(ch, s)
        return 0

    lax.fori_loop(0, LAST, rounds, 0)

    def out_piece(g, cc, yy):
        if g == 0:
            rows = pl.ds(64, 256) if yy is None else times(320 * yy, 64, 64)
            return gff_hbm.at[rows, times(384 * cc, 384, 384)]
        if g == 1:
            if yy is None:
                return gin_hbm.at[:, times(1536 * cc + 256, 1024, 256)]
            return gin_hbm.at[:, times(1536 * cc + 1280 * yy, 256, 256)]
        if yy is None:
            return gatt_hbm.at[:, :, times(384 * cc + 128, 128, 128)]
        return gatt_hbm.at[:, :, times(384 * cc + 256 * yy, 128, 128)]

    final = (f_ff, f_in, f_att)

    def share_a(g):
        return send(rs_piece(2 * g, dp, y), final[g], fa_s.at[g], fa_r.at[g], yp)

    def share_b(g, k):
        return send(rs_piece(2 * g + 1, dp, y), out_piece(g, c, y), fo_s.at[g, k], fo_r.at[g, k], peers[k])

    def share_sum(g):
        return send(final[g], out_piece(g, c, None), fo_s.at[g, 3], fo_r.at[g, 3], sib)

    def keep_b(g):
        return pltpu.make_async_copy(rs_piece(2 * g + 1, dp, y), out_piece(g, c, y), fl.at[g, 0])

    def keep_sum(g):
        return pltpu.make_async_copy(final[g], out_piece(g, c, None), fl.at[g, 1])

    for g in range(3):
        share_a(g).start()
        for k in range(3):
            share_b(g, k).start()
        keep_b(g).start()
    for g in range(3):
        share_a(g).wait()
        here = rs_piece(2 * g, dp, y)
        final[g][...] = (final[g][...].astype(F32) + here[...].astype(F32)).astype(BF)
        share_sum(g).start()
        keep_sum(g).start()
    for g in range(3):
        keep_b(g).wait()
        keep_sum(g).wait()
        for k, (cc, yy) in enumerate(((1 - c, y), (c, 1 - y), (1 - c, 1 - y))):
            share_b(g, k).wait_send()
            came = out_piece(g, cc, yy)
            send(came, came, fo_s.at[g, k], fo_r.at[g, k], peers[k]).wait_recv()
        share_sum(g).wait_send()
        came = out_piece(g, 1 - c, None)
        send(came, came, fo_s.at[g, 3], fo_r.at[g, 3], sib).wait_recv()
    for ch in range(6):
        rs_sent(ch)
    give_wait(lay, out_hbm, 2)
    give_wait(mixed, gx_hbm, 3)
    lay_own.wait()
    gx_own.wait()
    pool_own.wait()
    for k in range(3):
        pool_send(k).wait_send()
        theirs = pool_hbm.at[peers[k][1]]
        send(theirs, theirs, a2_s.at[4, k], a2_r.at[4, k], peers[k]).wait_recv()
        swap(k, x_hbm, xs, 0).wait_send()
        swap(k, cot_hbm, cot, 1).wait_send()


def passage_shards(
    passages, lengths, attn_gain, w_query, w_key, w_value, w_attn_out, bias_table, ffn_gain, w_in, w_ff_out, cotangent
):
    any_space = pl.BlockSpec(memory_space=pl.ANY)
    vmem = pl.BlockSpec(memory_space=pltpu.VMEM)
    dma = pltpu.SemaphoreType.DMA
    scratch = [
        pltpu.VMEM(shape, BF)
        for shape in (
            (4, 768, 768), (768, 3072), (3072, 768), (768, 3072), (8, 384, 768), (4, 1024, 768), (12, 512, 512),
            (512, 768), (512, 768), (512, 768), (3, 512, 768), (512, 768), (512, 768), (512, 768),
        )
    ]
    scratch += [pltpu.VMEM(shape, F32) for shape in ((512, 768), (512, 768), (16, 512), (16, 512))]
    scratch += [
        pltpu.VMEM(shape, BF)
        for shape in (
            (8, 384, 384), (8, 64, 384), (768, 256), (4, 768, 128),
            (7, 256, 384), (7, 64, 384), (7, 96, 1024), (7, 96, 256), (7, 4, 96, 128), (7, 4, 96, 128),
            (256, 384), (96, 1024), (4, 96, 128),
        )
    ]
    scratch += [pltpu.VMEM((6, 48, 128), F32), pltpu.VMEM((5, 48, 128), F32), pltpu.VMEM((8, 768), F32)]
    scratch += [
        dma(shape)
        for shape in (
            (6, 7), (6, 7), (6, 7), (6, 7), (3, 7), (3, 7), (3, 7), (3, 7), (6, 7), (6, 7), (8,), (5, 3), (5, 3),
            (3, 4), (3, 4), (3,), (3,), (3,), (3,), (3, 4), (3, 4), (3, 2), (5,), (5,),
        )
    ]
    scratch.append(pltpu.SemaphoreType.REGULAR)
    outs = pl.pallas_call(
        layer_kernel,
        out_shape=(
            jax.ShapeDtypeStruct((4, 128, 768), BF),
            jax.ShapeDtypeStruct((4, 128, 768), BF),
            jax.ShapeDtypeStruct((4, 96, 768), BF),
            jax.ShapeDtypeStruct((96, 3072), BF),
            jax.ShapeDtypeStruct((384, 768), BF),
            jax.ShapeDtypeStruct((4, 8, 768), F32),
            jax.ShapeDtypeStruct((48, 128), F32),
        ),
        in_specs=[any_space] * 8 + [pl.BlockSpec(memory_space=pltpu.SMEM)] + [vmem] * 3,
        out_specs=(any_space,) * 6 + (vmem,),
        scratch_shapes=scratch,
        compiler_params=pltpu.CompilerParams(collective_id=0, has_side_effects=True, vmem_limit_bytes=64 * 2**20),
        name="layer",
    )(
        passages, cotangent, w_query, w_key, w_value, w_attn_out, w_in, w_ff_out, lengths,
        attn_gain.reshape(1, WIDTH), ffn_gain.reshape(1, WIDTH), bias_table,
    )
    layer_out, grad_input, g_att, g_in, g_ff, pooled, small = outs
    g_att = g_att.astype(F32)
    return (
        layer_out,
        pooled[:, 0],
        grad_input,
        small[32:38].reshape(WIDTH),
        g_att[0],
        g_att[1],
        g_att[2],
        g_att[3],
        small[:32, :HEAD_N],
        small[38:44].reshape(WIDTH),
        g_in.astype(F32),
        g_ff.astype(F32),
    )


def solution(mesh):
    ring = (mesh.shape["dp"], mesh.shape["seq"]) == (DP, SEQ)
    return jax.shard_map(
        passage_shards if ring else shards,
        mesh=mesh,
        in_specs=(
            P("dp", "seq", None),
            P("dp"),
            P(),
            P("dp", None),
            P("dp", None),
            P("dp", None),
            P("dp", None),
            P(),
            P(),
            P("dp", None),
            P("dp", None),
            P("dp", "seq", None),
        ),
        out_specs=(
            P("dp", "seq", None),
            P("dp", None),
            P("dp", "seq", None),
            P(),
            P("dp", None),
            P("dp", None),
            P("dp", None),
            P("dp", None),
            P(),
            P(),
            P("dp", None),
            P("dp", None),
        ),
        check_vma=False,
    )
```

```python
import math

import jax
import jax.numpy as jnp
from jax import lax
from jax.experimental import pallas as pl
from jax.experimental.pallas import tpu as pltpu
from jax.sharding import PartitionSpec as P

MAXDIST = 128


EPS = 1e-06
HIGH = lax.Precision.HIGHEST
FLOOR = -1e30


def bucket_index(relative, buckets, reach):
    half_count = buckets // 2
    exact_count = half_count // 2
    distance = jnp.abs(relative)
    result = jnp.minimum(distance, exact_count)
    for power in range(1, half_count - exact_count):
        bound_at = math.ceil(
            exact_count * (reach / exact_count) ** (power / (half_count - exact_count)) - 1e-06
        )
        result = result + (distance >= bound_at).astype(jnp.int32)
    return result + (relative > 0).astype(jnp.int32) * half_count


def rms_norm(values, gain_vec):
    return values * lax.rsqrt(jnp.mean(values * values, axis=-1, keepdims=True) + EPS) * gain_vec


def attend_forward(query_four, key_four, value_four, bias_rows, key_valid):
    scores = (
        jnp.einsum("pqhe,pkhe->phqk", query_four, key_four, preferred_element_type=jnp.float32)
        + bias_rows[None]
    )
    scores = jnp.where(key_valid[:, None, None, :], scores, FLOOR)
    row_top = jnp.max(scores, axis=-1, keepdims=True)
    expo = jnp.exp(scores - row_top)
    row_total = jnp.sum(expo, axis=-1, keepdims=True)
    log_total = row_top + jnp.log(row_total)
    attn_probs = (expo / row_total).astype(jnp.bfloat16)
    mixed_rows = jnp.einsum(
        "phqk,pkhe->pqhe", attn_probs, value_four, preferred_element_type=jnp.float32
    )
    return (mixed_rows.astype(jnp.bfloat16), log_total)


def attend_backward(query_four, key_four, value_four, grad_mixed, log_total, key_valid, bias_rows):

    def one_passage(score_sum, pieces):
        query_p, key_p, value_p, grad_p, log_p, valid_p = pieces
        score_p = (
            jnp.einsum("qhe,khe->hqk", query_p, key_p, preferred_element_type=jnp.float32)
            + bias_rows
        )
        score_p = jnp.where(valid_p[None, None, :], score_p, FLOOR)
        prob_p = jnp.exp(score_p - log_p)
        grad_prob = jnp.einsum("qhe,khe->hqk", grad_p, value_p, preferred_element_type=jnp.float32)
        grad_score = (
            prob_p * (grad_prob - jnp.sum(prob_p * grad_prob, axis=-1, keepdims=True))
        ).astype(jnp.bfloat16)
        grad_query_p = jnp.einsum(
            "hqk,khe->qhe", grad_score, key_p, preferred_element_type=jnp.float32
        ).astype(jnp.bfloat16)
        grad_key_p = jnp.einsum(
            "hqk,qhe->khe", grad_score, query_p, preferred_element_type=jnp.float32
        )
        grad_value_p = jnp.einsum(
            "hqk,qhe->khe", prob_p.astype(jnp.bfloat16), grad_p, preferred_element_type=jnp.float32
        )
        return (
            score_sum + grad_score.astype(jnp.float32),
            (grad_query_p, grad_key_p, grad_value_p),
        )

    start_sum = jnp.zeros(bias_rows.shape, jnp.float32)
    return lax.scan(
        one_passage, start_sum, (query_four, key_four, value_four, grad_mixed, log_total, key_valid)
    )


def shards(
    passages,
    lengths,
    attn_gain,
    w_query,
    w_key,
    w_value,
    w_attn_out,
    bias_table,
    ffn_gain,
    w_in,
    w_ff_out,
    cotangent,
):
    n_pass, local_rows, width = passages.shape
    n_buckets, n_heads = bias_table.shape
    head_dim = width // n_heads
    seq_count = lax.axis_size("seq")
    full_len = local_rows * seq_count
    row_count = n_pass * local_rows
    first_row = lax.axis_index("seq") * local_rows
    gathered = (
        lax.all_gather(w_query, "dp", axis=0, tiled=True),
        lax.all_gather(w_key, "dp", axis=0, tiled=True),
        lax.all_gather(w_value, "dp", axis=0, tiled=True),
        lax.all_gather(w_attn_out, "dp", axis=0, tiled=True),
        lax.all_gather(w_in, "dp", axis=0, tiled=True),
        lax.all_gather(w_ff_out, "dp", axis=0, tiled=True),
    )
    wq_full, wk_full, wv_full, wo_full, win_full, wff_full = gathered
    key_pos = jnp.arange(full_len, dtype=jnp.int32)
    query_pos = first_row + jnp.arange(local_rows, dtype=jnp.int32)
    key_valid = key_pos[None, :] < lengths[:, None]
    query_valid = query_pos[None, :] < lengths[:, None]
    inputs = passages.astype(jnp.float32).reshape(row_count, width)
    normed = rms_norm(inputs, attn_gain).astype(jnp.bfloat16)
    query_rows = jnp.dot(normed, wq_full, preferred_element_type=jnp.float32).astype(jnp.bfloat16)
    key_rows = jnp.dot(normed, wk_full, preferred_element_type=jnp.float32).astype(jnp.bfloat16)
    value_rows = jnp.dot(normed, wv_full, preferred_element_type=jnp.float32).astype(jnp.bfloat16)
    query_local = query_rows.reshape(n_pass, local_rows, n_heads, head_dim)
    relative = key_pos[None, :] - query_pos[:, None]
    one_hot = (
        bucket_index(relative, n_buckets, MAXDIST)[:, :, None]
        == jnp.arange(n_buckets, dtype=jnp.int32)
    ).astype(jnp.float32)
    bias_rows = jnp.einsum("qkb,bh->hqk", one_hot, bias_table, precision=HIGH)
    key_all, value_all = (
        lax.all_gather(key_rows.reshape(n_pass, local_rows, width), "seq", axis=1, tiled=True),
        lax.all_gather(value_rows.reshape(n_pass, local_rows, width), "seq", axis=1, tiled=True),
    )
    key_four = key_all.reshape(n_pass, full_len, n_heads, head_dim)
    value_four = value_all.reshape(n_pass, full_len, n_heads, head_dim)
    mixed_four, log_total = attend_forward(query_local, key_four, value_four, bias_rows, key_valid)
    mixed_rows = mixed_four.reshape(row_count, width)
    hidden = inputs + jnp.dot(mixed_rows, wo_full, preferred_element_type=jnp.float32)
    normed_ffn = rms_norm(hidden, ffn_gain).astype(jnp.bfloat16)
    up_rows = jnp.dot(normed_ffn, win_full, preferred_element_type=jnp.float32)
    activated = jax.nn.gelu(up_rows).astype(jnp.bfloat16)
    output_rows = hidden + jnp.dot(activated, wff_full, preferred_element_type=jnp.float32)
    pool_part = jnp.sum(
        output_rows.reshape(n_pass, local_rows, width)
        * query_valid[:, :, None].astype(jnp.float32),
        axis=1,
    )
    pooled = lax.psum(pool_part, "seq") / lengths[:, None].astype(jnp.float32)
    gathered = (
        lax.all_gather(w_query, "dp", axis=0, tiled=True),
        lax.all_gather(w_key, "dp", axis=0, tiled=True),
        lax.all_gather(w_value, "dp", axis=0, tiled=True),
        lax.all_gather(w_attn_out, "dp", axis=0, tiled=True),
        lax.all_gather(w_in, "dp", axis=0, tiled=True),
        lax.all_gather(w_ff_out, "dp", axis=0, tiled=True),
    )
    wq_full, wk_full, wv_full, wo_full, win_full, wff_full = gathered
    grad_out = cotangent.astype(jnp.float32).reshape(row_count, width)
    grad_branch = grad_out.astype(jnp.bfloat16)
    g_ff_out = jnp.einsum("rf,rd->fd", activated, grad_branch, preferred_element_type=jnp.float32)
    grad_act = jnp.einsum("rd,fd->rf", grad_branch, wff_full, preferred_element_type=jnp.float32)
    _, gelu_pull = jax.vjp(jax.nn.gelu, up_rows)
    grad_up = gelu_pull(grad_act)[0].astype(jnp.bfloat16)
    g_in = jnp.einsum("rd,rf->df", normed_ffn, grad_up, preferred_element_type=jnp.float32)
    grad_normed_ffn = jnp.einsum("rf,df->rd", grad_up, win_full, preferred_element_type=jnp.float32)
    _, ffn_pull = jax.vjp(rms_norm, hidden, ffn_gain)
    grad_hidden_norm, g_ffn_gain = ffn_pull(grad_normed_ffn)
    grad_hidden = grad_out + grad_hidden_norm
    grad_attn = grad_hidden.astype(jnp.bfloat16)
    g_attn_out = jnp.einsum("rd,re->de", mixed_rows, grad_attn, preferred_element_type=jnp.float32)
    grad_mixed = jnp.einsum("re,de->rd", grad_attn, wo_full, preferred_element_type=jnp.float32)
    grad_mixed = grad_mixed.astype(jnp.bfloat16).reshape(n_pass, local_rows, n_heads, head_dim)
    score_sum, (grad_query, grad_key, grad_value) = attend_backward(
        query_local, key_four, value_four, grad_mixed, log_total, key_valid, bias_rows
    )
    grad_key, grad_value = (
        lax.psum_scatter(
            grad_key.reshape(n_pass, full_len, width).astype(jnp.bfloat16),
            "seq",
            scatter_dimension=1,
            tiled=True,
        ).astype(jnp.float32),
        lax.psum_scatter(
            grad_value.reshape(n_pass, full_len, width).astype(jnp.bfloat16),
            "seq",
            scatter_dimension=1,
            tiled=True,
        ).astype(jnp.float32),
    )
    grad_query = grad_query.reshape(row_count, width)
    grad_key = grad_key.astype(jnp.bfloat16).reshape(row_count, width)
    grad_value = grad_value.astype(jnp.bfloat16).reshape(row_count, width)
    g_table = jnp.einsum("qkb,hqk->bh", one_hot, score_sum, precision=HIGH)
    g_query = jnp.einsum("rd,re->de", normed, grad_query, preferred_element_type=jnp.float32)
    g_key = jnp.einsum("rd,re->de", normed, grad_key, preferred_element_type=jnp.float32)
    g_value = jnp.einsum("rd,re->de", normed, grad_value, preferred_element_type=jnp.float32)
    grad_normed = jnp.einsum("re,de->rd", grad_query, wq_full, preferred_element_type=jnp.float32)
    grad_normed = grad_normed + jnp.einsum(
        "re,de->rd", grad_key, wk_full, preferred_element_type=jnp.float32
    )
    grad_normed = grad_normed + jnp.einsum(
        "re,de->rd", grad_value, wv_full, preferred_element_type=jnp.float32
    )
    _, attn_pull = jax.vjp(rms_norm, inputs, attn_gain)
    grad_inputs_norm, g_attn_gain = attn_pull(grad_normed)
    grad_input = (
        (grad_hidden + grad_inputs_norm).astype(jnp.bfloat16).reshape(n_pass, local_rows, width)
    )
    row_grads = (
        lax.psum_scatter(g_query, "dp", scatter_dimension=0, tiled=True),
        lax.psum_scatter(g_key, "dp", scatter_dimension=0, tiled=True),
        lax.psum_scatter(g_value, "dp", scatter_dimension=0, tiled=True),
        lax.psum_scatter(g_attn_out, "dp", scatter_dimension=0, tiled=True),
        lax.psum_scatter(g_in, "dp", scatter_dimension=0, tiled=True),
        lax.psum_scatter(g_ff_out, "dp", scatter_dimension=0, tiled=True),
    )
    row_grads = (
        lax.psum(row_grads[0].astype(jnp.bfloat16), "seq").astype(jnp.float32),
        lax.psum(row_grads[1].astype(jnp.bfloat16), "seq").astype(jnp.float32),
        lax.psum(row_grads[2].astype(jnp.bfloat16), "seq").astype(jnp.float32),
        lax.psum(row_grads[3].astype(jnp.bfloat16), "seq").astype(jnp.float32),
        lax.psum(row_grads[4].astype(jnp.bfloat16), "seq").astype(jnp.float32),
        lax.psum(row_grads[5].astype(jnp.bfloat16), "seq").astype(jnp.float32),
    )
    small_sums = lax.psum((g_attn_gain, g_ffn_gain, g_table), ("dp", "seq"))
    layer_out = output_rows.astype(jnp.bfloat16).reshape(n_pass, local_rows, width)
    return (
        layer_out,
        pooled,
        grad_input,
        small_sums[0],
        row_grads[0],
        row_grads[1],
        row_grads[2],
        row_grads[3],
        small_sums[2],
        small_sums[1],
        row_grads[4],
        row_grads[5],
    )


DP, SEQ = 8, 4
FAR, EVENTS = 4, 7
BF, F32 = jnp.bfloat16, jnp.float32
MESH_ID = pl.DeviceIdType.MESH
TOKENS, WIDTH, HIDDEN, HEAD_N = 512, 768, 3072, 12
PAIRS = HEAD_N // 2
GELU_A, GELU_B = math.sqrt(2 / math.pi), 0.044715


def dg(left, right, on_left, on_right):
    return lax.dot_general(
        left, right, (((on_left,), (on_right,)), ((), ())), preferred_element_type=F32
    )


def exact(left, right, on_left, on_right):
    return lax.dot_general(
        left, right, (((on_left,), (on_right,)), ((), ())), precision=HIGH, preferred_element_type=F32
    )


def ring_dp(place):
    high = place // 4
    return 2 * (place * (1 - high) + (7 - place) * high) + high


def times(start, size, step):
    return pl.ds(pl.multiple_of(start, step), size)


def band_bucket(n_buckets):
    lane = lax.broadcasted_iota(jnp.int32, (n_buckets, 512), 1)
    relative = jnp.where(lane < 384, lane - 128, lane - 640)
    row = lax.broadcasted_iota(jnp.int32, (n_buckets, 512), 0)
    return (bucket_index(relative, n_buckets, MAXDIST) == row).astype(F32)


def layer_kernel(
    x_hbm, cot_hbm, wq_hbm, wk_hbm, wv_hbm, wo_hbm, win_hbm, wff_hbm, lengths, attn_gain, ffn_gain, table,
    out_hbm, gx_hbm, gatt_hbm, gin_hbm, gff_hbm, pool_hbm, small_out,
    watt, win, wff, gin, gff, big, probs, xs, cot, normed, qkv, mixed, nf, hid, acc, band, diag, d_both,
    sib_ff, sib_in, y_ff, y_in, r_ffa, r_ffb, r_ina, r_inb, r_att, f_ff, f_in, f_att, sums, sums_in, pool,
    ag_s, ag_r, sb_s, sb_r, yf_s, yf_r, yb_s, yb_r, rr_s, rr_r, loc, a2_s, a2_r, hs_s, hs_r, yx_s, yx_r,
    fa_s, fa_r, fo_s, fo_r, fl, bf_s, bf_r,
):
    dp, sq = lax.axis_index("dp"), lax.axis_index("seq")
    z, x, y, c = dp // 2, dp % 2, sq // 2, sq % 2
    place = x * (7 - z) + (1 - x) * z
    turn = 1 - 2 * c

    def owner(steps):
        return ring_dp((place + steps * turn + 16) % 8)

    nxt, prv = (owner(1), sq), (owner(-1), sq)
    sib, yp, ysib = (dp, 2 * y + 1 - c), (dp, 2 * (1 - y) + c), (dp, 2 * (1 - y) + 1 - c)
    xp = (2 * z + 1 - x, sq)
    z1 = (2 * (z + 1 - 2 * (z % 2)) + x, sq)
    z2 = (2 * ((z + 2) % 4) + x, sq)
    peers = (sib, yp, ysib)

    def send(src, dst, ss, rs, dev):
        return pltpu.make_async_remote_copy(
            src_ref=src, dst_ref=dst, send_sem=ss, recv_sem=rs, device_id=dev, device_id_type=MESH_ID
        )

    def when(condition, body):
        if isinstance(condition, bool):
            if condition:
                body()
        else:
            pl.when(condition)(body)

    def loop(count, body):
        def step(i, _):
            body(i)
            return 0

        lax.fori_loop(0, count, step, 0)

    barrier = pltpu.get_barrier_semaphore()
    for dev in (sib, yp, ysib, nxt, prv, xp, z1, z2):
        pl.semaphore_signal(barrier, inc=1, device_id=dev, device_id_type=MESH_ID)

    r96 = times(96 * dp, 96, 96)
    own = [pltpu.make_async_copy(w, watt.at[i, r96], loc.at[i]) for i, w in enumerate((wq_hbm, wk_hbm, wv_hbm, wo_hbm))]
    for i in range(2):
        own.append(pltpu.make_async_copy(win_hbm.at[pl.ds(48 * i, 48)], win.at[dp, i], loc.at[4 + i]))
    own.append(pltpu.make_async_copy(wff_hbm, wff.at[times(384 * dp, 384, 384)], loc.at[6]))
    mine = times(128 * sq, 128, 128)
    own.append(pltpu.make_async_copy(x_hbm.at[sq], xs.at[mine], loc.at[7]))
    own.append(pltpu.make_async_copy(cot_hbm.at[sq], cot.at[mine], loc.at[8]))
    for copy in own:
        copy.start()
    pl.semaphore_wait(barrier, 8)

    def swap(k, src_hbm, dst, at):
        dev = peers[k]
        return send(src_hbm.at[dev[1]], dst.at[mine], a2_s.at[at, k], a2_r.at[at, k], dev)

    def swap_wait(dst, at):
        for k in range(3):
            theirs = dst.at[times(128 * peers[k][1], 128, 128)]
            send(theirs, theirs, a2_s.at[at, k], a2_r.at[at, k], peers[k]).wait_recv()

    for k in range(3):
        swap(k, x_hbm, xs, 0).start()

    def piece(ch, d, cc, yy):
        if ch < 3:
            cols = pl.ds(128 + 256 * ch, 256) if ch < 2 else times(640 * yy, 128, 128)
            return watt.at[:, times(96 * d + 48 * cc, 48, 48), cols]
        if ch < 5:
            cols = pl.ds(1024, 1024) if ch == 3 else times(2048 * yy, 1024, 1024)
            return win.at[d, cc, :, cols]
        cols = pl.ds(256, 256) if ch == 5 else times(512 * yy, 256, 256)
        return wff.at[times(384 * d + 192 * cc, 192, 192), cols]

    crossing = (2, 4, 6)
    groups = ((0, 1, 2), (3, 4), (5, 6))

    def came_from(e):
        ahead = e // FAR
        return (1 - ahead) * (-e - 1) + ahead * (e - 3)

    def side(e):
        return (owner(1 - 2 * (e // FAR)), sq)

    def ring_send(ch, e):
        ahead = e // FAR
        part = piece(ch, owner((1 - ahead) * -e + ahead * (e - FAR)), c, y)
        return send(part, part, ag_s.at[ch, e], ag_r.at[ch, e], side(e))

    def hand_on(ch, e):
        part = piece(ch, owner(came_from(e)), c, y)
        return send(part, part, sb_s.at[ch, e], sb_r.at[ch, e], sib)

    def cross(ch, e):
        part = piece(ch, owner(came_from(e)), c, y)
        return send(part, part, yf_s.at[ch // 2 - 1, e], yf_r.at[ch // 2 - 1, e], yp)

    def cross_on(ch, e):
        part = piece(ch, owner(came_from(e)), c, 1 - y)
        return send(part, part, yb_s.at[ch // 2 - 1, e], yb_r.at[ch // 2 - 1, e], sib)

    def arrive(ch, e):
        part = piece(ch, owner(came_from(e)), c, y)
        send(part, part, ag_s.at[ch, e], ag_r.at[ch, e], side(e)).wait_recv()
        if e not in (FAR - 1, EVENTS - 1):
            ring_send(ch, e + 1).start()
        if ch in crossing:
            cross(ch, e).start()
        hand_on(ch, e).start()

    def arrive_cross(ch, e):
        part = piece(ch, owner(came_from(e)), c, 1 - y)
        send(part, part, yf_s.at[ch // 2 - 1, e], yf_r.at[ch // 2 - 1, e], yp).wait_recv()
        cross_on(ch, e).start()

    def both(s):
        return (s, FAR + s) if s < FAR - 1 else (s,)

    def ticks(group, s):
        for ch in reversed(groups[group]):
            for e in both(s):
                arrive(ch, e)
        if s > 0:
            for e in both(s - 1):
                arrive_cross(groups[group][-1], e)

    def gathered(group):
        arrive_cross(groups[group][-1], FAR - 1)

        def step(e):
            d = owner(-came_from(e))
            for ch in groups[group]:
                part = piece(ch, d, 1 - c, y)
                send(part, part, sb_s.at[ch, e], sb_r.at[ch, e], sib).wait_recv()
            part = piece(groups[group][-1], d, 1 - c, 1 - y)
            send(part, part, yb_s.at[group, e], yb_r.at[group, e], sib).wait_recv()

        loop(EVENTS, step)

    def gather_sent(group):
        def step(e):
            for ch in groups[group]:
                ring_send(ch, e).wait_send()
                hand_on(ch, e).wait_send()
            cross(groups[group][-1], e).wait_send()
            cross_on(groups[group][-1], e).wait_send()

        loop(EVENTS, step)

    def begin(group):
        for ch in reversed(groups[group]):
            ring_send(ch, 0).start()
            ring_send(ch, FAR).start()

    for i in range(4):
        own[i].wait()
    begin(0)

    band[pl.ds(0, HEAD_N), :] = exact(table[...], band_bucket(32), 1, 0)
    gain_a = attn_gain[...].reshape(1, WIDTH)
    gain_f = ffn_gain[...].reshape(1, WIDTH)

    ticks(0, 0)
    own[7].wait()
    swap_wait(xs, 0)
    for k in range(3):
        swap(k, cot_hbm, cot, 1).start()
    for i in range(4, 7):
        own[i].wait()

    def norm_rows(b):
        rows = times(128 * b, 128, 128)
        v = xs[rows, :].astype(F32)
        s = lax.rsqrt(jnp.mean(v * v, axis=-1, keepdims=True) + EPS)
        normed[rows, :] = (v * s * gain_a).astype(BF)

    loop(4, norm_rows)

    ticks(0, 1)
    ticks(0, 2)
    begin(1)
    ticks(0, 3)
    gathered(0)

    def project(m):
        qkv[m] = dg(normed[...], watt[m], 1, 0).astype(BF)

    loop(3, project)
    ticks(1, 0)

    count = lengths[sq]
    valid = lax.broadcasted_iota(jnp.int32, (1, TOKENS), 1) < count
    lane = lax.broadcasted_iota(jnp.int32, (1, 128), 1)
    keep = (lane < 64, lane >= 64)

    def only(h, v):
        return jnp.where(keep[h], v, jnp.zeros_like(v))

    def attend(hp):
        cols = times(128 * hp, 128, 128)
        key, value = qkv[1, :, cols], qkv[2, :, cols]
        total = [None] * 4
        for h in range(2):
            row = band[pl.ds(2 * hp + h, 1), :]
            tilted = pltpu.roll(jnp.broadcast_to(row, (128, 512)), 0, 1, stride=1, stride_axis=0)
            before = jnp.broadcast_to(row[:, 384:], (128, 128))
            after = jnp.broadcast_to(row[:, 256:384], (128, 128))
            value_h = only(h, value)
            for ib in range(4):
                rows = pl.ds(128 * ib, 128)
                blocks = []
                for jb in range(4):
                    off = jb - ib
                    if off < -1:
                        blocks.append(before)
                    elif off > 1:
                        blocks.append(after)
                    else:
                        blocks.append(tilted[:, 128 * (off + 1) : 128 * (off + 2)])
                scores = dg(only(h, qkv[0, rows, cols]), key, 1, 1) + jnp.concatenate(blocks, axis=1)
                scores = jnp.where(valid, scores, FLOOR)
                top = jnp.max(scores, axis=-1, keepdims=True)
                expo = jnp.exp(scores - top)
                part = jnp.sum(expo, axis=-1, keepdims=True)
                low = (expo * (1.0 / part)).astype(BF)
                probs[2 * hp + h, rows, :] = low
                one = dg(low, value_h, 1, 0)
                total[ib] = one if h == 0 else total[ib] + one
        for ib in range(4):
            mixed[pl.ds(128 * ib, 128), cols] = total[ib].astype(BF)

        @pl.when(hp == 1)
        def _():
            ticks(1, 1)

        @pl.when(hp == 3)
        def _():
            ticks(1, 2)
            begin(2)

        @pl.when(hp == 5)
        def _():
            ticks(1, 3)

    loop(PAIRS, attend)

    def residual(b):
        rows = times(256 * b, 256, 256)
        v = xs[rows, :].astype(F32) + dg(mixed[rows, :], watt[3], 1, 0)
        hid[rows, :] = v
        s = lax.rsqrt(jnp.mean(v * v, axis=-1, keepdims=True) + EPS)
        nf[rows, :] = (v * s * gain_f).astype(BF)

    loop(2, residual)

    ticks(2, 0)
    gathered(1)
    up_rows, down_rows = pl.ds(0, TOKENS), pl.ds(TOKENS, TOKENS)

    def block(j):
        return times(768 * j, 768, 768)

    def win_block(j):
        return win[:, :, :, block(j)].reshape(768, 768)

    def widen(j):
        v = dg(nf[...], win_block(j), 1, 0)
        sq_v = v * v
        t = jnp.tanh(v * (GELU_A + (GELU_A * GELU_B) * sq_v))
        half = 0.5 + 0.5 * t
        big[j, up_rows, :] = (v * half).astype(BF)
        slope = half + (v * half) * (1.0 - t) * (GELU_A + (3 * GELU_A * GELU_B) * sq_v)
        big[j, down_rows, :] = slope.astype(BF)

        @pl.when(j == 1)
        def _():
            ticks(2, 1)

        @pl.when(j == 3)
        def _():
            ticks(2, 2)

    loop(4, widen)
    own[8].wait()
    swap_wait(cot, 1)

    def half_ff(j):
        src = gff.at[pl.ds(2 * j, 2), times(192 * (1 - c), 192, 192)]
        return send(src, sib_ff.at[pl.ds(2 * j, 2)], hs_s.at[0, j], hs_r.at[0, j], sib)

    def grad_ff(j):
        v = dg(big[j, up_rows, :], cot[...], 0, 0).astype(BF)
        gff[pl.ds(2 * j, 2)] = v.reshape(2, 384, 768)
        half_ff(j).start()

    loop(4, grad_ff)
    ticks(2, 3)

    def merge_ff(j):
        half_ff(j).wait()
        rows = times(192 * c, 192, 192)
        for i in range(2):
            gff[2 * j + i, rows] = (gff[2 * j + i, rows].astype(F32) + sib_ff[2 * j + i].astype(F32)).astype(BF)

    loop(4, merge_ff)

    def cross_src(g, yy):
        if g == 0:
            return gff.at[:, times(192 * c + 160 * yy, 32, 32)]
        return gin.at[:, times(1536 * c + 1280 * yy, 256, 256)]

    cross_dst = (y_ff, y_in)

    def cross_sum(g):
        return send(cross_src(g, 1 - y), cross_dst[g], yx_s.at[g], yx_r.at[g], yp)

    def add_cross(g):
        cross_sum(g).wait()
        here, came = cross_src(g, y), cross_dst[g]
        here[...] = (here[...].astype(F32) + came[...].astype(F32)).astype(BF)

    def rs_piece(ch, d, yy):
        if ch < 3:
            rows = times(192 * c + 32 + 64 * ch, 64, 32) if ch < 2 else times(192 * c + 160 * yy, 32, 32)
            return gff.at[d, rows]
        if ch < 5:
            return gin.at[times(96 * d, 96, 96), times(1536 * c + 256 + 512 * (ch - 3), 512, 256)]
        if ch == 5:
            return gin.at[times(96 * d, 96, 96), times(1536 * c + 1280 * yy, 256, 256)]
        return win.at[d, c, :, pl.ds(768 * (ch - 6), 768)]

    landing = [r_ffa.at[0], r_ffa.at[1], r_ffb, r_ina.at[0], r_ina.at[1], r_inb, r_att.at[0]]
    landing += [r_ffa.at[0, :, pl.ds(0, 48)], r_ffa.at[1, :, pl.ds(0, 48)], r_att.at[1]]

    def rs_send(ch, e):
        ahead = e // FAR
        part = rs_piece(ch, owner((1 - ahead) * (FAR - e) + ahead * (e - EVENTS)), y)
        return send(part, landing[ch].at[e], rr_s.at[ch, e], rr_r.at[ch, e], side(e))

    def rs_begin(ch):
        rs_send(ch, 0).start()
        rs_send(ch, FAR).start()

    def rs_round(ch, s):
        for e in both(s):
            rs_send(ch, e).wait_recv()
            here = rs_piece(ch, owner(FAR - 1 - e if e < FAR else e - EVENTS + 1), y)
            here[...] = (here[...].astype(F32) + landing[ch][e].astype(F32)).astype(BF)
            if e not in (FAR - 1, EVENTS - 1):
                rs_send(ch, e + 1).start()

    cross_sum(0).start()
    rs_begin(0)
    rs_begin(1)
    gathered(2)

    def grad_up(j):
        v = dg(cot[...], wff[block(j), :], 1, 1) * big[j, down_rows, :].astype(F32)
        big[j, down_rows, :] = v.astype(BF)

    loop(4, grad_up)

    def grad_in(j):
        gin[:, block(j)] = dg(nf[...], big[j, down_rows, :], 0, 0).astype(BF)

        @pl.when(j == 1)
        def _():
            rs_round(0, 0)

        @pl.when(j == 3)
        def _():
            rs_round(1, 0)

    loop(4, grad_in)

    def half_in(k):
        src = gin.at[:, times(1536 * (1 - c) + 384 * k, 384, 384)]
        return send(src, sib_in.at[k], hs_s.at[1, k], hs_r.at[1, k], sib)

    for k in range(4):
        half_in(k).start()

    acc[...] = jnp.zeros_like(acc)

    def grad_nf(j):
        acc[...] += dg(big[j, down_rows, :], win_block(j), 1, 1)

        @pl.when(j == 2)
        def _():
            rs_round(0, 1)

    loop(4, grad_nf)
    add_cross(0)
    rs_begin(2)

    for k in range(4):
        half_in(k).wait()
        cols = times(1536 * c + 384 * k, 384, 384)
        gin[:, cols] = (gin[:, cols].astype(F32) + sib_in[k].astype(F32)).astype(BF)
    cross_sum(1).start()
    rs_begin(3)
    rs_begin(4)

    def norm_back(v, gain, grad):
        s = lax.rsqrt(jnp.mean(v * v, axis=-1, keepdims=True) + EPS)
        scaled = grad * gain
        back = s * scaled - v * (s * s * s) * jnp.mean(v * scaled, axis=-1, keepdims=True)
        return back, jnp.sum(grad * v * s, axis=0, keepdims=True)

    def ffn_norm_back(b, total):
        rows = times(128 * b, 128, 128)
        v = hid[rows, :]
        back, part = norm_back(v, gain_f, acc[rows, :])
        grad = cot[rows, :].astype(F32) + back
        acc[rows, :] = grad
        cot[rows, :] = grad.astype(BF)
        return total + part

    g_ffn_gain = lax.fori_loop(0, 4, ffn_norm_back, jnp.zeros((1, WIDTH), F32))

    rs_round(1, 1)
    gather_sent(1)
    win[:, :, :, block(3)] = dg(mixed[...], cot[...], 0, 0).astype(BF).reshape(8, 2, 48, 768)

    def sib_rows(t):
        return sib_ff.at[:, times(48 * t, 48, 48)]

    def half_att(t):
        return send(win.at[:, 1 - c, :, block(t)], sib_rows(t), hs_s.at[2, t], hs_r.at[2, t], sib)

    def merge_att(t):
        half_att(t).wait()
        win[:, c, :, block(t)] = (win[:, c, :, block(t)].astype(F32) + sib_rows(t)[...].astype(F32)).astype(BF)

    half_att(3).start()
    nf[...] = dg(cot[...], watt[3], 1, 1).astype(BF)

    final = [f_ff, f_in] + [f_att.at[t] for t in range(4)]

    def own_piece(g):
        if g == 0:
            return gff.at[dp, times(192 * c + 32, 128, 32)]
        if g == 1:
            return gin.at[r96, times(1536 * c + 256, 1024, 256)]
        return rs_piece(4 + g, dp, y)

    def out_piece(g, cc, yy):
        if g == 0:
            return gff_hbm.at[times(192 * cc + 32, 128, 32) if yy is None else times(192 * cc + 160 * yy, 32, 32)]
        if g == 1:
            if yy is None:
                return gin_hbm.at[:, times(1536 * cc + 256, 1024, 256)]
            return gin_hbm.at[:, times(1536 * cc + 1280 * yy, 256, 256)]
        return gatt_hbm.at[g - 2, times(48 * cc, 48, 48)]

    def share_a(g):
        return send(own_piece(g), final[g], fa_s.at[g], fa_r.at[g], yp)

    def share_b(g, k):
        return send(rs_piece(3 * g + 2, dp, y), out_piece(g, c, y), fo_s.at[g, k], fo_r.at[g, k], peers[k])

    def share_sum(g):
        return send(final[g], out_piece(g, c, None), fo_s.at[g, 3], fo_r.at[g, 3], sib)

    def keep_b(g):
        return pltpu.make_async_copy(rs_piece(3 * g + 2, dp, y), out_piece(g, c, y), fl.at[g, 0])

    def keep_sum(g):
        return pltpu.make_async_copy(final[g], out_piece(g, c, None), fl.at[g, 1])

    def finish_b(g):
        for k in range(3):
            share_b(g, k).start()
        keep_b(g).start()

    def finish_sum(g):
        share_a(g).wait()
        final[g][...] = (final[g][...].astype(F32) + own_piece(g)[...].astype(F32)).astype(BF)
        share_sum(g).start()
        keep_sum(g).start()

    rs_round(0, 2)

    flip_sum = lax.broadcasted_iota(jnp.int32, (128, 128), 0) + lax.broadcasted_iota(jnp.int32, (128, 128), 1)
    flip = (flip_sum == 127).astype(F32)

    def attend_back(hp):
        cols = times(128 * hp, 128, 128)
        key, value = qkv[1, :, cols], qkv[2, :, cols]
        query, grad = qkv[0, :, cols], nf[:, cols]
        g_query = [None] * 4
        for h in range(2):
            key_h = only(h, key)
            before = after = jnp.zeros((128, 128), F32)
            near = [jnp.zeros((128, 128), F32) for _ in range(3)]
            for ib in range(4):
                rows = pl.ds(128 * ib, 128)
                wide = probs[2 * hp + h, rows, :].astype(F32)
                d_probs = dg(only(h, nf[rows, cols]), value, 1, 1)
                mean_d = jnp.sum(wide * d_probs, axis=-1, keepdims=True)
                d_score = wide * (d_probs - mean_d)
                for jb in range(4):
                    off, part = jb - ib, d_score[:, 128 * jb : 128 * (jb + 1)]
                    if off < -1:
                        before = before + part
                    elif off > 1:
                        after = after + part
                    else:
                        near[off + 1] = near[off + 1] + part
                d_low = d_score.astype(BF)
                d_both[pl.ds(512 * h + 128 * ib, 128), :] = d_low
                one = dg(d_low, key_h, 1, 0)
                g_query[ib] = one if h == 0 else g_query[ib] + one
            tilted = exact(flip, jnp.concatenate(near, axis=1), 1, 0)
            tilted = jnp.concatenate([tilted, jnp.zeros((128, 128), F32)], axis=1)
            flat = jnp.sum(pltpu.roll(tilted, 385, 1, stride=1, stride_axis=0), axis=0, keepdims=True)
            far = jnp.concatenate(
                [
                    jnp.zeros((1, 256), F32),
                    jnp.sum(after, axis=0, keepdims=True),
                    jnp.sum(before, axis=0, keepdims=True),
                ],
                axis=1,
            )
            diag[pl.ds(2 * hp + h, 1), :] = flat + far
        both_query = jnp.concatenate([only(0, query), only(1, query)], axis=0)
        both_grad = jnp.concatenate([only(0, grad), only(1, grad)], axis=0)
        qkv[1, :, cols] = dg(d_both[...], both_query, 0, 0).astype(BF)
        qkv[2, :, cols] = dg(probs[pl.ds(2 * hp, 2)].reshape(1024, 512), both_grad, 0, 0).astype(BF)
        for ib in range(4):
            qkv[0, pl.ds(128 * ib, 128), cols] = g_query[ib].astype(BF)

        @pl.when(hp % 2 == 1)
        def _():
            t = hp // 2
            three = times(256 * t, 256, 256)
            grads = jnp.concatenate([qkv[0, :, three], qkv[1, :, three], qkv[2, :, three]], axis=1)
            win[:, :, :, block(t)] = dg(normed[...], grads, 0, 0).astype(BF).reshape(8, 2, 48, 768)
            half_att(t).start()

        def plan(at, *steps):
            @pl.when(hp == at)
            def _():
                for step in steps:
                    step()

        def round_of(ch, s):
            return lambda: rs_round(ch, s)

        def start_block(t):
            def run():
                merge_att(t)
                rs_begin(6 + t)

            return run

        def start_in():
            add_cross(1)
            rs_begin(5)

        plan(0, round_of(1, 2), round_of(0, 3), round_of(2, 0), start_block(3))
        plan(1, round_of(1, 3), round_of(2, 1), share_a(0).start, round_of(3, 0), round_of(9, 0))
        plan(2, round_of(4, 0), round_of(2, 2), round_of(3, 1), round_of(9, 1), start_in, start_block(0))
        plan(3, lambda: finish_sum(0), round_of(4, 1), round_of(2, 3), round_of(9, 2), round_of(5, 0), round_of(6, 0))
        plan(4, round_of(3, 2), round_of(4, 2), round_of(9, 3), round_of(5, 1), round_of(6, 1), start_block(1))
        plan(5, round_of(3, 3), round_of(4, 3), round_of(5, 2), round_of(6, 2), round_of(7, 0))

    loop(PAIRS, attend_back)
    finish_b(0)
    share_a(1).start()
    share_a(5).start()

    merge_att(2)
    rs_begin(8)

    def attn_norm_back(b, total):
        rows = times(256 * b, 256, 256)
        grad = dg(qkv[0, rows, :], watt[0], 1, 1) + dg(qkv[1, rows, :], watt[1], 1, 1) + dg(qkv[2, rows, :], watt[2], 1, 1)
        back, part = norm_back(xs[rows, :].astype(F32), gain_a, grad)
        mixed[rows, :] = (acc[rows, :] + back).astype(BF)
        return total + part

    g_attn_gain = lax.fori_loop(0, 2, attn_norm_back, jnp.zeros((1, WIDTH), F32))

    def give(src, dst_hbm, at, k):
        dev = peers[k]
        return send(src.at[times(128 * dev[1], 128, 128)], dst_hbm.at[sq], a2_s.at[at, k], a2_r.at[at, k], dev)

    def give_wait(src, dst_hbm, at):
        for k in range(3):
            give(src, dst_hbm, at, k).wait_send()
            theirs = dst_hbm.at[peers[k][1]]
            send(theirs, theirs, a2_s.at[at, k], a2_r.at[at, k], peers[k]).wait_recv()

    for k in range(3):
        give(mixed, gx_hbm, 3, k).start()
    gx_own = pltpu.make_async_copy(mixed.at[mine], gx_hbm.at[sq], loc.at[0])
    gx_own.start()

    sums[0] = jnp.zeros((32, 128), F32)
    sums[0, 0:16, 0:32] = exact(diag[...], band_bucket(32), 1, 1)
    for k in range(6):
        sums[0, 16 + k : 17 + k, :] = g_attn_gain[:, 128 * k : 128 * (k + 1)]
        sums[0, 22 + k : 23 + k, :] = g_ffn_gain[:, 128 * k : 128 * (k + 1)]

    def hop(k):
        dev = (sib, yp, xp, z1, z2)[k]
        return send(sums.at[k], sums_in.at[k], bf_s.at[k], bf_r.at[k], dev)

    def hop_done(k):
        hop(k).wait()
        sums[k + 1] = sums[k] + sums_in[k]

    def pool_send(k):
        return send(pool, pool_hbm.at[sq], a2_s.at[4, k], a2_r.at[4, k], peers[k])

    pool_own = pltpu.make_async_copy(pool, pool_hbm.at[sq], loc.at[2])
    lay_own = pltpu.make_async_copy(nf.at[mine], out_hbm.at[sq], loc.at[1])
    hop(0).start()
    for r in range(5):
        if r < 4:
            part = dg(big[r, up_rows, :], wff[block(r), :], 1, 0)
            acc[...] = part + (hid[...] if r == 0 else acc[...])
        if r == 0:
            rs_round(6, 3)
            share_a(2).start()
            rs_round(5, 3)
            finish_b(1)
        if r < 3:
            rs_round(7, r + 1)
        if r == 2:
            share_a(3).start()
        if r > 0:
            rs_round(8, r - 1)
        hop_done(r)
        if r < 4:
            hop(r + 1).start()
        if r == 1:
            finish_sum(1)
            finish_sum(5)
        if r == 3:
            nf[...] = acc[...].astype(BF)
            for k in range(3):
                give(nf, out_hbm, 2, k).start()
            lay_own.start()
            here_t = lax.broadcasted_iota(jnp.int32, (TOKENS, 1), 0) < count
            mean = jnp.sum(jnp.where(here_t, acc[...], 0.0), axis=0, keepdims=True) / count.astype(F32)
            pool[...] = jnp.broadcast_to(mean, (8, WIDTH))
            pool_own.start()
            for k in range(3):
                pool_send(k).start()
            finish_sum(2)
    share_a(4).start()
    small_out[...] = sums[5]
    finish_sum(3)
    finish_sum(4)

    for g in range(6):
        if g < 2:
            keep_b(g).wait()
            for k, (cc, yy) in enumerate(((1 - c, y), (c, 1 - y), (1 - c, 1 - y))):
                share_b(g, k).wait_send()
                came = out_piece(g, cc, yy)
                send(came, came, fo_s.at[g, k], fo_r.at[g, k], peers[k]).wait_recv()
        keep_sum(g).wait()
        share_sum(g).wait_send()
        came = out_piece(g, 1 - c, None)
        send(came, came, fo_s.at[g, 3], fo_r.at[g, 3], sib).wait_recv()

    def ring_sent(e):
        for ch in range(10):
            rs_send(ch, e).wait_send()

    loop(EVENTS, ring_sent)
    gather_sent(0)
    gather_sent(2)
    give_wait(nf, out_hbm, 2)
    give_wait(mixed, gx_hbm, 3)
    lay_own.wait()
    gx_own.wait()
    pool_own.wait()
    for k in range(3):
        pool_send(k).wait_send()
        theirs = pool_hbm.at[peers[k][1]]
        send(theirs, theirs, a2_s.at[4, k], a2_r.at[4, k], peers[k]).wait_recv()
        swap(k, x_hbm, xs, 0).wait_send()
        swap(k, cot_hbm, cot, 1).wait_send()


def finish_kernel(
    out_in, gx_in, g_att, g_in, g_ff, pooled, small,
    out, gx, pool_out, gain_a, gq, gk, gv, go, g_table, gain_f, gin_out, gff_out, sem,
):
    copies = [pltpu.make_async_copy(out_in, out, sem.at[0]), pltpu.make_async_copy(gx_in, gx, sem.at[1])]
    for copy in copies:
        copy.start()
    for t in range(3):
        for i, ref in enumerate((gq, gk, gv)):
            ref[:, 256 * t : 256 * (t + 1)] = g_att[t, :, 256 * i : 256 * (i + 1)].astype(F32)
    go[...] = g_att[3].astype(F32)
    gin_out[...] = g_in[...].astype(F32)
    gff_out[...] = g_ff[...].astype(F32)
    for p in range(SEQ):
        pool_out[p : p + 1, :] = pooled[p, 0:1, :]
    g_table[...] = small[0:HEAD_N, 0:32]
    for k in range(6):
        gain_a[128 * k : 128 * (k + 1)] = small[16 + k : 17 + k, :].reshape(128)
        gain_f[128 * k : 128 * (k + 1)] = small[22 + k : 23 + k, :].reshape(128)
    for copy in copies:
        copy.wait()


def passage_shards(
    passages, lengths, attn_gain, w_query, w_key, w_value, w_attn_out, bias_table, ffn_gain, w_in, w_ff_out, cotangent
):
    any_space = pl.BlockSpec(memory_space=pl.ANY)
    vmem = pl.BlockSpec(memory_space=pltpu.VMEM)
    dma = pltpu.SemaphoreType.DMA
    scratch = [
        pltpu.VMEM(shape, BF)
        for shape in (
            (4, 768, 768), (8, 2, 48, 3072), (3072, 768), (768, 3072), (8, 384, 768), (4, 1024, 768), (12, 512, 512),
            (512, 768), (512, 768), (512, 768), (3, 512, 768), (512, 768), (512, 768),
        )
    ]
    scratch += [pltpu.VMEM(shape, F32) for shape in ((512, 768), (512, 768), (16, 512), (16, 512))]
    scratch += [
        pltpu.VMEM(shape, BF)
        for shape in (
            (1024, 512), (8, 192, 768), (4, 768, 384), (8, 32, 768), (768, 256),
            (2, 7, 64, 768), (7, 32, 768), (2, 7, 96, 512), (7, 96, 256), (2, 7, 48, 768),
            (128, 768), (96, 1024), (4, 48, 768),
        )
    ]
    scratch += [pltpu.VMEM((6, 32, 128), F32), pltpu.VMEM((5, 32, 128), F32), pltpu.VMEM((8, 768), F32)]
    scratch += [
        dma(shape)
        for shape in (
            (7, 7), (7, 7), (7, 7), (7, 7), (3, 7), (3, 7), (3, 7), (3, 7), (10, 7), (10, 7), (9,), (5, 3), (5, 3),
            (3, 4), (3, 4), (2,), (2,), (6,), (6,), (6, 4), (6, 4), (6, 2), (5,), (5,),
        )
    ]
    sums = pl.pallas_call(
        layer_kernel,
        out_shape=(
            jax.ShapeDtypeStruct((4, 128, 768), BF),
            jax.ShapeDtypeStruct((4, 128, 768), BF),
            jax.ShapeDtypeStruct((4, 96, 768), BF),
            jax.ShapeDtypeStruct((96, 3072), BF),
            jax.ShapeDtypeStruct((384, 768), BF),
            jax.ShapeDtypeStruct((4, 8, 768), F32),
            jax.ShapeDtypeStruct((32, 128), F32),
        ),
        in_specs=[any_space] * 8 + [pl.BlockSpec(memory_space=pltpu.SMEM)] + [vmem] * 3,
        out_specs=(any_space,) * 6 + (vmem,),
        scratch_shapes=scratch,
        compiler_params=pltpu.CompilerParams(collective_id=0, has_side_effects=True, vmem_limit_bytes=64 * 2**20),
        name="layer",
    )(
        passages, cotangent, w_query, w_key, w_value, w_attn_out, w_in, w_ff_out, lengths,
        attn_gain, ffn_gain, bias_table.T,
    )
    square = jax.ShapeDtypeStruct((96, 768), F32)
    gain = jax.ShapeDtypeStruct((WIDTH,), F32)
    outs = pl.pallas_call(
        finish_kernel,
        out_shape=(
            jax.ShapeDtypeStruct((4, 128, 768), BF),
            jax.ShapeDtypeStruct((4, 128, 768), BF),
            jax.ShapeDtypeStruct((4, 768), F32),
            gain,
            square,
            square,
            square,
            square,
            jax.ShapeDtypeStruct((HEAD_N, 32), F32),
            gain,
            jax.ShapeDtypeStruct((96, 3072), F32),
            jax.ShapeDtypeStruct((384, 768), F32),
        ),
        in_specs=[vmem] * 7,
        out_specs=(any_space,) * 2 + (vmem,) * 10,
        scratch_shapes=[dma((2,))],
        compiler_params=pltpu.CompilerParams(vmem_limit_bytes=64 * 2**20),
        name="finish",
    )(*sums)
    return (outs[0], outs[2], outs[1], *outs[3:8], outs[8].T, *outs[9:])


def solution(mesh):
    ring = (mesh.shape["dp"], mesh.shape["seq"]) == (DP, SEQ)
    return jax.shard_map(
        passage_shards if ring else shards,
        mesh=mesh,
        in_specs=(
            P("dp", "seq", None),
            P("dp"),
            P(),
            P("dp", None),
            P("dp", None),
            P("dp", None),
            P("dp", None),
            P(),
            P(),
            P("dp", None),
            P("dp", None),
            P("dp", "seq", None),
        ),
        out_specs=(
            P("dp", "seq", None),
            P("dp", None),
            P("dp", "seq", None),
            P(),
            P("dp", None),
            P("dp", None),
            P("dp", None),
            P("dp", None),
            P(),
            P(),
            P("dp", None),
            P("dp", None),
        ),
        check_vma=False,
    )
```

```python
import math

import jax
import jax.numpy as jnp
from jax import lax
from jax.experimental import pallas as pl
from jax.experimental.pallas import tpu as pltpu
from jax.sharding import PartitionSpec as P

MAXDIST = 128


EPS = 1e-06
HIGH = lax.Precision.HIGHEST
FLOOR = -1e30


def bucket_index(relative, buckets, reach):
    half_count = buckets // 2
    exact_count = half_count // 2
    distance = jnp.abs(relative)
    result = jnp.minimum(distance, exact_count)
    for power in range(1, half_count - exact_count):
        bound_at = math.ceil(
            exact_count * (reach / exact_count) ** (power / (half_count - exact_count)) - 1e-06
        )
        result = result + (distance >= bound_at).astype(jnp.int32)
    return result + (relative > 0).astype(jnp.int32) * half_count


def rms_norm(values, gain_vec):
    return values * lax.rsqrt(jnp.mean(values * values, axis=-1, keepdims=True) + EPS) * gain_vec


def attend_forward(query_four, key_four, value_four, bias_rows, key_valid):
    scores = (
        jnp.einsum("pqhe,pkhe->phqk", query_four, key_four, preferred_element_type=jnp.float32)
        + bias_rows[None]
    )
    scores = jnp.where(key_valid[:, None, None, :], scores, FLOOR)
    row_top = jnp.max(scores, axis=-1, keepdims=True)
    expo = jnp.exp(scores - row_top)
    row_total = jnp.sum(expo, axis=-1, keepdims=True)
    log_total = row_top + jnp.log(row_total)
    attn_probs = (expo / row_total).astype(jnp.bfloat16)
    mixed_rows = jnp.einsum(
        "phqk,pkhe->pqhe", attn_probs, value_four, preferred_element_type=jnp.float32
    )
    return (mixed_rows.astype(jnp.bfloat16), log_total)


def attend_backward(query_four, key_four, value_four, grad_mixed, log_total, key_valid, bias_rows):

    def one_passage(score_sum, pieces):
        query_p, key_p, value_p, grad_p, log_p, valid_p = pieces
        score_p = (
            jnp.einsum("qhe,khe->hqk", query_p, key_p, preferred_element_type=jnp.float32)
            + bias_rows
        )
        score_p = jnp.where(valid_p[None, None, :], score_p, FLOOR)
        prob_p = jnp.exp(score_p - log_p)
        grad_prob = jnp.einsum("qhe,khe->hqk", grad_p, value_p, preferred_element_type=jnp.float32)
        grad_score = (
            prob_p * (grad_prob - jnp.sum(prob_p * grad_prob, axis=-1, keepdims=True))
        ).astype(jnp.bfloat16)
        grad_query_p = jnp.einsum(
            "hqk,khe->qhe", grad_score, key_p, preferred_element_type=jnp.float32
        ).astype(jnp.bfloat16)
        grad_key_p = jnp.einsum(
            "hqk,qhe->khe", grad_score, query_p, preferred_element_type=jnp.float32
        )
        grad_value_p = jnp.einsum(
            "hqk,qhe->khe", prob_p.astype(jnp.bfloat16), grad_p, preferred_element_type=jnp.float32
        )
        return (
            score_sum + grad_score.astype(jnp.float32),
            (grad_query_p, grad_key_p, grad_value_p),
        )

    start_sum = jnp.zeros(bias_rows.shape, jnp.float32)
    return lax.scan(
        one_passage, start_sum, (query_four, key_four, value_four, grad_mixed, log_total, key_valid)
    )


def shards(
    passages,
    lengths,
    attn_gain,
    w_query,
    w_key,
    w_value,
    w_attn_out,
    bias_table,
    ffn_gain,
    w_in,
    w_ff_out,
    cotangent,
):
    n_pass, local_rows, width = passages.shape
    n_buckets, n_heads = bias_table.shape
    head_dim = width // n_heads
    seq_count = lax.axis_size("seq")
    full_len = local_rows * seq_count
    row_count = n_pass * local_rows
    first_row = lax.axis_index("seq") * local_rows
    gathered = (
        lax.all_gather(w_query, "dp", axis=0, tiled=True),
        lax.all_gather(w_key, "dp", axis=0, tiled=True),
        lax.all_gather(w_value, "dp", axis=0, tiled=True),
        lax.all_gather(w_attn_out, "dp", axis=0, tiled=True),
        lax.all_gather(w_in, "dp", axis=0, tiled=True),
        lax.all_gather(w_ff_out, "dp", axis=0, tiled=True),
    )
    wq_full, wk_full, wv_full, wo_full, win_full, wff_full = gathered
    key_pos = jnp.arange(full_len, dtype=jnp.int32)
    query_pos = first_row + jnp.arange(local_rows, dtype=jnp.int32)
    key_valid = key_pos[None, :] < lengths[:, None]
    query_valid = query_pos[None, :] < lengths[:, None]
    inputs = passages.astype(jnp.float32).reshape(row_count, width)
    normed = rms_norm(inputs, attn_gain).astype(jnp.bfloat16)
    query_rows = jnp.dot(normed, wq_full, preferred_element_type=jnp.float32).astype(jnp.bfloat16)
    key_rows = jnp.dot(normed, wk_full, preferred_element_type=jnp.float32).astype(jnp.bfloat16)
    value_rows = jnp.dot(normed, wv_full, preferred_element_type=jnp.float32).astype(jnp.bfloat16)
    query_local = query_rows.reshape(n_pass, local_rows, n_heads, head_dim)
    relative = key_pos[None, :] - query_pos[:, None]
    one_hot = (
        bucket_index(relative, n_buckets, MAXDIST)[:, :, None]
        == jnp.arange(n_buckets, dtype=jnp.int32)
    ).astype(jnp.float32)
    bias_rows = jnp.einsum("qkb,bh->hqk", one_hot, bias_table, precision=HIGH)
    key_all, value_all = (
        lax.all_gather(key_rows.reshape(n_pass, local_rows, width), "seq", axis=1, tiled=True),
        lax.all_gather(value_rows.reshape(n_pass, local_rows, width), "seq", axis=1, tiled=True),
    )
    key_four = key_all.reshape(n_pass, full_len, n_heads, head_dim)
    value_four = value_all.reshape(n_pass, full_len, n_heads, head_dim)
    mixed_four, log_total = attend_forward(query_local, key_four, value_four, bias_rows, key_valid)
    mixed_rows = mixed_four.reshape(row_count, width)
    hidden = inputs + jnp.dot(mixed_rows, wo_full, preferred_element_type=jnp.float32)
    normed_ffn = rms_norm(hidden, ffn_gain).astype(jnp.bfloat16)
    up_rows = jnp.dot(normed_ffn, win_full, preferred_element_type=jnp.float32)
    activated = jax.nn.gelu(up_rows).astype(jnp.bfloat16)
    output_rows = hidden + jnp.dot(activated, wff_full, preferred_element_type=jnp.float32)
    pool_part = jnp.sum(
        output_rows.reshape(n_pass, local_rows, width)
        * query_valid[:, :, None].astype(jnp.float32),
        axis=1,
    )
    pooled = lax.psum(pool_part, "seq") / lengths[:, None].astype(jnp.float32)
    gathered = (
        lax.all_gather(w_query, "dp", axis=0, tiled=True),
        lax.all_gather(w_key, "dp", axis=0, tiled=True),
        lax.all_gather(w_value, "dp", axis=0, tiled=True),
        lax.all_gather(w_attn_out, "dp", axis=0, tiled=True),
        lax.all_gather(w_in, "dp", axis=0, tiled=True),
        lax.all_gather(w_ff_out, "dp", axis=0, tiled=True),
    )
    wq_full, wk_full, wv_full, wo_full, win_full, wff_full = gathered
    grad_out = cotangent.astype(jnp.float32).reshape(row_count, width)
    grad_branch = grad_out.astype(jnp.bfloat16)
    g_ff_out = jnp.einsum("rf,rd->fd", activated, grad_branch, preferred_element_type=jnp.float32)
    grad_act = jnp.einsum("rd,fd->rf", grad_branch, wff_full, preferred_element_type=jnp.float32)
    _, gelu_pull = jax.vjp(jax.nn.gelu, up_rows)
    grad_up = gelu_pull(grad_act)[0].astype(jnp.bfloat16)
    g_in = jnp.einsum("rd,rf->df", normed_ffn, grad_up, preferred_element_type=jnp.float32)
    grad_normed_ffn = jnp.einsum("rf,df->rd", grad_up, win_full, preferred_element_type=jnp.float32)
    _, ffn_pull = jax.vjp(rms_norm, hidden, ffn_gain)
    grad_hidden_norm, g_ffn_gain = ffn_pull(grad_normed_ffn)
    grad_hidden = grad_out + grad_hidden_norm
    grad_attn = grad_hidden.astype(jnp.bfloat16)
    g_attn_out = jnp.einsum("rd,re->de", mixed_rows, grad_attn, preferred_element_type=jnp.float32)
    grad_mixed = jnp.einsum("re,de->rd", grad_attn, wo_full, preferred_element_type=jnp.float32)
    grad_mixed = grad_mixed.astype(jnp.bfloat16).reshape(n_pass, local_rows, n_heads, head_dim)
    score_sum, (grad_query, grad_key, grad_value) = attend_backward(
        query_local, key_four, value_four, grad_mixed, log_total, key_valid, bias_rows
    )
    grad_key, grad_value = (
        lax.psum_scatter(
            grad_key.reshape(n_pass, full_len, width).astype(jnp.bfloat16),
            "seq",
            scatter_dimension=1,
            tiled=True,
        ).astype(jnp.float32),
        lax.psum_scatter(
            grad_value.reshape(n_pass, full_len, width).astype(jnp.bfloat16),
            "seq",
            scatter_dimension=1,
            tiled=True,
        ).astype(jnp.float32),
    )
    grad_query = grad_query.reshape(row_count, width)
    grad_key = grad_key.astype(jnp.bfloat16).reshape(row_count, width)
    grad_value = grad_value.astype(jnp.bfloat16).reshape(row_count, width)
    g_table = jnp.einsum("qkb,hqk->bh", one_hot, score_sum, precision=HIGH)
    g_query = jnp.einsum("rd,re->de", normed, grad_query, preferred_element_type=jnp.float32)
    g_key = jnp.einsum("rd,re->de", normed, grad_key, preferred_element_type=jnp.float32)
    g_value = jnp.einsum("rd,re->de", normed, grad_value, preferred_element_type=jnp.float32)
    grad_normed = jnp.einsum("re,de->rd", grad_query, wq_full, preferred_element_type=jnp.float32)
    grad_normed = grad_normed + jnp.einsum(
        "re,de->rd", grad_key, wk_full, preferred_element_type=jnp.float32
    )
    grad_normed = grad_normed + jnp.einsum(
        "re,de->rd", grad_value, wv_full, preferred_element_type=jnp.float32
    )
    _, attn_pull = jax.vjp(rms_norm, inputs, attn_gain)
    grad_inputs_norm, g_attn_gain = attn_pull(grad_normed)
    grad_input = (
        (grad_hidden + grad_inputs_norm).astype(jnp.bfloat16).reshape(n_pass, local_rows, width)
    )
    row_grads = (
        lax.psum_scatter(g_query, "dp", scatter_dimension=0, tiled=True),
        lax.psum_scatter(g_key, "dp", scatter_dimension=0, tiled=True),
        lax.psum_scatter(g_value, "dp", scatter_dimension=0, tiled=True),
        lax.psum_scatter(g_attn_out, "dp", scatter_dimension=0, tiled=True),
        lax.psum_scatter(g_in, "dp", scatter_dimension=0, tiled=True),
        lax.psum_scatter(g_ff_out, "dp", scatter_dimension=0, tiled=True),
    )
    row_grads = (
        lax.psum(row_grads[0].astype(jnp.bfloat16), "seq").astype(jnp.float32),
        lax.psum(row_grads[1].astype(jnp.bfloat16), "seq").astype(jnp.float32),
        lax.psum(row_grads[2].astype(jnp.bfloat16), "seq").astype(jnp.float32),
        lax.psum(row_grads[3].astype(jnp.bfloat16), "seq").astype(jnp.float32),
        lax.psum(row_grads[4].astype(jnp.bfloat16), "seq").astype(jnp.float32),
        lax.psum(row_grads[5].astype(jnp.bfloat16), "seq").astype(jnp.float32),
    )
    small_sums = lax.psum((g_attn_gain, g_ffn_gain, g_table), ("dp", "seq"))
    layer_out = output_rows.astype(jnp.bfloat16).reshape(n_pass, local_rows, width)
    return (
        layer_out,
        pooled,
        grad_input,
        small_sums[0],
        row_grads[0],
        row_grads[1],
        row_grads[2],
        row_grads[3],
        small_sums[2],
        small_sums[1],
        row_grads[4],
        row_grads[5],
    )


DP, SEQ = 8, 4
FAR, EVENTS = 4, 7
BF, F32 = jnp.bfloat16, jnp.float32
MESH_ID = pl.DeviceIdType.MESH
TOKENS, WIDTH, HIDDEN, HEAD_N = 512, 768, 3072, 12
PAIRS = HEAD_N // 2
GELU_A, GELU_B = math.sqrt(2 / math.pi), 0.044715


AG, CR, BEGIN, RS, HALF, GO, XC, SHARE_A, FIN_B, FSUM, HOP = range(11)
(
    AT_A1, AT_NORM, AT_ATT, AT_WO, AT_IN, AT_COTW, AT_MFF, AT_FF, AT_FNORM, AT_PREWO, AT_GWO, AT_GMIX, AT_LAY,
    AT_GX, AT_TAIL, AT_PROJECT, AT_ATTEND, AT_RESIDUAL, AT_WIDEN, AT_GFF, AT_GUP, AT_GIN, AT_GNF, AT_NARROW, AT_AB,
    AT_GN,
) = range(26)
PLAN = {
    AT_A1: (
        (AG, 2, 0), (AG, 2, 4), (AG, 1, 0), (AG, 1, 4), (AG, 0, 0), (AG, 0, 4), (AG, 2, 1), (AG, 2, 5), (AG, 1, 1),
        (AG, 1, 5), (AG, 0, 1), (AG, 0, 5), (AG, 2, 2),
    ),
    AT_NORM: (
        (AG, 2, 6),
    ),
    AT_ATT: (
        (CR, 2, 0), (AG, 1, 2), (CR, 2, 4), (AG, 1, 6), (CR, 2, 1), (AG, 0, 2), (BEGIN, 3), (BEGIN, 1), (CR, 2, 5),
        (AG, 0, 6), (AG, 2, 3), (CR, 2, 2), (AG, 1, 3), (CR, 2, 6), (AG, 0, 3), (AG, 7, 0), (CR, 2, 3), (AG, 7, 4),
        (AG, 4, 0),
    ),
    (AT_PROJECT, 0): (
        (AG, 4, 4),
    ),
    (AT_PROJECT, 2): (
        (AG, 3, 0),
    ),
    (AT_ATTEND, 0): (
        (CR, 4, 0), (AG, 3, 4), (AG, 7, 1),
    ),
    (AT_ATTEND, 1): (
        (AG, 7, 5), (AG, 4, 1), (AG, 4, 5),
    ),
    (AT_ATTEND, 2): (
        (AG, 3, 1),
    ),
    (AT_ATTEND, 3): (
        (AG, 3, 5), (AG, 7, 2),
    ),
    (AT_ATTEND, 4): (
        (AG, 7, 6), (AG, 4, 2), (AG, 4, 6), (CR, 4, 4),
    ),
    (AT_ATTEND, 5): (
        (AG, 3, 2), (CR, 4, 1), (BEGIN, 2),
    ),
    AT_WO: (
        (AG, 3, 6), (CR, 4, 5), (AG, 7, 3), (AG, 4, 3), (CR, 4, 2),
    ),
    (AT_RESIDUAL, 1): (
        (AG, 3, 3), (CR, 4, 6),
    ),
    AT_IN: (
        (AG, 6, 0), (CR, 4, 3), (AG, 6, 4), (AG, 5, 0),
    ),
    (AT_WIDEN, 0): (
        (AG, 5, 4),
    ),
    (AT_WIDEN, 1): (
        (CR, 6, 0), (AG, 6, 1), (AG, 6, 5),
    ),
    (AT_WIDEN, 2): (
        (CR, 6, 4), (AG, 5, 1),
    ),
    (AT_WIDEN, 3): (
        (AG, 5, 5),
    ),
    (AT_GFF, 0): (
        (AG, 6, 2),
    ),
    (AT_GFF, 1): (
        (CR, 6, 1), (AG, 6, 6),
    ),
    (AT_GFF, 2): (
        (AG, 5, 2),
    ),
    (AT_GFF, 3): (
        (CR, 6, 5), (AG, 5, 6), (HALF, 0, 0),
    ),
    AT_MFF: (
        (AG, 6, 3), (HALF, 0, 1), (CR, 6, 2), (AG, 5, 3), (HALF, 0, 2), (HALF, 0, 3), (GO, 0), (CR, 6, 6),
    ),
    AT_FF: (
        (CR, 6, 3), (RS, 0, 0),
    ),
    (AT_GUP, 0): (
        (RS, 0, 4),
    ),
    (AT_GUP, 1): (
        (RS, 1, 0),
    ),
    (AT_GUP, 3): (
        (RS, 1, 4),
    ),
    (AT_GIN, 0): (
        (RS, 0, 1),
    ),
    (AT_GIN, 1): (
        (RS, 0, 5),
    ),
    (AT_GIN, 2): (
        (RS, 1, 1),
    ),
    (AT_GIN, 3): (
        (RS, 1, 5), (XC, 0),
    ),
    (AT_GNF, 0): (
        (RS, 0, 2),
    ),
    (AT_GNF, 2): (
        (RS, 0, 6), (HALF, 1, 0),
    ),
    (AT_GNF, 3): (
        (RS, 1, 2), (HALF, 1, 1), (RS, 1, 6),
    ),
    AT_FNORM: (
        (RS, 2, 0), (HALF, 1, 2), (RS, 2, 4),
    ),
    AT_GWO: (
        (HALF, 1, 3), (GO, 1), (RS, 0, 3),
    ),
    AT_GMIX: (
        (RS, 1, 3), (SHARE_A, 0),
    ),
    (AT_NARROW, 0): (
        (RS, 2, 1), (RS, 2, 5),
    ),
    (AT_NARROW, 1): (
        (HALF, 2, 3), (GO, 5), (RS, 3, 0),
    ),
    (AT_NARROW, 3): (
        (RS, 3, 4),
    ),
    AT_LAY: (
        (RS, 4, 0),
    ),
    (AT_AB, 0): (
        (RS, 4, 4), (RS, 2, 2), (RS, 2, 6), (RS, 9, 0),
    ),
    (AT_AB, 1): (
        (RS, 9, 4), (RS, 3, 1), (XC, 1), (RS, 3, 5), (RS, 4, 1),
    ),
    (AT_AB, 2): (
        (RS, 4, 5), (RS, 2, 3), (FIN_B, 0), (RS, 9, 1), (FSUM, 0), (HALF, 2, 0), (GO, 2), (RS, 9, 5),
    ),
    (AT_AB, 3): (
        (RS, 3, 2), (RS, 5, 0), (RS, 5, 4), (RS, 3, 6), (RS, 4, 2), (RS, 4, 6),
    ),
    (AT_AB, 4): (
        (RS, 9, 2), (RS, 6, 0), (RS, 6, 4), (HALF, 2, 1), (GO, 3), (RS, 9, 6),
    ),
    (AT_AB, 5): (
        (RS, 3, 3), (RS, 5, 1), (RS, 5, 5), (RS, 4, 3), (SHARE_A, 1), (RS, 9, 3), (SHARE_A, 5),
    ),
    (AT_GN, 0): (
        (RS, 6, 1), (RS, 6, 5),
    ),
    (AT_GN, 1): (
        (RS, 7, 0), (RS, 7, 4), (HALF, 2, 2), (GO, 4),
    ),
    AT_TAIL: (
        (RS, 5, 2), (RS, 5, 6), (RS, 6, 2), (RS, 6, 6), (RS, 7, 1), (FSUM, 1), (RS, 7, 5), (RS, 8, 0), (FSUM, 5),
        (HOP, 0), (RS, 8, 4), (RS, 5, 3), (FIN_B, 1), (RS, 6, 3), (SHARE_A, 2), (HOP, 1), (RS, 7, 2), (RS, 7, 6),
        (RS, 8, 1), (RS, 8, 5), (RS, 7, 3), (SHARE_A, 3), (HOP, 2), (RS, 8, 2), (RS, 8, 6), (RS, 8, 3), (SHARE_A, 4),
        (HOP, 3), (FSUM, 2), (HOP, 4), (FSUM, 3), (FSUM, 4),
    ),
}

def dg(left, right, on_left, on_right):
    return lax.dot_general(
        left, right, (((on_left,), (on_right,)), ((), ())), preferred_element_type=F32
    )


def exact(left, right, on_left, on_right):
    return lax.dot_general(
        left, right, (((on_left,), (on_right,)), ((), ())), precision=HIGH, preferred_element_type=F32
    )


def ring_dp(place):
    high = place // 4
    return 2 * (place * (1 - high) + (7 - place) * high) + high


def times(start, size, step):
    return pl.ds(pl.multiple_of(start, step), size)


def band_bucket(n_buckets):
    lane = lax.broadcasted_iota(jnp.int32, (n_buckets, 512), 1)
    relative = jnp.where(lane < 384, lane - 128, lane - 640)
    row = lax.broadcasted_iota(jnp.int32, (n_buckets, 512), 0)
    return (bucket_index(relative, n_buckets, MAXDIST) == row).astype(F32)


def layer_kernel(
    x_hbm, cot_hbm, wq_hbm, wk_hbm, wv_hbm, wo_hbm, win_hbm, wff_hbm, lengths, attn_gain, ffn_gain, table,
    out_hbm, gx_hbm, gatt_hbm, gin_hbm, gff_hbm, pool_hbm, small_out,
    watt, win, wff, gin, gff, big, probs, xs, cot, normed, qkv, mixed, nf, hid, acc, band, diag, d_both,
    sib_ff, sib_in, y_ff, y_in, r_ffa, r_ffb, r_ina, r_inb, r_att, f_ff, f_in, f_att, sums, sums_in, pool,
    ag_s, ag_r, sb_s, sb_r, yf_s, yf_r, yb_s, yb_r, rr_s, rr_r, loc, a2_s, a2_r, hs_s, hs_r, yx_s, yx_r,
    fa_s, fa_r, fo_s, fo_r, fl, bf_s, bf_r,
):
    dp, sq = lax.axis_index("dp"), lax.axis_index("seq")
    z, x, y, c = dp // 2, dp % 2, sq // 2, sq % 2
    place = x * (7 - z) + (1 - x) * z
    turn = 1 - 2 * c

    def owner(steps):
        return ring_dp((place + steps * turn + 16) % 8)

    nxt, prv = (owner(1), sq), (owner(-1), sq)
    sib, yp, ysib = (dp, 2 * y + 1 - c), (dp, 2 * (1 - y) + c), (dp, 2 * (1 - y) + 1 - c)
    xp = (2 * z + 1 - x, sq)
    z1 = (2 * (z + 1 - 2 * (z % 2)) + x, sq)
    z2 = (2 * ((z + 2) % 4) + x, sq)
    peers = (sib, yp, ysib)

    def send(src, dst, ss, rs, dev):
        return pltpu.make_async_remote_copy(
            src_ref=src, dst_ref=dst, send_sem=ss, recv_sem=rs, device_id=dev, device_id_type=MESH_ID
        )

    def when(condition, body):
        if isinstance(condition, bool):
            if condition:
                body()
        else:
            pl.when(condition)(body)

    def loop(count, body):
        def step(i, _):
            body(i)
            return 0

        lax.fori_loop(0, count, step, 0)

    barrier = pltpu.get_barrier_semaphore()
    for dev in (sib, yp, ysib, nxt, prv, xp, z1, z2):
        pl.semaphore_signal(barrier, inc=1, device_id=dev, device_id_type=MESH_ID)

    r96 = times(96 * dp, 96, 96)
    own = [pltpu.make_async_copy(w, watt.at[i, r96], loc.at[i]) for i, w in enumerate((wq_hbm, wk_hbm, wv_hbm, wo_hbm))]
    for i in range(2):
        own.append(pltpu.make_async_copy(win_hbm.at[pl.ds(48 * i, 48)], win.at[dp, i], loc.at[4 + i]))
    own.append(pltpu.make_async_copy(wff_hbm, wff.at[times(384 * dp, 384, 384)], loc.at[6]))
    mine = times(128 * sq, 128, 128)
    own.append(pltpu.make_async_copy(x_hbm.at[sq], xs.at[mine], loc.at[7]))
    own.append(pltpu.make_async_copy(cot_hbm.at[sq], cot.at[mine], loc.at[8]))
    for copy in own:
        copy.start()
    pl.semaphore_wait(barrier, 8)

    def swap(k, src_hbm, dst, at):
        dev = peers[k]
        return send(src_hbm.at[dev[1]], dst.at[mine], a2_s.at[at, k], a2_r.at[at, k], dev)

    def swap_wait(dst, at):
        for k in range(3):
            theirs = dst.at[times(128 * peers[k][1], 128, 128)]
            send(theirs, theirs, a2_s.at[at, k], a2_r.at[at, k], peers[k]).wait_recv()

    for k in range(3):
        swap(k, x_hbm, xs, 0).start()

    def piece(ch, d, cc, yy):
        if ch < 3:
            cols = pl.ds(128 + 256 * ch, 256) if ch < 2 else times(640 * yy, 128, 128)
            return watt.at[0:3, times(96 * d + 48 * cc, 48, 48), cols]
        if ch < 5:
            cols = pl.ds(768, 1536) if ch == 3 else times(2304 * yy, 768, 768)
            return win.at[d, cc, :, cols]
        if ch == 7:
            return watt.at[3, times(96 * d + 48 * cc, 48, 48)]
        cols = pl.ds(256, 256) if ch == 5 else times(512 * yy, 256, 256)
        return wff.at[times(384 * d + 192 * cc, 192, 192), cols]

    crossing = (2, 4, 6)
    groups = ((0, 1, 2), (3, 4), (5, 6), (7,))

    def came_from(e):
        ahead = e // FAR
        return (1 - ahead) * (-e - 1) + ahead * (e - 3)

    def side(e):
        return (owner(1 - 2 * (e // FAR)), sq)

    def ring_send(ch, e):
        ahead = e // FAR
        part = piece(ch, owner((1 - ahead) * -e + ahead * (e - FAR)), c, y)
        return send(part, part, ag_s.at[ch, e], ag_r.at[ch, e], side(e))

    def hand_on(ch, e):
        part = piece(ch, owner(came_from(e)), c, y)
        return send(part, part, sb_s.at[ch, e], sb_r.at[ch, e], sib)

    def cross(ch, e):
        part = piece(ch, owner(came_from(e)), c, y)
        return send(part, part, yf_s.at[ch // 2 - 1, e], yf_r.at[ch // 2 - 1, e], yp)

    def cross_on(ch, e):
        part = piece(ch, owner(came_from(e)), c, 1 - y)
        return send(part, part, yb_s.at[ch // 2 - 1, e], yb_r.at[ch // 2 - 1, e], sib)

    def arrive(ch, e):
        part = piece(ch, owner(came_from(e)), c, y)
        send(part, part, ag_s.at[ch, e], ag_r.at[ch, e], side(e)).wait_recv()
        if e not in (FAR - 1, EVENTS - 1):
            ring_send(ch, e + 1).start()
        if ch in crossing:
            cross(ch, e).start()
        hand_on(ch, e).start()

    def arrive_cross(ch, e):
        part = piece(ch, owner(came_from(e)), c, 1 - y)
        send(part, part, yf_s.at[ch // 2 - 1, e], yf_r.at[ch // 2 - 1, e], yp).wait_recv()
        cross_on(ch, e).start()

    def settled(group):
        last = groups[group][-1]

        def step(e):
            d = owner(-came_from(e))
            for ch in groups[group]:
                part = piece(ch, d, 1 - c, y)
                send(part, part, sb_s.at[ch, e], sb_r.at[ch, e], sib).wait_recv()
            if last in crossing:
                part = piece(last, d, 1 - c, 1 - y)
                send(part, part, yb_s.at[group, e], yb_r.at[group, e], sib).wait_recv()

        loop(EVENTS, step)

    def gather_sent(group):
        def step(e):
            for ch in groups[group]:
                ring_send(ch, e).wait_send()
                hand_on(ch, e).wait_send()
            if groups[group][-1] in crossing:
                cross(groups[group][-1], e).wait_send()
                cross_on(groups[group][-1], e).wait_send()

        loop(EVENTS, step)

    def begin(group):
        for ch in reversed(groups[group]):
            ring_send(ch, 0).start()
            ring_send(ch, FAR).start()

    acts = {AG: arrive, CR: arrive_cross, BEGIN: begin}

    def serve(slot):
        for name, *place in PLAN.get(slot, ()):
            acts[name](*place)

    def serve_at(slot, count, i):
        for k in range(count):
            if (slot, k) in PLAN:

                @pl.when(i == k)
                def _(k=k):
                    serve((slot, k))

    for i in range(4):
        own[i].wait()
    begin(0)

    band[pl.ds(0, HEAD_N), :] = exact(table[...], band_bucket(32), 1, 0)
    gain_a = attn_gain[...].reshape(1, WIDTH)
    gain_f = ffn_gain[...].reshape(1, WIDTH)

    serve(AT_A1)
    own[7].wait()
    swap_wait(xs, 0)
    for i in range(4, 7):
        own[i].wait()

    def norm_rows(b):
        rows = times(128 * b, 128, 128)
        v = xs[rows, :].astype(F32)
        s = lax.rsqrt(jnp.mean(v * v, axis=-1, keepdims=True) + EPS)
        normed[rows, :] = (v * s * gain_a).astype(BF)

    loop(4, norm_rows)

    serve(AT_NORM)
    serve(AT_ATT)
    settled(0)
    for k in range(3):
        swap(k, cot_hbm, cot, 1).start()

    def project(m):
        qkv[m] = dg(normed[...], watt[m], 1, 0).astype(BF)
        serve_at(AT_PROJECT, 3, m)

    loop(3, project)

    count = lengths[sq]
    valid = lax.broadcasted_iota(jnp.int32, (1, TOKENS), 1) < count
    lane = lax.broadcasted_iota(jnp.int32, (1, 128), 1)
    keep = (lane < 64, lane >= 64)

    def only(h, v):
        return jnp.where(keep[h], v, jnp.zeros_like(v))

    def attend(hp):
        cols = times(128 * hp, 128, 128)
        key, value = qkv[1, :, cols], qkv[2, :, cols]
        total = [None] * 4
        for h in range(2):
            row = band[pl.ds(2 * hp + h, 1), :]
            tilted = pltpu.roll(jnp.broadcast_to(row, (128, 512)), 0, 1, stride=1, stride_axis=0)
            before = jnp.broadcast_to(row[:, 384:], (128, 128))
            after = jnp.broadcast_to(row[:, 256:384], (128, 128))
            value_h = only(h, value)
            for ib in range(4):
                rows = pl.ds(128 * ib, 128)
                blocks = []
                for jb in range(4):
                    off = jb - ib
                    if off < -1:
                        blocks.append(before)
                    elif off > 1:
                        blocks.append(after)
                    else:
                        blocks.append(tilted[:, 128 * (off + 1) : 128 * (off + 2)])
                scores = dg(only(h, qkv[0, rows, cols]), key, 1, 1) + jnp.concatenate(blocks, axis=1)
                scores = jnp.where(valid, scores, FLOOR)
                top = jnp.max(scores, axis=-1, keepdims=True)
                expo = jnp.exp(scores - top)
                part = jnp.sum(expo, axis=-1, keepdims=True)
                low = (expo * (1.0 / part)).astype(BF)
                probs[2 * hp + h, rows, :] = low
                one = dg(low, value_h, 1, 0)
                total[ib] = one if h == 0 else total[ib] + one
        for ib in range(4):
            mixed[pl.ds(128 * ib, 128), cols] = total[ib].astype(BF)
        serve_at(AT_ATTEND, PAIRS, hp)

    loop(PAIRS, attend)
    serve(AT_WO)
    settled(3)

    def residual(b):
        rows = times(256 * b, 256, 256)
        v = xs[rows, :].astype(F32) + dg(mixed[rows, :], watt[3], 1, 0)
        hid[rows, :] = v
        s = lax.rsqrt(jnp.mean(v * v, axis=-1, keepdims=True) + EPS)
        nf[rows, :] = (v * s * gain_f).astype(BF)
        serve_at(AT_RESIDUAL, 2, b)

    loop(2, residual)

    serve(AT_IN)
    settled(1)
    up_rows, down_rows = pl.ds(0, TOKENS), pl.ds(TOKENS, TOKENS)

    def block(j):
        return times(768 * j, 768, 768)

    def win_block(j):
        return win[:, :, :, block(j)].reshape(768, 768)

    def widen(j):
        v = dg(nf[...], win_block(j), 1, 0)
        sq_v = v * v
        t = jnp.tanh(v * (GELU_A + (GELU_A * GELU_B) * sq_v))
        half = 0.5 + 0.5 * t
        big[j, up_rows, :] = (v * half).astype(BF)
        slope = half + (v * half) * (1.0 - t) * (GELU_A + (3 * GELU_A * GELU_B) * sq_v)
        big[j, down_rows, :] = slope.astype(BF)
        serve_at(AT_WIDEN, 4, j)

    loop(4, widen)
    serve(AT_COTW)
    own[8].wait()
    swap_wait(cot, 1)

    def half_ff(j):
        src = gff.at[pl.ds(2 * j, 2), times(192 * (1 - c), 192, 192)]
        return send(src, sib_ff.at[pl.ds(2 * j, 2)], hs_s.at[0, j], hs_r.at[0, j], sib)

    def grad_ff(j):
        v = dg(big[j, up_rows, :], cot[...], 0, 0).astype(BF)
        gff[pl.ds(2 * j, 2)] = v.reshape(2, 384, 768)
        half_ff(j).start()
        serve_at(AT_GFF, 4, j)


    def merge_ff(j):
        half_ff(j).wait()
        rows = times(192 * c, 192, 192)
        for i in range(2):
            gff[2 * j + i, rows] = (gff[2 * j + i, rows].astype(F32) + sib_ff[2 * j + i].astype(F32)).astype(BF)

    def cross_src(g, yy):
        if g == 0:
            return gff.at[:, times(192 * c + 160 * yy, 32, 32)]
        return gin.at[:, times(1536 * c + 1280 * yy, 256, 256)]

    cross_dst = (y_ff, y_in)

    def cross_sum(g):
        return send(cross_src(g, 1 - y), cross_dst[g], yx_s.at[g], yx_r.at[g], yp)

    def add_cross(g):
        cross_sum(g).wait()
        here, came = cross_src(g, y), cross_dst[g]
        here[...] = (here[...].astype(F32) + came[...].astype(F32)).astype(BF)

    def rs_piece(ch, d, yy):
        if ch < 3:
            rows = times(192 * c + 32 + 64 * ch, 64, 32) if ch < 2 else times(192 * c + 160 * yy, 32, 32)
            return gff.at[d, rows]
        if ch < 5:
            return gin.at[times(96 * d, 96, 96), times(1536 * c + 256 + 512 * (ch - 3), 512, 256)]
        if ch == 5:
            return gin.at[times(96 * d, 96, 96), times(1536 * c + 1280 * yy, 256, 256)]
        return win.at[d, c, :, pl.ds(768 * (ch - 6), 768)]

    landing = [r_ffa.at[0], r_ffa.at[1], r_ffb, r_ina.at[0], r_ina.at[1], r_inb, r_att.at[0]]
    landing += [r_ffa.at[0, :, pl.ds(0, 48)], r_ffa.at[1, :, pl.ds(0, 48)], r_att.at[1]]

    def rs_send(ch, e):
        ahead = e // FAR
        part = rs_piece(ch, owner((1 - ahead) * (FAR - e) + ahead * (e - EVENTS)), y)
        return send(part, landing[ch].at[e], rr_s.at[ch, e], rr_r.at[ch, e], side(e))

    def rs_begin(ch):
        rs_send(ch, 0).start()
        rs_send(ch, FAR).start()

    def rs_event(ch, e):
        rs_send(ch, e).wait_recv()
        here = rs_piece(ch, owner(FAR - 1 - e if e < FAR else e - EVENTS + 1), y)
        here[...] = (here[...].astype(F32) + landing[ch][e].astype(F32)).astype(BF)
        if e not in (FAR - 1, EVENTS - 1):
            rs_send(ch, e + 1).start()

    def half_in(k):
        src = gin.at[:, times(1536 * (1 - c) + 384 * k, 384, 384)]
        return send(src, sib_in.at[k], hs_s.at[1, k], hs_r.at[1, k], sib)

    def merge_in(k):
        half_in(k).wait()
        cols = times(1536 * c + 384 * k, 384, 384)
        gin[:, cols] = (gin[:, cols].astype(F32) + sib_in[k].astype(F32)).astype(BF)

    def sib_rows(t):
        return sib_ff.at[:, times(48 * t, 48, 48)]

    def half_att(t):
        return send(win.at[:, 1 - c, :, block(t)], sib_rows(t), hs_s.at[2, t], hs_r.at[2, t], sib)

    def merge_att(t):
        half_att(t).wait()
        win[:, c, :, block(t)] = (win[:, c, :, block(t)].astype(F32) + sib_rows(t)[...].astype(F32)).astype(BF)

    final = [f_ff, f_in] + [f_att.at[t] for t in range(4)]

    def own_piece(g):
        if g == 0:
            return gff.at[dp, times(192 * c + 32, 128, 32)]
        if g == 1:
            return gin.at[r96, times(1536 * c + 256, 1024, 256)]
        return rs_piece(4 + g, dp, y)

    def out_piece(g, cc, yy):
        if g == 0:
            return gff_hbm.at[times(192 * cc + 32, 128, 32) if yy is None else times(192 * cc + 160 * yy, 32, 32)]
        if g == 1:
            if yy is None:
                return gin_hbm.at[:, times(1536 * cc + 256, 1024, 256)]
            return gin_hbm.at[:, times(1536 * cc + 1280 * yy, 256, 256)]
        return gatt_hbm.at[g - 2, times(48 * cc, 48, 48)]

    def share_a(g):
        return send(own_piece(g), final[g], fa_s.at[g], fa_r.at[g], yp)

    def share_b(g, k):
        return send(rs_piece(3 * g + 2, dp, y), out_piece(g, c, y), fo_s.at[g, k], fo_r.at[g, k], peers[k])

    def share_sum(g):
        return send(final[g], out_piece(g, c, None), fo_s.at[g, 3], fo_r.at[g, 3], sib)

    def keep_b(g):
        return pltpu.make_async_copy(rs_piece(3 * g + 2, dp, y), out_piece(g, c, y), fl.at[g, 0])

    def keep_sum(g):
        return pltpu.make_async_copy(final[g], out_piece(g, c, None), fl.at[g, 1])

    def finish_b(g):
        for k in range(3):
            share_b(g, k).start()
        keep_b(g).start()

    def finish_sum(g):
        share_a(g).wait()
        final[g][...] = (final[g][...].astype(F32) + own_piece(g)[...].astype(F32)).astype(BF)
        share_sum(g).start()
        keep_sum(g).start()

    def hop(k):
        dev = (yp, sib, xp, z1, z2)[k]
        return send(sums.at[k], sums_in.at[k], bf_s.at[k], bf_r.at[k], dev)

    def hop_done(k):
        hop(k).wait()
        sums[k + 1] = sums[k] + sums_in[k]

    def merge(g, k):
        (merge_ff, merge_in, merge_att)[g](k)

    def go(g):
        if g < 2:
            cross_sum(g).start()
            rs_begin(3 * g)
            rs_begin(3 * g + 1)
        else:
            rs_begin(4 + g)

    def cross_in(g):
        add_cross(g)
        rs_begin(3 * g + 2)

    def hop_on(k):
        hop_done(k)
        if k < 4:
            hop(k + 1).start()

    acts |= {
        RS: rs_event, HALF: merge, GO: go, XC: cross_in, SHARE_A: lambda g: share_a(g).start(), FIN_B: finish_b,
        FSUM: finish_sum, HOP: hop_on,
    }

    loop(4, grad_ff)
    serve(AT_MFF)
    serve(AT_FF)
    settled(2)

    def grad_up(j):
        v = dg(cot[...], wff[block(j), :], 1, 1) * big[j, down_rows, :].astype(F32)
        big[j, down_rows, :] = v.astype(BF)
        serve_at(AT_GUP, 4, j)

    loop(4, grad_up)

    def grad_in(j):
        gin[:, block(j)] = dg(nf[...], big[j, down_rows, :], 0, 0).astype(BF)
        serve_at(AT_GIN, 4, j)

    loop(4, grad_in)

    for k in range(4):
        half_in(k).start()

    acc[...] = jnp.zeros_like(acc)

    def grad_nf(j):
        acc[...] += dg(big[j, down_rows, :], win_block(j), 1, 1)
        serve_at(AT_GNF, 4, j)

    loop(4, grad_nf)

    def norm_back(v, gain, grad):
        s = lax.rsqrt(jnp.mean(v * v, axis=-1, keepdims=True) + EPS)
        scaled = grad * gain
        back = s * scaled - v * (s * s * s) * jnp.mean(v * scaled, axis=-1, keepdims=True)
        return back, jnp.sum(grad * v * s, axis=0, keepdims=True)

    def ffn_norm_back(b, total):
        rows = times(128 * b, 128, 128)
        v = hid[rows, :]
        back, part = norm_back(v, gain_f, acc[rows, :])
        grad = cot[rows, :].astype(F32) + back
        acc[rows, :] = grad
        cot[rows, :] = grad.astype(BF)
        return total + part

    g_ffn_gain = lax.fori_loop(0, 4, ffn_norm_back, jnp.zeros((1, WIDTH), F32))

    serve(AT_FNORM)
    serve(AT_PREWO)
    gather_sent(1)
    win[:, :, :, block(3)] = dg(mixed[...], cot[...], 0, 0).astype(BF).reshape(8, 2, 48, 768)

    half_att(3).start()
    serve(AT_GWO)
    nf[...] = dg(cot[...], watt[3], 1, 1).astype(BF)
    serve(AT_GMIX)


    def give(src, dst_hbm, at, k):
        dev = peers[k]
        return send(src.at[times(128 * dev[1], 128, 128)], dst_hbm.at[sq], a2_s.at[at, k], a2_r.at[at, k], dev)

    def give_wait(src, dst_hbm, at):
        for k in range(3):
            give(src, dst_hbm, at, k).wait_send()
            theirs = dst_hbm.at[peers[k][1]]
            send(theirs, theirs, a2_s.at[at, k], a2_r.at[at, k], peers[k]).wait_recv()

    def pool_send(k):
        return send(pool, pool_hbm.at[sq], a2_s.at[4, k], a2_r.at[4, k], peers[k])

    pool_own = pltpu.make_async_copy(pool, pool_hbm.at[sq], loc.at[2])
    lay = big.at[0, up_rows]
    lay_own = pltpu.make_async_copy(lay.at[mine], out_hbm.at[sq], loc.at[1])
    def narrow(j):
        part = dg(big[j, up_rows, :], wff[block(j), :], 1, 0)
        hid[...] += part
        serve_at(AT_NARROW, 4, j)

    loop(4, narrow)
    lay[...] = hid[...].astype(BF)
    for k in range(3):
        give(lay, out_hbm, 2, k).start()
    lay_own.start()
    here_t = lax.broadcasted_iota(jnp.int32, (TOKENS, 1), 0) < count
    mean = jnp.sum(jnp.where(here_t, hid[...], 0.0), axis=0, keepdims=True) / count.astype(F32)
    pool[...] = jnp.broadcast_to(mean, (8, WIDTH))
    pool_own.start()
    for k in range(3):
        pool_send(k).start()
    serve(AT_LAY)

    flip_sum = lax.broadcasted_iota(jnp.int32, (128, 128), 0) + lax.broadcasted_iota(jnp.int32, (128, 128), 1)
    flip = (flip_sum == 127).astype(F32)

    def attend_back(hp):
        cols = times(128 * hp, 128, 128)
        key, value = qkv[1, :, cols], qkv[2, :, cols]
        query, grad = qkv[0, :, cols], nf[:, cols]
        g_query = [None] * 4
        for h in range(2):
            key_h = only(h, key)
            before = after = jnp.zeros((128, 128), F32)
            near = [jnp.zeros((128, 128), F32) for _ in range(3)]
            for ib in range(4):
                rows = pl.ds(128 * ib, 128)
                wide = probs[2 * hp + h, rows, :].astype(F32)
                d_probs = dg(only(h, nf[rows, cols]), value, 1, 1)
                mean_d = jnp.sum(wide * d_probs, axis=-1, keepdims=True)
                d_score = wide * (d_probs - mean_d)
                for jb in range(4):
                    off, part = jb - ib, d_score[:, 128 * jb : 128 * (jb + 1)]
                    if off < -1:
                        before = before + part
                    elif off > 1:
                        after = after + part
                    else:
                        near[off + 1] = near[off + 1] + part
                d_low = d_score.astype(BF)
                d_both[pl.ds(512 * h + 128 * ib, 128), :] = d_low
                one = dg(d_low, key_h, 1, 0)
                g_query[ib] = one if h == 0 else g_query[ib] + one
            tilted = exact(flip, jnp.concatenate(near, axis=1), 1, 0)
            tilted = jnp.concatenate([tilted, jnp.zeros((128, 128), F32)], axis=1)
            flat = jnp.sum(pltpu.roll(tilted, 385, 1, stride=1, stride_axis=0), axis=0, keepdims=True)
            far = jnp.concatenate(
                [
                    jnp.zeros((1, 256), F32),
                    jnp.sum(after, axis=0, keepdims=True),
                    jnp.sum(before, axis=0, keepdims=True),
                ],
                axis=1,
            )
            diag[pl.ds(2 * hp + h, 1), :] = flat + far
        both_query = jnp.concatenate([only(0, query), only(1, query)], axis=0)
        both_grad = jnp.concatenate([only(0, grad), only(1, grad)], axis=0)
        qkv[1, :, cols] = dg(d_both[...], both_query, 0, 0).astype(BF)
        qkv[2, :, cols] = dg(probs[pl.ds(2 * hp, 2)].reshape(1024, 512), both_grad, 0, 0).astype(BF)
        for ib in range(4):
            qkv[0, pl.ds(128 * ib, 128), cols] = g_query[ib].astype(BF)

        @pl.when(hp % 2 == 1)
        def _():
            t = hp // 2
            three = times(256 * t, 256, 256)
            grads = jnp.concatenate([qkv[0, :, three], qkv[1, :, three], qkv[2, :, three]], axis=1)
            win[:, :, :, block(t)] = dg(normed[...], grads, 0, 0).astype(BF).reshape(8, 2, 48, 768)
            half_att(t).start()

        serve_at(AT_AB, PAIRS, hp)

    loop(PAIRS, attend_back)
    def attn_norm_back(b, total):
        rows = times(256 * b, 256, 256)
        grad = dg(qkv[0, rows, :], watt[0], 1, 1) + dg(qkv[1, rows, :], watt[1], 1, 1) + dg(qkv[2, rows, :], watt[2], 1, 1)
        back, part = norm_back(xs[rows, :].astype(F32), gain_a, grad)
        mixed[rows, :] = (acc[rows, :] + back).astype(BF)
        serve_at(AT_GN, 2, b)
        return total + part

    g_attn_gain = lax.fori_loop(0, 2, attn_norm_back, jnp.zeros((1, WIDTH), F32))

    sums[0] = jnp.zeros((32, 128), F32)
    sums[0, 0:16, 0:32] = exact(diag[...], band_bucket(32), 1, 1)
    for k in range(6):
        sums[0, 16 + k : 17 + k, :] = g_attn_gain[:, 128 * k : 128 * (k + 1)]
        sums[0, 22 + k : 23 + k, :] = g_ffn_gain[:, 128 * k : 128 * (k + 1)]

    hop(0).start()
    for k in range(3):
        give(mixed, gx_hbm, 3, k).start()
    gx_own = pltpu.make_async_copy(mixed.at[mine], gx_hbm.at[sq], loc.at[0])
    gx_own.start()
    serve(AT_GX)
    serve(AT_TAIL)
    small_out[...] = sums[5]

    for g in range(6):
        if g < 2:
            keep_b(g).wait()
            for k, (cc, yy) in enumerate(((1 - c, y), (c, 1 - y), (1 - c, 1 - y))):
                share_b(g, k).wait_send()
                came = out_piece(g, cc, yy)
                send(came, came, fo_s.at[g, k], fo_r.at[g, k], peers[k]).wait_recv()
        keep_sum(g).wait()
        share_sum(g).wait_send()
        came = out_piece(g, 1 - c, None)
        send(came, came, fo_s.at[g, 3], fo_r.at[g, 3], sib).wait_recv()

    def ring_sent(e):
        for ch in range(10):
            rs_send(ch, e).wait_send()

    loop(EVENTS, ring_sent)
    gather_sent(0)
    gather_sent(2)
    gather_sent(3)
    give_wait(lay, out_hbm, 2)
    give_wait(mixed, gx_hbm, 3)
    lay_own.wait()
    gx_own.wait()
    pool_own.wait()
    for k in range(3):
        pool_send(k).wait_send()
        theirs = pool_hbm.at[peers[k][1]]
        send(theirs, theirs, a2_s.at[4, k], a2_r.at[4, k], peers[k]).wait_recv()
        swap(k, x_hbm, xs, 0).wait_send()
        swap(k, cot_hbm, cot, 1).wait_send()


def finish_kernel(
    out_in, gx_in, att_in, in_in, ff_in, pool_in, small_in,
    out, gx, pool_out, gain_a, gq, gk, gv, go, g_table, gain_f, gin_out, gff_out,
    v_out, v_gx, v_att, v_in, v_ff, v_pool, w_att, w_in, w_ff, w_pool, sem_in, sem_out,
):
    sources = (in_in, ff_in, att_in, pool_in, out_in, gx_in)
    held = (v_in, v_ff, v_att, v_pool, v_out, v_gx)
    reads = [pltpu.make_async_copy(a, b, sem_in.at[k]) for k, (a, b) in enumerate(zip(sources, held))]
    for read in reads:
        read.start()
    g_table[...] = small_in[0:HEAD_N, 0:32]
    for k in range(6):
        gain_a[128 * k : 128 * (k + 1)] = small_in[16 + k : 17 + k, :].reshape(128)
        gain_f[128 * k : 128 * (k + 1)] = small_in[22 + k : 23 + k, :].reshape(128)
    writes = []

    def write(src, dst):
        writes.append(pltpu.make_async_copy(src, dst, sem_out.at[len(writes)]))
        writes[-1].start()

    reads[0].wait()
    w_in[...] = v_in[...].astype(F32)
    write(w_in, gin_out)
    reads[1].wait()
    w_ff[...] = v_ff[...].astype(F32)
    write(w_ff, gff_out)
    reads[2].wait()
    w_att[3] = v_att[3].astype(F32)
    for t in range(3):
        for i in range(3):
            w_att[i, :, 256 * t : 256 * (t + 1)] = v_att[t, :, 256 * i : 256 * (i + 1)].astype(F32)
    for i, ref in enumerate((gq, gk, gv, go)):
        write(w_att.at[i], ref)
    reads[3].wait()
    for p in range(SEQ):
        w_pool[p : p + 1, :] = v_pool[p, 0:1, :]
    write(w_pool, pool_out)
    reads[4].wait()
    write(v_out, out)
    reads[5].wait()
    write(v_gx, gx)
    for copy in writes:
        copy.wait()


def passage_shards(
    passages, lengths, attn_gain, w_query, w_key, w_value, w_attn_out, bias_table, ffn_gain, w_in, w_ff_out, cotangent
):
    any_space = pl.BlockSpec(memory_space=pl.ANY)
    vmem = pl.BlockSpec(memory_space=pltpu.VMEM)
    dma = pltpu.SemaphoreType.DMA
    scratch = [
        pltpu.VMEM(shape, BF)
        for shape in (
            (4, 768, 768), (8, 2, 48, 3072), (3072, 768), (768, 3072), (8, 384, 768), (4, 1024, 768), (12, 512, 512),
            (512, 768), (512, 768), (512, 768), (3, 512, 768), (512, 768), (512, 768),
        )
    ]
    scratch += [pltpu.VMEM(shape, F32) for shape in ((512, 768), (512, 768), (16, 512), (16, 512))]
    scratch += [
        pltpu.VMEM(shape, BF)
        for shape in (
            (1024, 512), (8, 192, 768), (4, 768, 384), (8, 32, 768), (768, 256),
            (2, 7, 64, 768), (7, 32, 768), (2, 7, 96, 512), (7, 96, 256), (2, 7, 48, 768),
            (128, 768), (96, 1024), (4, 48, 768),
        )
    ]
    scratch += [pltpu.VMEM((6, 32, 128), F32), pltpu.VMEM((5, 32, 128), F32), pltpu.VMEM((8, 768), F32)]
    scratch += [
        dma(shape)
        for shape in (
            (8, 7), (8, 7), (8, 7), (8, 7), (3, 7), (3, 7), (3, 7), (3, 7), (10, 7), (10, 7), (9,), (5, 3), (5, 3),
            (3, 4), (3, 4), (2,), (2,), (6,), (6,), (6, 4), (6, 4), (6, 2), (5,), (5,),
        )
    ]
    sums = pl.pallas_call(
        layer_kernel,
        out_shape=(
            jax.ShapeDtypeStruct((4, 128, 768), BF),
            jax.ShapeDtypeStruct((4, 128, 768), BF),
            jax.ShapeDtypeStruct((4, 96, 768), BF),
            jax.ShapeDtypeStruct((96, 3072), BF),
            jax.ShapeDtypeStruct((384, 768), BF),
            jax.ShapeDtypeStruct((4, 8, 768), F32),
            jax.ShapeDtypeStruct((32, 128), F32),
        ),
        in_specs=[any_space] * 8 + [pl.BlockSpec(memory_space=pltpu.SMEM)] + [vmem] * 3,
        out_specs=(any_space,) * 6 + (vmem,),
        scratch_shapes=scratch,
        compiler_params=pltpu.CompilerParams(collective_id=0, has_side_effects=True, vmem_limit_bytes=64 * 2**20),
        name="layer",
    )(
        passages, cotangent, w_query, w_key, w_value, w_attn_out, w_in, w_ff_out, lengths,
        attn_gain, ffn_gain, bias_table.T,
    )
    square = jax.ShapeDtypeStruct((96, 768), F32)
    gain = jax.ShapeDtypeStruct((WIDTH,), F32)
    outs = pl.pallas_call(
        finish_kernel,
        out_shape=(
            jax.ShapeDtypeStruct((4, 128, 768), BF),
            jax.ShapeDtypeStruct((4, 128, 768), BF),
            jax.ShapeDtypeStruct((4, 768), F32),
            gain,
            square,
            square,
            square,
            square,
            jax.ShapeDtypeStruct((HEAD_N, 32), F32),
            gain,
            jax.ShapeDtypeStruct((96, 3072), F32),
            jax.ShapeDtypeStruct((384, 768), F32),
        ),
        in_specs=[any_space] * 6 + [vmem],
        out_specs=(any_space,) * 3 + (vmem,) + (any_space,) * 4 + (vmem,) * 2 + (any_space,) * 2,
        scratch_shapes=[
            pltpu.VMEM((4, 128, 768), BF),
            pltpu.VMEM((4, 128, 768), BF),
            pltpu.VMEM((4, 96, 768), BF),
            pltpu.VMEM((96, 3072), BF),
            pltpu.VMEM((384, 768), BF),
            pltpu.VMEM((4, 8, 768), F32),
            pltpu.VMEM((4, 96, 768), F32),
            pltpu.VMEM((96, 3072), F32),
            pltpu.VMEM((384, 768), F32),
            pltpu.VMEM((4, 768), F32),
            dma((6,)),
            dma((9,)),
        ],
        compiler_params=pltpu.CompilerParams(vmem_limit_bytes=64 * 2**20),
        name="finish",
    )(*sums)
    return (outs[0], outs[2], outs[1], *outs[3:8], outs[8].T, *outs[9:])


def solution(mesh):
    ring = (mesh.shape["dp"], mesh.shape["seq"]) == (DP, SEQ)
    return jax.shard_map(
        passage_shards if ring else shards,
        mesh=mesh,
        in_specs=(
            P("dp", "seq", None),
            P("dp"),
            P(),
            P("dp", None),
            P("dp", None),
            P("dp", None),
            P("dp", None),
            P(),
            P(),
            P("dp", None),
            P("dp", None),
            P("dp", "seq", None),
        ),
        out_specs=(
            P("dp", "seq", None),
            P("dp", None),
            P("dp", "seq", None),
            P(),
            P("dp", None),
            P("dp", None),
            P("dp", None),
            P("dp", None),
            P(),
            P(),
            P("dp", None),
            P("dp", None),
        ),
        check_vma=False,
    )
```

```python
import math

import jax
import jax.numpy as jnp
from jax import lax
from jax.experimental import pallas as pl
from jax.experimental.pallas import tpu as pltpu
from jax.sharding import PartitionSpec as P

MAXDIST = 128


EPS = 1e-06
HIGH = lax.Precision.HIGHEST
FLOOR = -1e30


def bucket_index(relative, buckets, reach):
    half_count = buckets // 2
    exact_count = half_count // 2
    distance = jnp.abs(relative)
    result = jnp.minimum(distance, exact_count)
    for power in range(1, half_count - exact_count):
        bound_at = math.ceil(
            exact_count * (reach / exact_count) ** (power / (half_count - exact_count)) - 1e-06
        )
        result = result + (distance >= bound_at).astype(jnp.int32)
    return result + (relative > 0).astype(jnp.int32) * half_count


def rms_norm(values, gain_vec):
    return values * lax.rsqrt(jnp.mean(values * values, axis=-1, keepdims=True) + EPS) * gain_vec


def attend_forward(query_four, key_four, value_four, bias_rows, key_valid):
    scores = (
        jnp.einsum("pqhe,pkhe->phqk", query_four, key_four, preferred_element_type=jnp.float32)
        + bias_rows[None]
    )
    scores = jnp.where(key_valid[:, None, None, :], scores, FLOOR)
    row_top = jnp.max(scores, axis=-1, keepdims=True)
    expo = jnp.exp(scores - row_top)
    row_total = jnp.sum(expo, axis=-1, keepdims=True)
    log_total = row_top + jnp.log(row_total)
    attn_probs = (expo / row_total).astype(jnp.bfloat16)
    mixed_rows = jnp.einsum(
        "phqk,pkhe->pqhe", attn_probs, value_four, preferred_element_type=jnp.float32
    )
    return (mixed_rows.astype(jnp.bfloat16), log_total)


def attend_backward(query_four, key_four, value_four, grad_mixed, log_total, key_valid, bias_rows):

    def one_passage(score_sum, pieces):
        query_p, key_p, value_p, grad_p, log_p, valid_p = pieces
        score_p = (
            jnp.einsum("qhe,khe->hqk", query_p, key_p, preferred_element_type=jnp.float32)
            + bias_rows
        )
        score_p = jnp.where(valid_p[None, None, :], score_p, FLOOR)
        prob_p = jnp.exp(score_p - log_p)
        grad_prob = jnp.einsum("qhe,khe->hqk", grad_p, value_p, preferred_element_type=jnp.float32)
        grad_score = (
            prob_p * (grad_prob - jnp.sum(prob_p * grad_prob, axis=-1, keepdims=True))
        ).astype(jnp.bfloat16)
        grad_query_p = jnp.einsum(
            "hqk,khe->qhe", grad_score, key_p, preferred_element_type=jnp.float32
        ).astype(jnp.bfloat16)
        grad_key_p = jnp.einsum(
            "hqk,qhe->khe", grad_score, query_p, preferred_element_type=jnp.float32
        )
        grad_value_p = jnp.einsum(
            "hqk,qhe->khe", prob_p.astype(jnp.bfloat16), grad_p, preferred_element_type=jnp.float32
        )
        return (
            score_sum + grad_score.astype(jnp.float32),
            (grad_query_p, grad_key_p, grad_value_p),
        )

    start_sum = jnp.zeros(bias_rows.shape, jnp.float32)
    return lax.scan(
        one_passage, start_sum, (query_four, key_four, value_four, grad_mixed, log_total, key_valid)
    )


def shards(
    passages,
    lengths,
    attn_gain,
    w_query,
    w_key,
    w_value,
    w_attn_out,
    bias_table,
    ffn_gain,
    w_in,
    w_ff_out,
    cotangent,
):
    n_pass, local_rows, width = passages.shape
    n_buckets, n_heads = bias_table.shape
    head_dim = width // n_heads
    seq_count = lax.axis_size("seq")
    full_len = local_rows * seq_count
    row_count = n_pass * local_rows
    first_row = lax.axis_index("seq") * local_rows
    gathered = (
        lax.all_gather(w_query, "dp", axis=0, tiled=True),
        lax.all_gather(w_key, "dp", axis=0, tiled=True),
        lax.all_gather(w_value, "dp", axis=0, tiled=True),
        lax.all_gather(w_attn_out, "dp", axis=0, tiled=True),
        lax.all_gather(w_in, "dp", axis=0, tiled=True),
        lax.all_gather(w_ff_out, "dp", axis=0, tiled=True),
    )
    wq_full, wk_full, wv_full, wo_full, win_full, wff_full = gathered
    key_pos = jnp.arange(full_len, dtype=jnp.int32)
    query_pos = first_row + jnp.arange(local_rows, dtype=jnp.int32)
    key_valid = key_pos[None, :] < lengths[:, None]
    query_valid = query_pos[None, :] < lengths[:, None]
    inputs = passages.astype(jnp.float32).reshape(row_count, width)
    normed = rms_norm(inputs, attn_gain).astype(jnp.bfloat16)
    query_rows = jnp.dot(normed, wq_full, preferred_element_type=jnp.float32).astype(jnp.bfloat16)
    key_rows = jnp.dot(normed, wk_full, preferred_element_type=jnp.float32).astype(jnp.bfloat16)
    value_rows = jnp.dot(normed, wv_full, preferred_element_type=jnp.float32).astype(jnp.bfloat16)
    query_local = query_rows.reshape(n_pass, local_rows, n_heads, head_dim)
    relative = key_pos[None, :] - query_pos[:, None]
    one_hot = (
        bucket_index(relative, n_buckets, MAXDIST)[:, :, None]
        == jnp.arange(n_buckets, dtype=jnp.int32)
    ).astype(jnp.float32)
    bias_rows = jnp.einsum("qkb,bh->hqk", one_hot, bias_table, precision=HIGH)
    key_all, value_all = (
        lax.all_gather(key_rows.reshape(n_pass, local_rows, width), "seq", axis=1, tiled=True),
        lax.all_gather(value_rows.reshape(n_pass, local_rows, width), "seq", axis=1, tiled=True),
    )
    key_four = key_all.reshape(n_pass, full_len, n_heads, head_dim)
    value_four = value_all.reshape(n_pass, full_len, n_heads, head_dim)
    mixed_four, log_total = attend_forward(query_local, key_four, value_four, bias_rows, key_valid)
    mixed_rows = mixed_four.reshape(row_count, width)
    hidden = inputs + jnp.dot(mixed_rows, wo_full, preferred_element_type=jnp.float32)
    normed_ffn = rms_norm(hidden, ffn_gain).astype(jnp.bfloat16)
    up_rows = jnp.dot(normed_ffn, win_full, preferred_element_type=jnp.float32)
    activated = jax.nn.gelu(up_rows).astype(jnp.bfloat16)
    output_rows = hidden + jnp.dot(activated, wff_full, preferred_element_type=jnp.float32)
    pool_part = jnp.sum(
        output_rows.reshape(n_pass, local_rows, width)
        * query_valid[:, :, None].astype(jnp.float32),
        axis=1,
    )
    pooled = lax.psum(pool_part, "seq") / lengths[:, None].astype(jnp.float32)
    gathered = (
        lax.all_gather(w_query, "dp", axis=0, tiled=True),
        lax.all_gather(w_key, "dp", axis=0, tiled=True),
        lax.all_gather(w_value, "dp", axis=0, tiled=True),
        lax.all_gather(w_attn_out, "dp", axis=0, tiled=True),
        lax.all_gather(w_in, "dp", axis=0, tiled=True),
        lax.all_gather(w_ff_out, "dp", axis=0, tiled=True),
    )
    wq_full, wk_full, wv_full, wo_full, win_full, wff_full = gathered
    grad_out = cotangent.astype(jnp.float32).reshape(row_count, width)
    grad_branch = grad_out.astype(jnp.bfloat16)
    g_ff_out = jnp.einsum("rf,rd->fd", activated, grad_branch, preferred_element_type=jnp.float32)
    grad_act = jnp.einsum("rd,fd->rf", grad_branch, wff_full, preferred_element_type=jnp.float32)
    _, gelu_pull = jax.vjp(jax.nn.gelu, up_rows)
    grad_up = gelu_pull(grad_act)[0].astype(jnp.bfloat16)
    g_in = jnp.einsum("rd,rf->df", normed_ffn, grad_up, preferred_element_type=jnp.float32)
    grad_normed_ffn = jnp.einsum("rf,df->rd", grad_up, win_full, preferred_element_type=jnp.float32)
    _, ffn_pull = jax.vjp(rms_norm, hidden, ffn_gain)
    grad_hidden_norm, g_ffn_gain = ffn_pull(grad_normed_ffn)
    grad_hidden = grad_out + grad_hidden_norm
    grad_attn = grad_hidden.astype(jnp.bfloat16)
    g_attn_out = jnp.einsum("rd,re->de", mixed_rows, grad_attn, preferred_element_type=jnp.float32)
    grad_mixed = jnp.einsum("re,de->rd", grad_attn, wo_full, preferred_element_type=jnp.float32)
    grad_mixed = grad_mixed.astype(jnp.bfloat16).reshape(n_pass, local_rows, n_heads, head_dim)
    score_sum, (grad_query, grad_key, grad_value) = attend_backward(
        query_local, key_four, value_four, grad_mixed, log_total, key_valid, bias_rows
    )
    grad_key, grad_value = (
        lax.psum_scatter(
            grad_key.reshape(n_pass, full_len, width).astype(jnp.bfloat16),
            "seq",
            scatter_dimension=1,
            tiled=True,
        ).astype(jnp.float32),
        lax.psum_scatter(
            grad_value.reshape(n_pass, full_len, width).astype(jnp.bfloat16),
            "seq",
            scatter_dimension=1,
            tiled=True,
        ).astype(jnp.float32),
    )
    grad_query = grad_query.reshape(row_count, width)
    grad_key = grad_key.astype(jnp.bfloat16).reshape(row_count, width)
    grad_value = grad_value.astype(jnp.bfloat16).reshape(row_count, width)
    g_table = jnp.einsum("qkb,hqk->bh", one_hot, score_sum, precision=HIGH)
    g_query = jnp.einsum("rd,re->de", normed, grad_query, preferred_element_type=jnp.float32)
    g_key = jnp.einsum("rd,re->de", normed, grad_key, preferred_element_type=jnp.float32)
    g_value = jnp.einsum("rd,re->de", normed, grad_value, preferred_element_type=jnp.float32)
    grad_normed = jnp.einsum("re,de->rd", grad_query, wq_full, preferred_element_type=jnp.float32)
    grad_normed = grad_normed + jnp.einsum(
        "re,de->rd", grad_key, wk_full, preferred_element_type=jnp.float32
    )
    grad_normed = grad_normed + jnp.einsum(
        "re,de->rd", grad_value, wv_full, preferred_element_type=jnp.float32
    )
    _, attn_pull = jax.vjp(rms_norm, inputs, attn_gain)
    grad_inputs_norm, g_attn_gain = attn_pull(grad_normed)
    grad_input = (
        (grad_hidden + grad_inputs_norm).astype(jnp.bfloat16).reshape(n_pass, local_rows, width)
    )
    row_grads = (
        lax.psum_scatter(g_query, "dp", scatter_dimension=0, tiled=True),
        lax.psum_scatter(g_key, "dp", scatter_dimension=0, tiled=True),
        lax.psum_scatter(g_value, "dp", scatter_dimension=0, tiled=True),
        lax.psum_scatter(g_attn_out, "dp", scatter_dimension=0, tiled=True),
        lax.psum_scatter(g_in, "dp", scatter_dimension=0, tiled=True),
        lax.psum_scatter(g_ff_out, "dp", scatter_dimension=0, tiled=True),
    )
    row_grads = (
        lax.psum(row_grads[0].astype(jnp.bfloat16), "seq").astype(jnp.float32),
        lax.psum(row_grads[1].astype(jnp.bfloat16), "seq").astype(jnp.float32),
        lax.psum(row_grads[2].astype(jnp.bfloat16), "seq").astype(jnp.float32),
        lax.psum(row_grads[3].astype(jnp.bfloat16), "seq").astype(jnp.float32),
        lax.psum(row_grads[4].astype(jnp.bfloat16), "seq").astype(jnp.float32),
        lax.psum(row_grads[5].astype(jnp.bfloat16), "seq").astype(jnp.float32),
    )
    small_sums = lax.psum((g_attn_gain, g_ffn_gain, g_table), ("dp", "seq"))
    layer_out = output_rows.astype(jnp.bfloat16).reshape(n_pass, local_rows, width)
    return (
        layer_out,
        pooled,
        grad_input,
        small_sums[0],
        row_grads[0],
        row_grads[1],
        row_grads[2],
        row_grads[3],
        small_sums[2],
        small_sums[1],
        row_grads[4],
        row_grads[5],
    )


DP, SEQ = 8, 4
FAR, EVENTS = 4, 7
BF, F32 = jnp.bfloat16, jnp.float32
MESH_ID = pl.DeviceIdType.MESH
TOKENS, WIDTH, HIDDEN, HEAD_N = 512, 768, 3072, 12
PAIRS = HEAD_N // 2
GELU_A, GELU_B = math.sqrt(2 / math.pi), 0.044715


AG, CR, BEGIN, RS, HALF, GO, XC, SHARE_A, FIN_B, FSUM, HOP, LEAVE = range(12)
(
    AT_A1, AT_NORM, AT_ATT, AT_WO, AT_IN, AT_COTW, AT_MFF, AT_FF, AT_FNORM, AT_PREWO, AT_GWO, AT_GMIX, AT_LAY,
    AT_GX, AT_TAIL, AT_PROJECT, AT_ATTEND, AT_RESIDUAL, AT_WIDEN, AT_GFF, AT_GUP, AT_GIN, AT_GNF, AT_NARROW, AT_AB,
    AT_GN,
) = range(26)
PLAN = {
    AT_A1: (
        (AG, 2, 0), (AG, 2, 4), (AG, 1, 0), (AG, 1, 4), (AG, 0, 0), (AG, 0, 4), (AG, 2, 1), (AG, 2, 5), (AG, 1, 1),
        (AG, 1, 5), (AG, 0, 1), (AG, 0, 5), (AG, 2, 2),
    ),
    AT_NORM: (
        (AG, 2, 6),
    ),
    AT_ATT: (
        (CR, 2, 0), (AG, 1, 2), (CR, 2, 4), (AG, 1, 6), (CR, 2, 1), (AG, 0, 2), (BEGIN, 3), (BEGIN, 1), (CR, 2, 5),
        (AG, 0, 6), (AG, 2, 3), (CR, 2, 2), (AG, 1, 3), (CR, 2, 6), (AG, 0, 3), (AG, 7, 0), (CR, 2, 3), (AG, 7, 4),
        (AG, 4, 0),
    ),
    (AT_PROJECT, 0): (
        (AG, 4, 4),
    ),
    (AT_PROJECT, 2): (
        (AG, 3, 0),
    ),
    (AT_ATTEND, 0): (
        (CR, 4, 0), (AG, 3, 4), (AG, 7, 1),
    ),
    (AT_ATTEND, 1): (
        (AG, 7, 5), (AG, 4, 1),
    ),
    (AT_ATTEND, 2): (
        (AG, 4, 5), (AG, 3, 1),
    ),
    (AT_ATTEND, 3): (
        (AG, 3, 5), (AG, 7, 2),
    ),
    (AT_ATTEND, 4): (
        (AG, 7, 6), (AG, 4, 2),
    ),
    (AT_ATTEND, 5): (
        (AG, 4, 6), (CR, 4, 4), (AG, 3, 2), (CR, 4, 1), (BEGIN, 2),
    ),
    AT_WO: (
        (AG, 3, 6), (CR, 4, 5), (AG, 7, 3), (AG, 4, 3), (CR, 4, 2),
    ),
    (AT_RESIDUAL, 1): (
        (AG, 3, 3), (CR, 4, 6),
    ),
    AT_IN: (
        (AG, 6, 0), (AG, 6, 4), (CR, 4, 3), (AG, 5, 0),
    ),
    (AT_WIDEN, 0): (
        (AG, 5, 4), (AG, 6, 1), (CR, 6, 0),
    ),
    (AT_WIDEN, 1): (
        (AG, 6, 5),
    ),
    (AT_WIDEN, 2): (
        (AG, 5, 1), (CR, 6, 4),
    ),
    (AT_WIDEN, 3): (
        (AG, 5, 5), (AG, 6, 2), (CR, 6, 1),
    ),
    (AT_GFF, 1): (
        (AG, 6, 6),
    ),
    (AT_GFF, 2): (
        (AG, 5, 2), (CR, 6, 5),
    ),
    (AT_GFF, 3): (
        (AG, 5, 6), (HALF, 0, 0), (LEAVE, 0),
    ),
    AT_MFF: (
        (AG, 6, 3), (CR, 6, 2), (HALF, 0, 1), (HALF, 0, 2), (LEAVE, 4), (AG, 5, 3), (CR, 6, 6), (HALF, 0, 3), (GO, 0),
        (RS, 0, 0),
    ),
    AT_FF: (
        (RS, 1, 0), (CR, 6, 3), (RS, 0, 4),
    ),
    (AT_GUP, 0): (
        (RS, 1, 4),
    ),
    (AT_GUP, 1): (
        (RS, 0, 1),
    ),
    (AT_GUP, 2): (
        (RS, 1, 1),
    ),
    (AT_GUP, 3): (
        (RS, 0, 5),
    ),
    (AT_GIN, 1): (
        (RS, 1, 5),
    ),
    (AT_GIN, 2): (
        (RS, 0, 2),
    ),
    (AT_GIN, 3): (
        (RS, 1, 2),
    ),
    (AT_GNF, 0): (
        (RS, 0, 6), (HALF, 1, 0), (XC, 0),
    ),
    (AT_GNF, 1): (
        (RS, 1, 6), (HALF, 1, 1),
    ),
    (AT_GNF, 2): (
        (RS, 0, 3), (HALF, 1, 2), (RS, 1, 3), (SHARE_A, 0),
    ),
    (AT_GNF, 3): (
        (HALF, 1, 3), (GO, 1), (RS, 2, 0), (RS, 2, 4),
    ),
    (AT_NARROW, 0): (
        (RS, 3, 0),
    ),
    (AT_NARROW, 1): (
        (RS, 3, 4), (HALF, 2, 3), (GO, 5),
    ),
    (AT_NARROW, 2): (
        (FSUM, 0), (RS, 4, 0),
    ),
    (AT_NARROW, 3): (
        (RS, 4, 4), (RS, 2, 1),
    ),
    (AT_AB, 0): (
        (RS, 2, 5), (RS, 3, 1), (RS, 3, 5), (RS, 9, 0),
    ),
    (AT_AB, 1): (
        (RS, 9, 4), (RS, 4, 1), (RS, 4, 5), (XC, 1), (RS, 2, 2), (RS, 2, 6),
    ),
    (AT_AB, 2): (
        (RS, 3, 2), (RS, 3, 6), (RS, 9, 1), (HALF, 2, 0), (GO, 2), (RS, 9, 5),
    ),
    (AT_AB, 3): (
        (RS, 4, 2), (RS, 4, 6), (RS, 5, 0), (RS, 5, 4), (RS, 2, 3), (FIN_B, 0), (RS, 3, 3),
    ),
    (AT_AB, 4): (
        (RS, 9, 2), (RS, 6, 0), (RS, 6, 4), (HALF, 2, 1), (GO, 3), (RS, 9, 6),
    ),
    (AT_AB, 5): (
        (RS, 4, 3), (SHARE_A, 1), (RS, 5, 1), (RS, 5, 5), (RS, 9, 3), (SHARE_A, 5), (RS, 6, 1),
    ),
    (AT_GN, 0): (
        (RS, 6, 5), (RS, 7, 0),
    ),
    (AT_GN, 1): (
        (RS, 7, 4), (HALF, 2, 2), (GO, 4), (RS, 5, 2),
    ),
    AT_GX: (
        (RS, 5, 6),
    ),
    AT_TAIL: (
        (RS, 6, 2), (RS, 6, 6), (RS, 7, 1), (FSUM, 1), (RS, 7, 5), (RS, 8, 0), (FSUM, 5), (RS, 8, 4), (RS, 5, 3),
        (FIN_B, 1), (RS, 6, 3), (SHARE_A, 2), (RS, 7, 2), (HOP, 0), (RS, 7, 6), (RS, 8, 1), (RS, 8, 5), (RS, 7, 3),
        (SHARE_A, 3), (HOP, 1), (RS, 8, 2), (RS, 8, 6), (RS, 8, 3), (SHARE_A, 4), (FSUM, 2), (HOP, 2), (FSUM, 3),
        (FSUM, 4),
    ),
}

def dg(left, right, on_left, on_right):
    return lax.dot_general(
        left, right, (((on_left,), (on_right,)), ((), ())), preferred_element_type=F32
    )


def exact(left, right, on_left, on_right):
    return lax.dot_general(
        left, right, (((on_left,), (on_right,)), ((), ())), precision=HIGH, preferred_element_type=F32
    )


def ring_dp(place):
    high = place // 4
    return 2 * (place * (1 - high) + (7 - place) * high) + high


def times(start, size, step):
    return pl.ds(pl.multiple_of(start, step), size)


def band_bucket(n_buckets):
    lane = lax.broadcasted_iota(jnp.int32, (n_buckets, 512), 1)
    relative = jnp.where(lane < 384, lane - 128, lane - 640)
    row = lax.broadcasted_iota(jnp.int32, (n_buckets, 512), 0)
    return (bucket_index(relative, n_buckets, MAXDIST) == row).astype(F32)


def layer_kernel(
    x_hbm, cot_hbm, wq_hbm, wk_hbm, wv_hbm, wo_hbm, win_hbm, wff_hbm, lengths, attn_gain, ffn_gain, table,
    out_hbm, gx_hbm, gatt_hbm, gin_hbm, gff_hbm, pool_hbm, small_out,
    watt, win, wff, gin, gff, big, probs, xs, cot, normed, qkv, mixed, nf, hid, acc, band, diag, d_both,
    sib_ff, sib_in, y_ff, y_in, r_ffa, r_ffb, r_ina, r_inb, r_att, f_ff, f_in, f_att, sums, sums_in, spread, pool,
    ag_s, ag_r, sb_s, sb_r, yf_s, yf_r, yb_s, yb_r, rr_s, loc, a2_s, a2_r, hs_s, hs_r, yx_s, yx_r,
    fa_s, fa_r, fb_s, fb_r, fo_s, fo_r, fl, bf_s, bf_r,
):
    dp, sq = lax.axis_index("dp"), lax.axis_index("seq")
    z, x, y, c = dp // 2, dp % 2, sq // 2, sq % 2
    place = x * (7 - z) + (1 - x) * z
    turn = 1 - 2 * c

    def owner(steps):
        return ring_dp((place + steps * turn + 16) % 8)

    sib, yp, ysib = (dp, 2 * y + 1 - c), (dp, 2 * (1 - y) + c), (dp, 2 * (1 - y) + 1 - c)
    peers = (sib, yp, ysib)
    others = [((dp + k) % DP, sq) for k in range(1, DP)]

    def send(src, dst, ss, rs, dev):
        return pltpu.make_async_remote_copy(
            src_ref=src, dst_ref=dst, send_sem=ss, recv_sem=rs, device_id=dev, device_id_type=MESH_ID
        )

    def when(condition, body):
        if isinstance(condition, bool):
            if condition:
                body()
        else:
            pl.when(condition)(body)

    def loop(count, body):
        def step(i, _):
            body(i)
            return 0

        lax.fori_loop(0, count, step, 0)

    barrier = pltpu.get_barrier_semaphore()
    for dev in (*peers, *others):
        pl.semaphore_signal(barrier, inc=1, device_id=dev, device_id_type=MESH_ID)

    r96 = times(96 * dp, 96, 96)
    own = [pltpu.make_async_copy(w, watt.at[i, r96], loc.at[i]) for i, w in enumerate((wq_hbm, wk_hbm, wv_hbm, wo_hbm))]
    for i in range(2):
        own.append(pltpu.make_async_copy(win_hbm.at[pl.ds(48 * i, 48)], win.at[dp, i], loc.at[4 + i]))
    own.append(pltpu.make_async_copy(wff_hbm, wff.at[times(384 * dp, 384, 384)], loc.at[6]))
    mine = times(128 * sq, 128, 128)
    own.append(pltpu.make_async_copy(x_hbm.at[sq], xs.at[mine], loc.at[7]))
    own.append(pltpu.make_async_copy(cot_hbm.at[sq], cot.at[mine], loc.at[8]))
    for copy in own:
        copy.start()
    pl.semaphore_wait(barrier, len(peers) + len(others))

    def swap(k, src_hbm, dst, at):
        dev = peers[k]
        return send(src_hbm.at[dev[1]], dst.at[mine], a2_s.at[at], a2_r.at[at], dev)

    def three(ref, at):
        return send(ref, ref, a2_s.at[at], a2_r.at[at], sib)

    def swap_wait(dst, at):
        three(dst.at[pl.ds(0, 384)], at).wait_recv()

    for k in range(3):
        swap(k, x_hbm, xs, 0).start()

    def piece(ch, d, cc, yy):
        if ch < 3:
            cols = pl.ds(128 + 256 * ch, 256) if ch < 2 else times(640 * yy, 128, 128)
            return watt.at[0:3, times(96 * d + 48 * cc, 48, 48), cols]
        if ch < 5:
            cols = pl.ds(768, 1536) if ch == 3 else times(2304 * yy, 768, 768)
            return win.at[d, cc, :, cols]
        if ch == 7:
            return watt.at[3, times(96 * d + 48 * cc, 48, 48)]
        cols = pl.ds(256, 256) if ch == 5 else times(512 * yy, 256, 256)
        return wff.at[times(384 * d + 192 * cc, 192, 192), cols]

    crossing = (2, 4, 6)
    groups = ((0, 1, 2), (3, 4), (5, 6), (7,))

    def came_from(e):
        ahead = e // FAR
        return (1 - ahead) * (-e - 1) + ahead * (e - 3)

    def side(e):
        return (owner(1 - 2 * (e // FAR)), sq)

    def ring_send(ch, e):
        ahead = e // FAR
        part = piece(ch, owner((1 - ahead) * -e + ahead * (e - FAR)), c, y)
        return send(part, part, ag_s.at[ch], ag_r.at[ch, e], side(e))

    def hand_on(ch, e):
        part = piece(ch, owner(came_from(e)), c, y)
        return send(part, part, sb_s.at[ch], sb_r.at[ch], sib)

    def cross(ch, e):
        part = piece(ch, owner(came_from(e)), c, y)
        return send(part, part, yf_s.at[ch // 2 - 1], yf_r.at[ch // 2 - 1, e], yp)

    def cross_on(ch, e):
        part = piece(ch, owner(came_from(e)), c, 1 - y)
        return send(part, part, yb_s.at[ch // 2 - 1], yb_r.at[ch // 2 - 1], sib)

    def arrive(ch, e):
        part = piece(ch, owner(came_from(e)), c, y)
        send(part, part, ag_s.at[ch], ag_r.at[ch, e], side(e)).wait_recv()
        if e not in (FAR - 1, EVENTS - 1):
            ring_send(ch, e + 1).start()
        if ch in crossing:
            cross(ch, e).start()
        hand_on(ch, e).start()

    def arrive_cross(ch, e):
        part = piece(ch, owner(came_from(e)), c, 1 - y)
        send(part, part, yf_s.at[ch // 2 - 1], yf_r.at[ch // 2 - 1, e], yp).wait_recv()
        cross_on(ch, e).start()

    def seven(ch):
        if ch < 3:
            return watt.at[0:3, pl.ds(0, 336), pl.ds(0, 256 if ch < 2 else 128)]
        if ch < 5:
            return win.at[pl.ds(0, 7), 0, :, pl.ds(0, 1536 if ch == 3 else 768)]
        return watt.at[3, pl.ds(0, 336)] if ch == 7 else wff.at[pl.ds(0, 1344), pl.ds(0, 256)]

    def all_seven(ch, ss, rs, dev):
        return send(seven(ch), seven(ch), ss, rs, dev)

    def settled(group):
        for ch in groups[group]:
            all_seven(ch, sb_s.at[ch], sb_r.at[ch], sib).wait_recv()
            if ch in crossing:
                all_seven(ch, yb_s.at[group], yb_r.at[group], sib).wait_recv()

    def gather_sent(group):
        for ch in groups[group]:
            all_seven(ch, ag_s.at[ch], ag_r.at[ch, 0], sib).wait_send()
            all_seven(ch, sb_s.at[ch], sb_r.at[ch], sib).wait_send()
            if ch in crossing:
                all_seven(ch, yf_s.at[group], yf_r.at[group, 0], yp).wait_send()
                all_seven(ch, yb_s.at[group], yb_r.at[group], sib).wait_send()

    def begin(group):
        for ch in reversed(groups[group]):
            ring_send(ch, 0).start()
            ring_send(ch, FAR).start()

    acts = {AG: arrive, CR: arrive_cross, BEGIN: begin}

    def serve(slot):
        for name, *place in PLAN.get(slot, ()):
            acts[name](*place)

    def serve_at(slot, count, i):
        for k in range(count):
            if (slot, k) in PLAN:

                @pl.when(i == k)
                def _(k=k):
                    serve((slot, k))

    for i in range(4):
        own[i].wait()
    begin(0)

    band[pl.ds(0, HEAD_N), :] = exact(table[...], band_bucket(32), 1, 0)
    gain_a = attn_gain[...].reshape(1, WIDTH)
    gain_f = ffn_gain[...].reshape(1, WIDTH)

    serve(AT_A1)
    own[7].wait()
    swap_wait(xs, 0)
    for i in range(4, 7):
        own[i].wait()

    def norm_rows(b):
        rows = times(128 * b, 128, 128)
        v = xs[rows, :].astype(F32)
        s = lax.rsqrt(jnp.mean(v * v, axis=-1, keepdims=True) + EPS)
        normed[rows, :] = (v * s * gain_a).astype(BF)

    loop(4, norm_rows)

    serve(AT_NORM)
    serve(AT_ATT)
    settled(0)
    for k in range(3):
        swap(k, cot_hbm, cot, 1).start()

    def project(m):
        qkv[m] = dg(normed[...], watt[m], 1, 0).astype(BF)
        serve_at(AT_PROJECT, 3, m)

    loop(3, project)

    count = lengths[sq]
    valid = lax.broadcasted_iota(jnp.int32, (1, TOKENS), 1) < count
    lane = lax.broadcasted_iota(jnp.int32, (1, 128), 1)
    keep = (lane < 64, lane >= 64)

    def only(h, v):
        return jnp.where(keep[h], v, jnp.zeros_like(v))

    def attend(hp):
        cols = times(128 * hp, 128, 128)
        key, value = qkv[1, :, cols], qkv[2, :, cols]
        total = [None] * 4
        for h in range(2):
            row = band[pl.ds(2 * hp + h, 1), :]
            tilted = pltpu.roll(jnp.broadcast_to(row, (128, 512)), 0, 1, stride=1, stride_axis=0)
            before = jnp.broadcast_to(row[:, 384:], (128, 128))
            after = jnp.broadcast_to(row[:, 256:384], (128, 128))
            value_h = only(h, value)
            for ib in range(4):
                rows = pl.ds(128 * ib, 128)
                blocks = []
                for jb in range(4):
                    off = jb - ib
                    if off < -1:
                        blocks.append(before)
                    elif off > 1:
                        blocks.append(after)
                    else:
                        blocks.append(tilted[:, 128 * (off + 1) : 128 * (off + 2)])
                scores = dg(only(h, qkv[0, rows, cols]), key, 1, 1) + jnp.concatenate(blocks, axis=1)
                scores = jnp.where(valid, scores, FLOOR)
                top = jnp.max(scores, axis=-1, keepdims=True)
                expo = jnp.exp(scores - top)
                part = jnp.sum(expo, axis=-1, keepdims=True)
                low = (expo * (1.0 / part)).astype(BF)
                probs[2 * hp + h, rows, :] = low
                one = dg(low, value_h, 1, 0)
                total[ib] = one if h == 0 else total[ib] + one
        for ib in range(4):
            mixed[pl.ds(128 * ib, 128), cols] = total[ib].astype(BF)
        serve_at(AT_ATTEND, PAIRS, hp)

    loop(PAIRS, attend)
    serve(AT_WO)
    settled(3)

    def residual(b):
        rows = times(256 * b, 256, 256)
        v = xs[rows, :].astype(F32) + dg(mixed[rows, :], watt[3], 1, 0)
        hid[rows, :] = v
        s = lax.rsqrt(jnp.mean(v * v, axis=-1, keepdims=True) + EPS)
        nf[rows, :] = (v * s * gain_f).astype(BF)
        serve_at(AT_RESIDUAL, 2, b)

    loop(2, residual)

    serve(AT_IN)
    settled(1)
    up_rows, down_rows = pl.ds(0, TOKENS), pl.ds(TOKENS, TOKENS)

    def block(j):
        return times(768 * j, 768, 768)

    def win_block(j):
        return win[:, :, :, block(j)].reshape(768, 768)

    def widen(j):
        v = dg(nf[...], win_block(j), 1, 0)
        sq_v = v * v
        t = jnp.tanh(v * (GELU_A + (GELU_A * GELU_B) * sq_v))
        half = 0.5 + 0.5 * t
        big[j, up_rows, :] = (v * half).astype(BF)
        slope = half + (v * half) * (1.0 - t) * (GELU_A + (3 * GELU_A * GELU_B) * sq_v)
        big[j, down_rows, :] = slope.astype(BF)
        serve_at(AT_WIDEN, 4, j)

    loop(4, widen)
    serve(AT_COTW)
    own[8].wait()
    swap_wait(cot, 1)

    def chunk(i):
        return (3 - z + (i + 1) // 2 + 2 * (i % 2) * (1 - i // 2)) % 4

    def half_ff(i):
        two = pl.ds(2 * chunk(i), 2)
        src = gff.at[two, times(192 * (1 - c), 192, 192)]
        return send(src, sib_ff.at[two], hs_s.at[0], hs_r.at[0, i], sib)

    def grad_ff(i):
        j = chunk(i)
        v = dg(big[j, up_rows, :], cot[...], 0, 0).astype(BF)
        gff[pl.ds(2 * j, 2)] = v.reshape(2, 384, 768)
        half_ff(i).start()
        serve_at(AT_GFF, 4, i)


    def merge_ff(i):
        j = chunk(i)
        half_ff(i).wait_recv()
        rows = times(192 * c, 192, 192)
        for i in range(2):
            gff[2 * j + i, rows] = (gff[2 * j + i, rows].astype(F32) + sib_ff[2 * j + i].astype(F32)).astype(BF)

    def cross_src(g, yy):
        if g == 0:
            return gff.at[:, times(192 * c + 160 * yy, 32, 32)]
        return gin.at[:, times(1536 * c + 1280 * yy, 256, 256)]

    cross_dst = (y_ff, y_in)

    def cross_sum(g):
        return send(cross_src(g, 1 - y), cross_dst[g], yx_s.at[g], yx_r.at[g], yp)

    def add_cross(g):
        cross_sum(g).wait()
        here, came = cross_src(g, y), cross_dst[g]
        here[...] = (here[...].astype(F32) + came[...].astype(F32)).astype(BF)

    def rs_piece(ch, d, yy):
        if ch < 3:
            rows = times(192 * c + 32 + 64 * ch, 64, 32) if ch < 2 else times(192 * c + 160 * yy, 32, 32)
            return gff.at[d, rows]
        if ch < 5:
            return gin.at[times(96 * d, 96, 96), times(1536 * c + 256 + 512 * (ch - 3), 512, 256)]
        if ch == 5:
            return gin.at[times(96 * d, 96, 96), times(1536 * c + 1280 * yy, 256, 256)]
        return win.at[d, c, :, pl.ds(768 * (ch - 6), 768)]

    landing = [r_ffa.at[0], r_ffa.at[1], r_ffb, r_ina.at[0], r_ina.at[1], r_inb, r_att.at[0]]
    landing += [r_ffa.at[0, :, pl.ds(0, 48)], r_ffa.at[1, :, pl.ds(0, 48)], r_att.at[1]]

    def rs_send(ch, e):
        ahead = e // FAR
        part = rs_piece(ch, owner((1 - ahead) * (FAR - e) + ahead * (e - EVENTS)), y)
        return send(part, landing[ch].at[e], rr_s.at[ch], ag_r.at[ch, e], side(e))

    def rs_begin(ch):
        rs_send(ch, 0).start()
        rs_send(ch, FAR).start()

    def rs_event(ch, e):
        rs_send(ch, e).wait_recv()
        here = rs_piece(ch, owner(FAR - 1 - e if e < FAR else e - EVENTS + 1), y)
        here[...] = (here[...].astype(F32) + landing[ch][e].astype(F32)).astype(BF)
        if e not in (FAR - 1, EVENTS - 1):
            rs_send(ch, e + 1).start()

    def half_in(k):
        src = gin.at[:, times(1536 * (1 - c) + 384 * k, 384, 384)]
        return send(src, sib_in.at[k], hs_s.at[1], hs_r.at[1, k], sib)

    def merge_in(k):
        half_in(k).wait_recv()
        cols = times(1536 * c + 384 * k, 384, 384)
        gin[:, cols] = (gin[:, cols].astype(F32) + sib_in[k].astype(F32)).astype(BF)

    def sib_rows(t):
        return sib_ff.at[:, times(48 * t, 48, 48)]

    def half_att(t):
        return send(win.at[:, 1 - c, :, block(t)], sib_rows(t), hs_s.at[2], hs_r.at[2, t], sib)

    def merge_att(t):
        half_att(t).wait_recv()
        win[:, c, :, block(t)] = (win[:, c, :, block(t)].astype(F32) + sib_rows(t)[...].astype(F32)).astype(BF)

    final = [f_ff, f_in] + [f_att.at[t] for t in range(4)]

    def own_piece(g):
        if g == 0:
            return gff.at[dp, times(192 * c + 32, 128, 32)]
        if g == 1:
            return gin.at[r96, times(1536 * c + 256, 1024, 256)]
        return rs_piece(4 + g, dp, y)

    def out_piece(g, cc, yy):
        if g == 0:
            return gff_hbm.at[times(192 * cc + 32, 128, 32) if yy is None else times(192 * cc + 160 * yy, 32, 32)]
        if g == 1:
            if yy is None:
                return gin_hbm.at[:, times(1536 * cc + 256, 1024, 256)]
            return gin_hbm.at[:, times(1536 * cc + 1280 * yy, 256, 256)]
        return gatt_hbm.at[g - 2, times(48 * cc, 48, 48)]

    def share_a(g):
        return send(own_piece(g), final[g], fa_s.at[g], fa_r.at[g], yp)

    def share_b(g, k):
        return send(rs_piece(3 * g + 2, dp, y), out_piece(g, c, y), fb_s.at[g], fb_r.at[g], peers[k])

    def share_sum(g):
        return send(final[g], out_piece(g, c, None), fo_s.at[g], fo_r.at[g], sib)

    def keep_b(g):
        return pltpu.make_async_copy(rs_piece(3 * g + 2, dp, y), out_piece(g, c, y), fl.at[g, 0])

    def keep_sum(g):
        return pltpu.make_async_copy(final[g], out_piece(g, c, None), fl.at[g, 1])

    def finish_b(g):
        for k in range(3):
            share_b(g, k).start()
        keep_b(g).start()

    def finish_sum(g):
        share_a(g).wait()
        final[g][...] = (final[g][...].astype(F32) + own_piece(g)[...].astype(F32)).astype(BF)
        share_sum(g).start()
        keep_sum(g).start()

    def hop(k):
        return send(sums.at[k], sums_in.at[k], bf_s.at[k], bf_r.at[k], (yp, sib)[k])

    def hop_on(k):
        if k < 2:
            hop(k).wait()
            sums[k + 1] = sums[k] + sums_in[k]
        if k == 0:
            hop(1).start()
        elif k == 1:
            for dev in others:
                send(sums.at[2], spread.at[dp], bf_s.at[2], bf_r.at[2], dev).start()
            spread[dp] = sums[2]
        else:
            send(spread.at[pl.ds(0, 7)], spread.at[pl.ds(0, 7)], bf_s.at[2], bf_r.at[2], sib).wait()
            total = spread[0]
            for k in range(1, DP):
                total = total + spread[k]
            small_out[...] = total

    def merge(g, k):
        (merge_ff, merge_in, merge_att)[g](k)

    def go(g):
        if g == 0:
            cross_sum(0).start()
        elif g == 1:
            cross_sum(1).start()
            rs_begin(3)
            rs_begin(4)
        else:
            rs_begin(4 + g)

    def leave(e):
        for ch in range(2):
            rs_send(ch, e).start()

    def cross_in(g):
        add_cross(g)
        rs_begin(3 * g + 2)

    acts |= {
        RS: rs_event, HALF: merge, GO: go, LEAVE: leave, XC: cross_in, SHARE_A: lambda g: share_a(g).start(), FIN_B: finish_b,
        FSUM: finish_sum, HOP: hop_on,
    }

    loop(4, grad_ff)
    serve(AT_MFF)
    serve(AT_FF)
    settled(2)

    def grad_up(j):
        v = dg(cot[...], wff[block(j), :], 1, 1) * big[j, down_rows, :].astype(F32)
        big[j, down_rows, :] = v.astype(BF)
        serve_at(AT_GUP, 4, j)

    loop(4, grad_up)

    def grad_in(i):
        j = (2 * (1 - c) + i) % 4
        gin[:, block(j)] = dg(nf[...], big[j, down_rows, :], 0, 0).astype(BF)

        @pl.when(i == 1)
        def _():
            for k in range(4):
                half_in(k).start()

        serve_at(AT_GIN, 4, i)

    loop(4, grad_in)

    acc[...] = jnp.zeros_like(acc)

    def grad_nf(j):
        acc[...] += dg(big[j, down_rows, :], win_block(j), 1, 1)
        serve_at(AT_GNF, 4, j)

    loop(4, grad_nf)

    def norm_back(v, gain, grad):
        s = lax.rsqrt(jnp.mean(v * v, axis=-1, keepdims=True) + EPS)
        scaled = grad * gain
        back = s * scaled - v * (s * s * s) * jnp.mean(v * scaled, axis=-1, keepdims=True)
        return back, jnp.sum(grad * v * s, axis=0, keepdims=True)

    def ffn_norm_back(b, total):
        rows = times(128 * b, 128, 128)
        v = hid[rows, :]
        back, part = norm_back(v, gain_f, acc[rows, :])
        grad = cot[rows, :].astype(F32) + back
        acc[rows, :] = grad
        cot[rows, :] = grad.astype(BF)
        return total + part

    g_ffn_gain = lax.fori_loop(0, 4, ffn_norm_back, jnp.zeros((1, WIDTH), F32))

    serve(AT_FNORM)
    serve(AT_PREWO)
    gather_sent(1)
    win[:, :, :, block(3)] = dg(mixed[...], cot[...], 0, 0).astype(BF).reshape(8, 2, 48, 768)

    half_att(3).start()
    serve(AT_GWO)
    nf[...] = dg(cot[...], watt[3], 1, 1).astype(BF)
    serve(AT_GMIX)


    def give(src, dst_hbm, at, k):
        dev = peers[k]
        return send(src.at[times(128 * dev[1], 128, 128)], dst_hbm.at[sq], a2_s.at[at], a2_r.at[at], dev)

    def pool_send(k):
        return send(pool, pool_hbm.at[sq], a2_s.at[4], a2_r.at[4], peers[k])

    pool_own = pltpu.make_async_copy(pool, pool_hbm.at[sq], loc.at[2])
    lay = big.at[0, up_rows]
    lay_own = pltpu.make_async_copy(lay.at[mine], out_hbm.at[sq], loc.at[1])
    def narrow(j):
        part = dg(big[j, up_rows, :], wff[block(j), :], 1, 0)
        hid[...] += part
        serve_at(AT_NARROW, 4, j)

    loop(4, narrow)
    lay[...] = hid[...].astype(BF)
    for k in range(3):
        give(lay, out_hbm, 2, k).start()
    lay_own.start()
    here_t = lax.broadcasted_iota(jnp.int32, (TOKENS, 1), 0) < count
    mean = jnp.sum(jnp.where(here_t, hid[...], 0.0), axis=0, keepdims=True) / count.astype(F32)
    pool[...] = jnp.broadcast_to(mean, (8, WIDTH))
    pool_own.start()
    for k in range(3):
        pool_send(k).start()
    serve(AT_LAY)

    flip_sum = lax.broadcasted_iota(jnp.int32, (128, 128), 0) + lax.broadcasted_iota(jnp.int32, (128, 128), 1)
    flip = (flip_sum == 127).astype(F32)

    def attend_back(hp):
        cols = times(128 * hp, 128, 128)
        key, value = qkv[1, :, cols], qkv[2, :, cols]
        query, grad = qkv[0, :, cols], nf[:, cols]
        g_query = [None] * 4
        for h in range(2):
            key_h = only(h, key)
            before = after = jnp.zeros((128, 128), F32)
            near = [jnp.zeros((128, 128), F32) for _ in range(3)]
            for ib in range(4):
                rows = pl.ds(128 * ib, 128)
                wide = probs[2 * hp + h, rows, :].astype(F32)
                d_probs = dg(only(h, nf[rows, cols]), value, 1, 1)
                mean_d = jnp.sum(wide * d_probs, axis=-1, keepdims=True)
                d_score = wide * (d_probs - mean_d)
                for jb in range(4):
                    off, part = jb - ib, d_score[:, 128 * jb : 128 * (jb + 1)]
                    if off < -1:
                        before = before + part
                    elif off > 1:
                        after = after + part
                    else:
                        near[off + 1] = near[off + 1] + part
                d_low = d_score.astype(BF)
                d_both[pl.ds(512 * h + 128 * ib, 128), :] = d_low
                one = dg(d_low, key_h, 1, 0)
                g_query[ib] = one if h == 0 else g_query[ib] + one
            tilted = exact(flip, jnp.concatenate(near, axis=1), 1, 0)
            tilted = jnp.concatenate([tilted, jnp.zeros((128, 128), F32)], axis=1)
            flat = jnp.sum(pltpu.roll(tilted, 385, 1, stride=1, stride_axis=0), axis=0, keepdims=True)
            far = jnp.concatenate(
                [
                    jnp.zeros((1, 256), F32),
                    jnp.sum(after, axis=0, keepdims=True),
                    jnp.sum(before, axis=0, keepdims=True),
                ],
                axis=1,
            )
            diag[pl.ds(2 * hp + h, 1), :] = flat + far
        both_query = jnp.concatenate([only(0, query), only(1, query)], axis=0)
        both_grad = jnp.concatenate([only(0, grad), only(1, grad)], axis=0)
        qkv[1, :, cols] = dg(d_both[...], both_query, 0, 0).astype(BF)
        qkv[2, :, cols] = dg(probs[pl.ds(2 * hp, 2)].reshape(1024, 512), both_grad, 0, 0).astype(BF)
        for ib in range(4):
            qkv[0, pl.ds(128 * ib, 128), cols] = g_query[ib].astype(BF)

        @pl.when(hp % 2 == 1)
        def _():
            t = hp // 2
            three = times(256 * t, 256, 256)
            grads = jnp.concatenate([qkv[0, :, three], qkv[1, :, three], qkv[2, :, three]], axis=1)
            win[:, :, :, block(t)] = dg(normed[...], grads, 0, 0).astype(BF).reshape(8, 2, 48, 768)
            half_att(t).start()

        serve_at(AT_AB, PAIRS, hp)

    loop(PAIRS, attend_back)
    def attn_norm_back(b, total):
        rows = times(256 * b, 256, 256)
        grad = dg(qkv[0, rows, :], watt[0], 1, 1) + dg(qkv[1, rows, :], watt[1], 1, 1) + dg(qkv[2, rows, :], watt[2], 1, 1)
        back, part = norm_back(xs[rows, :].astype(F32), gain_a, grad)
        mixed[rows, :] = (acc[rows, :] + back).astype(BF)
        serve_at(AT_GN, 2, b)
        return total + part

    g_attn_gain = lax.fori_loop(0, 2, attn_norm_back, jnp.zeros((1, WIDTH), F32))

    sums[0] = jnp.zeros((32, 128), F32)
    sums[0, 0:16, 0:32] = exact(diag[...], band_bucket(32), 1, 1)
    for k in range(6):
        sums[0, 16 + k : 17 + k, :] = g_attn_gain[:, 128 * k : 128 * (k + 1)]
        sums[0, 22 + k : 23 + k, :] = g_ffn_gain[:, 128 * k : 128 * (k + 1)]

    hop(0).start()
    for k in range(3):
        give(mixed, gx_hbm, 3, k).start()
    gx_own = pltpu.make_async_copy(mixed.at[mine], gx_hbm.at[sq], loc.at[0])
    gx_own.start()
    serve(AT_GX)
    serve(AT_TAIL)

    for g in range(6):
        if g < 2:
            keep_b(g).wait()
            same = (sib_ff.at[pl.ds(0, 3), pl.ds(0, 32)], gin.at[pl.ds(0, 288), pl.ds(0, 256)])[g]
            send(same, same, fb_s.at[g], fb_r.at[g], sib).wait()
        keep_sum(g).wait()
        share_sum(g).wait_send()
        came = out_piece(g, 1 - c, None)
        send(came, came, fo_s.at[g], fo_r.at[g], sib).wait_recv()
    for ch in range(10):
        send(landing[ch], landing[ch], rr_s.at[ch], ag_r.at[ch, 0], sib).wait_send()
    for g, same in enumerate((sib_ff, sib_in, sib_ff)):
        send(same, same, hs_s.at[g], hs_r.at[g, 0], sib).wait_send()
    gather_sent(0)
    gather_sent(2)
    gather_sent(3)
    three(out_hbm.at[pl.ds(0, 3)], 2).wait()
    three(gx_hbm.at[pl.ds(0, 3)], 3).wait()
    three(pool_hbm.at[pl.ds(0, 3)], 4).wait()
    three(xs.at[pl.ds(0, 384)], 0).wait_send()
    three(cot.at[pl.ds(0, 384)], 1).wait_send()
    lay_own.wait()
    gx_own.wait()
    pool_own.wait()


def finish_kernel(
    out_in, gx_in, att_in, in_in, ff_in, pool_in, small_in,
    out, gx, pool_out, gain_a, gq, gk, gv, go, g_table, gain_f, gin_out, gff_out,
    v_out, v_gx, v_att, v_in, v_ff, v_pool, w_att, w_in, w_ff, w_pool, sem_in, sem_out,
):
    sources = (in_in, ff_in, att_in, pool_in, out_in, gx_in)
    held = (v_in, v_ff, v_att, v_pool, v_out, v_gx)
    reads = [pltpu.make_async_copy(a, b, sem_in.at[k]) for k, (a, b) in enumerate(zip(sources, held))]
    for read in reads:
        read.start()
    g_table[...] = small_in[0:HEAD_N, 0:32]
    for k in range(6):
        gain_a[128 * k : 128 * (k + 1)] = small_in[16 + k : 17 + k, :].reshape(128)
        gain_f[128 * k : 128 * (k + 1)] = small_in[22 + k : 23 + k, :].reshape(128)
    writes = []

    def write(src, dst):
        writes.append(pltpu.make_async_copy(src, dst, sem_out.at[len(writes)]))
        writes[-1].start()

    reads[0].wait()
    w_in[...] = v_in[...].astype(F32)
    write(w_in, gin_out)
    reads[1].wait()
    w_ff[...] = v_ff[...].astype(F32)
    write(w_ff, gff_out)
    reads[2].wait()
    w_att[3] = v_att[3].astype(F32)
    for t in range(3):
        for i in range(3):
            w_att[i, :, 256 * t : 256 * (t + 1)] = v_att[t, :, 256 * i : 256 * (i + 1)].astype(F32)
    for i, ref in enumerate((gq, gk, gv, go)):
        write(w_att.at[i], ref)
    reads[3].wait()
    for p in range(SEQ):
        w_pool[p : p + 1, :] = v_pool[p, 0:1, :]
    write(w_pool, pool_out)
    reads[4].wait()
    write(v_out, out)
    reads[5].wait()
    write(v_gx, gx)
    for copy in writes:
        copy.wait()


def passage_shards(
    passages, lengths, attn_gain, w_query, w_key, w_value, w_attn_out, bias_table, ffn_gain, w_in, w_ff_out, cotangent
):
    any_space = pl.BlockSpec(memory_space=pl.ANY)
    vmem = pl.BlockSpec(memory_space=pltpu.VMEM)
    dma = pltpu.SemaphoreType.DMA
    scratch = [
        pltpu.VMEM(shape, BF)
        for shape in (
            (4, 768, 768), (8, 2, 48, 3072), (3072, 768), (768, 3072), (8, 384, 768), (4, 1024, 768), (12, 512, 512),
            (512, 768), (512, 768), (512, 768), (3, 512, 768), (512, 768), (512, 768),
        )
    ]
    scratch += [pltpu.VMEM(shape, F32) for shape in ((512, 768), (512, 768), (16, 512), (16, 512))]
    scratch += [
        pltpu.VMEM(shape, BF)
        for shape in (
            (1024, 512), (8, 192, 768), (4, 768, 384), (8, 32, 768), (768, 256),
            (2, 7, 64, 768), (7, 32, 768), (2, 7, 96, 512), (7, 96, 256), (2, 7, 48, 768),
            (128, 768), (96, 1024), (4, 48, 768),
        )
    ]
    scratch += [pltpu.VMEM((n, 32, 128), F32) for n in (3, 2, DP)]
    scratch.append(pltpu.VMEM((8, 768), F32))
    scratch += [
        dma(shape)
        for shape in (
            (8,), (10, 7), (8,), (8,), (3,), (3, 7), (3,), (3,), (10,), (9,), (5,), (5,), (3,), (3, 4), (2,), (2,),
            (6,), (6,), (2,), (2,), (6,), (6,), (6, 2), (3,), (3,),
        )
    ]
    sums = pl.pallas_call(
        layer_kernel,
        out_shape=(
            jax.ShapeDtypeStruct((4, 128, 768), BF),
            jax.ShapeDtypeStruct((4, 128, 768), BF),
            jax.ShapeDtypeStruct((4, 96, 768), BF),
            jax.ShapeDtypeStruct((96, 3072), BF),
            jax.ShapeDtypeStruct((384, 768), BF),
            jax.ShapeDtypeStruct((4, 8, 768), F32),
            jax.ShapeDtypeStruct((32, 128), F32),
        ),
        in_specs=[any_space] * 8 + [pl.BlockSpec(memory_space=pltpu.SMEM)] + [vmem] * 3,
        out_specs=(any_space,) * 6 + (vmem,),
        scratch_shapes=scratch,
        compiler_params=pltpu.CompilerParams(collective_id=0, has_side_effects=True, vmem_limit_bytes=64 * 2**20),
        name="layer",
    )(
        passages, cotangent, w_query, w_key, w_value, w_attn_out, w_in, w_ff_out, lengths,
        attn_gain, ffn_gain, bias_table.T,
    )
    square = jax.ShapeDtypeStruct((96, 768), F32)
    gain = jax.ShapeDtypeStruct((WIDTH,), F32)
    outs = pl.pallas_call(
        finish_kernel,
        out_shape=(
            jax.ShapeDtypeStruct((4, 128, 768), BF),
            jax.ShapeDtypeStruct((4, 128, 768), BF),
            jax.ShapeDtypeStruct((4, 768), F32),
            gain,
            square,
            square,
            square,
            square,
            jax.ShapeDtypeStruct((HEAD_N, 32), F32),
            gain,
            jax.ShapeDtypeStruct((96, 3072), F32),
            jax.ShapeDtypeStruct((384, 768), F32),
        ),
        in_specs=[any_space] * 6 + [vmem],
        out_specs=(any_space,) * 3 + (vmem,) + (any_space,) * 4 + (vmem,) * 2 + (any_space,) * 2,
        scratch_shapes=[
            pltpu.VMEM((4, 128, 768), BF),
            pltpu.VMEM((4, 128, 768), BF),
            pltpu.VMEM((4, 96, 768), BF),
            pltpu.VMEM((96, 3072), BF),
            pltpu.VMEM((384, 768), BF),
            pltpu.VMEM((4, 8, 768), F32),
            pltpu.VMEM((4, 96, 768), F32),
            pltpu.VMEM((96, 3072), F32),
            pltpu.VMEM((384, 768), F32),
            pltpu.VMEM((4, 768), F32),
            dma((6,)),
            dma((9,)),
        ],
        compiler_params=pltpu.CompilerParams(vmem_limit_bytes=64 * 2**20),
        name="finish",
    )(*sums)
    return (outs[0], outs[2], outs[1], *outs[3:8], outs[8].T, *outs[9:])


def solution(mesh):
    ring = (mesh.shape["dp"], mesh.shape["seq"]) == (DP, SEQ)
    return jax.shard_map(
        passage_shards if ring else shards,
        mesh=mesh,
        in_specs=(
            P("dp", "seq", None),
            P("dp"),
            P(),
            P("dp", None),
            P("dp", None),
            P("dp", None),
            P("dp", None),
            P(),
            P(),
            P("dp", None),
            P("dp", None),
            P("dp", "seq", None),
        ),
        out_specs=(
            P("dp", "seq", None),
            P("dp", None),
            P("dp", "seq", None),
            P(),
            P("dp", None),
            P("dp", None),
            P("dp", None),
            P("dp", None),
            P(),
            P(),
            P("dp", None),
            P("dp", None),
        ),
        check_vma=False,
    )
```

```python
import math

import jax
import jax.numpy as jnp
from jax import lax
from jax.experimental import pallas as pl
from jax.experimental.pallas import tpu as pltpu
from jax.sharding import PartitionSpec as P

MAXDIST = 128


EPS = 1e-06
HIGH = lax.Precision.HIGHEST
FLOOR = -1e30


def bucket_index(relative, buckets, reach):
    half_count = buckets // 2
    exact_count = half_count // 2
    distance = jnp.abs(relative)
    result = jnp.minimum(distance, exact_count)
    for power in range(1, half_count - exact_count):
        bound_at = math.ceil(
            exact_count * (reach / exact_count) ** (power / (half_count - exact_count)) - 1e-06
        )
        result = result + (distance >= bound_at).astype(jnp.int32)
    return result + (relative > 0).astype(jnp.int32) * half_count


def rms_norm(values, gain_vec):
    return values * lax.rsqrt(jnp.mean(values * values, axis=-1, keepdims=True) + EPS) * gain_vec


def attend_forward(query_four, key_four, value_four, bias_rows, key_valid):
    scores = (
        jnp.einsum("pqhe,pkhe->phqk", query_four, key_four, preferred_element_type=jnp.float32)
        + bias_rows[None]
    )
    scores = jnp.where(key_valid[:, None, None, :], scores, FLOOR)
    row_top = jnp.max(scores, axis=-1, keepdims=True)
    expo = jnp.exp(scores - row_top)
    row_total = jnp.sum(expo, axis=-1, keepdims=True)
    log_total = row_top + jnp.log(row_total)
    attn_probs = (expo / row_total).astype(jnp.bfloat16)
    mixed_rows = jnp.einsum(
        "phqk,pkhe->pqhe", attn_probs, value_four, preferred_element_type=jnp.float32
    )
    return (mixed_rows.astype(jnp.bfloat16), log_total)


def attend_backward(query_four, key_four, value_four, grad_mixed, log_total, key_valid, bias_rows):

    def one_passage(score_sum, pieces):
        query_p, key_p, value_p, grad_p, log_p, valid_p = pieces
        score_p = (
            jnp.einsum("qhe,khe->hqk", query_p, key_p, preferred_element_type=jnp.float32)
            + bias_rows
        )
        score_p = jnp.where(valid_p[None, None, :], score_p, FLOOR)
        prob_p = jnp.exp(score_p - log_p)
        grad_prob = jnp.einsum("qhe,khe->hqk", grad_p, value_p, preferred_element_type=jnp.float32)
        grad_score = (
            prob_p * (grad_prob - jnp.sum(prob_p * grad_prob, axis=-1, keepdims=True))
        ).astype(jnp.bfloat16)
        grad_query_p = jnp.einsum(
            "hqk,khe->qhe", grad_score, key_p, preferred_element_type=jnp.float32
        ).astype(jnp.bfloat16)
        grad_key_p = jnp.einsum(
            "hqk,qhe->khe", grad_score, query_p, preferred_element_type=jnp.float32
        )
        grad_value_p = jnp.einsum(
            "hqk,qhe->khe", prob_p.astype(jnp.bfloat16), grad_p, preferred_element_type=jnp.float32
        )
        return (
            score_sum + grad_score.astype(jnp.float32),
            (grad_query_p, grad_key_p, grad_value_p),
        )

    start_sum = jnp.zeros(bias_rows.shape, jnp.float32)
    return lax.scan(
        one_passage, start_sum, (query_four, key_four, value_four, grad_mixed, log_total, key_valid)
    )


def shards(
    passages,
    lengths,
    attn_gain,
    w_query,
    w_key,
    w_value,
    w_attn_out,
    bias_table,
    ffn_gain,
    w_in,
    w_ff_out,
    cotangent,
):
    n_pass, local_rows, width = passages.shape
    n_buckets, n_heads = bias_table.shape
    head_dim = width // n_heads
    seq_count = lax.axis_size("seq")
    full_len = local_rows * seq_count
    row_count = n_pass * local_rows
    first_row = lax.axis_index("seq") * local_rows
    gathered = (
        lax.all_gather(w_query, "dp", axis=0, tiled=True),
        lax.all_gather(w_key, "dp", axis=0, tiled=True),
        lax.all_gather(w_value, "dp", axis=0, tiled=True),
        lax.all_gather(w_attn_out, "dp", axis=0, tiled=True),
        lax.all_gather(w_in, "dp", axis=0, tiled=True),
        lax.all_gather(w_ff_out, "dp", axis=0, tiled=True),
    )
    wq_full, wk_full, wv_full, wo_full, win_full, wff_full = gathered
    key_pos = jnp.arange(full_len, dtype=jnp.int32)
    query_pos = first_row + jnp.arange(local_rows, dtype=jnp.int32)
    key_valid = key_pos[None, :] < lengths[:, None]
    query_valid = query_pos[None, :] < lengths[:, None]
    inputs = passages.astype(jnp.float32).reshape(row_count, width)
    normed = rms_norm(inputs, attn_gain).astype(jnp.bfloat16)
    query_rows = jnp.dot(normed, wq_full, preferred_element_type=jnp.float32).astype(jnp.bfloat16)
    key_rows = jnp.dot(normed, wk_full, preferred_element_type=jnp.float32).astype(jnp.bfloat16)
    value_rows = jnp.dot(normed, wv_full, preferred_element_type=jnp.float32).astype(jnp.bfloat16)
    query_local = query_rows.reshape(n_pass, local_rows, n_heads, head_dim)
    relative = key_pos[None, :] - query_pos[:, None]
    one_hot = (
        bucket_index(relative, n_buckets, MAXDIST)[:, :, None]
        == jnp.arange(n_buckets, dtype=jnp.int32)
    ).astype(jnp.float32)
    bias_rows = jnp.einsum("qkb,bh->hqk", one_hot, bias_table, precision=HIGH)
    key_all, value_all = (
        lax.all_gather(key_rows.reshape(n_pass, local_rows, width), "seq", axis=1, tiled=True),
        lax.all_gather(value_rows.reshape(n_pass, local_rows, width), "seq", axis=1, tiled=True),
    )
    key_four = key_all.reshape(n_pass, full_len, n_heads, head_dim)
    value_four = value_all.reshape(n_pass, full_len, n_heads, head_dim)
    mixed_four, log_total = attend_forward(query_local, key_four, value_four, bias_rows, key_valid)
    mixed_rows = mixed_four.reshape(row_count, width)
    hidden = inputs + jnp.dot(mixed_rows, wo_full, preferred_element_type=jnp.float32)
    normed_ffn = rms_norm(hidden, ffn_gain).astype(jnp.bfloat16)
    up_rows = jnp.dot(normed_ffn, win_full, preferred_element_type=jnp.float32)
    activated = jax.nn.gelu(up_rows).astype(jnp.bfloat16)
    output_rows = hidden + jnp.dot(activated, wff_full, preferred_element_type=jnp.float32)
    pool_part = jnp.sum(
        output_rows.reshape(n_pass, local_rows, width)
        * query_valid[:, :, None].astype(jnp.float32),
        axis=1,
    )
    pooled = lax.psum(pool_part, "seq") / lengths[:, None].astype(jnp.float32)
    gathered = (
        lax.all_gather(w_query, "dp", axis=0, tiled=True),
        lax.all_gather(w_key, "dp", axis=0, tiled=True),
        lax.all_gather(w_value, "dp", axis=0, tiled=True),
        lax.all_gather(w_attn_out, "dp", axis=0, tiled=True),
        lax.all_gather(w_in, "dp", axis=0, tiled=True),
        lax.all_gather(w_ff_out, "dp", axis=0, tiled=True),
    )
    wq_full, wk_full, wv_full, wo_full, win_full, wff_full = gathered
    grad_out = cotangent.astype(jnp.float32).reshape(row_count, width)
    grad_branch = grad_out.astype(jnp.bfloat16)
    g_ff_out = jnp.einsum("rf,rd->fd", activated, grad_branch, preferred_element_type=jnp.float32)
    grad_act = jnp.einsum("rd,fd->rf", grad_branch, wff_full, preferred_element_type=jnp.float32)
    _, gelu_pull = jax.vjp(jax.nn.gelu, up_rows)
    grad_up = gelu_pull(grad_act)[0].astype(jnp.bfloat16)
    g_in = jnp.einsum("rd,rf->df", normed_ffn, grad_up, preferred_element_type=jnp.float32)
    grad_normed_ffn = jnp.einsum("rf,df->rd", grad_up, win_full, preferred_element_type=jnp.float32)
    _, ffn_pull = jax.vjp(rms_norm, hidden, ffn_gain)
    grad_hidden_norm, g_ffn_gain = ffn_pull(grad_normed_ffn)
    grad_hidden = grad_out + grad_hidden_norm
    grad_attn = grad_hidden.astype(jnp.bfloat16)
    g_attn_out = jnp.einsum("rd,re->de", mixed_rows, grad_attn, preferred_element_type=jnp.float32)
    grad_mixed = jnp.einsum("re,de->rd", grad_attn, wo_full, preferred_element_type=jnp.float32)
    grad_mixed = grad_mixed.astype(jnp.bfloat16).reshape(n_pass, local_rows, n_heads, head_dim)
    score_sum, (grad_query, grad_key, grad_value) = attend_backward(
        query_local, key_four, value_four, grad_mixed, log_total, key_valid, bias_rows
    )
    grad_key, grad_value = (
        lax.psum_scatter(
            grad_key.reshape(n_pass, full_len, width).astype(jnp.bfloat16),
            "seq",
            scatter_dimension=1,
            tiled=True,
        ).astype(jnp.float32),
        lax.psum_scatter(
            grad_value.reshape(n_pass, full_len, width).astype(jnp.bfloat16),
            "seq",
            scatter_dimension=1,
            tiled=True,
        ).astype(jnp.float32),
    )
    grad_query = grad_query.reshape(row_count, width)
    grad_key = grad_key.astype(jnp.bfloat16).reshape(row_count, width)
    grad_value = grad_value.astype(jnp.bfloat16).reshape(row_count, width)
    g_table = jnp.einsum("qkb,hqk->bh", one_hot, score_sum, precision=HIGH)
    g_query = jnp.einsum("rd,re->de", normed, grad_query, preferred_element_type=jnp.float32)
    g_key = jnp.einsum("rd,re->de", normed, grad_key, preferred_element_type=jnp.float32)
    g_value = jnp.einsum("rd,re->de", normed, grad_value, preferred_element_type=jnp.float32)
    grad_normed = jnp.einsum("re,de->rd", grad_query, wq_full, preferred_element_type=jnp.float32)
    grad_normed = grad_normed + jnp.einsum(
        "re,de->rd", grad_key, wk_full, preferred_element_type=jnp.float32
    )
    grad_normed = grad_normed + jnp.einsum(
        "re,de->rd", grad_value, wv_full, preferred_element_type=jnp.float32
    )
    _, attn_pull = jax.vjp(rms_norm, inputs, attn_gain)
    grad_inputs_norm, g_attn_gain = attn_pull(grad_normed)
    grad_input = (
        (grad_hidden + grad_inputs_norm).astype(jnp.bfloat16).reshape(n_pass, local_rows, width)
    )
    row_grads = (
        lax.psum_scatter(g_query, "dp", scatter_dimension=0, tiled=True),
        lax.psum_scatter(g_key, "dp", scatter_dimension=0, tiled=True),
        lax.psum_scatter(g_value, "dp", scatter_dimension=0, tiled=True),
        lax.psum_scatter(g_attn_out, "dp", scatter_dimension=0, tiled=True),
        lax.psum_scatter(g_in, "dp", scatter_dimension=0, tiled=True),
        lax.psum_scatter(g_ff_out, "dp", scatter_dimension=0, tiled=True),
    )
    row_grads = (
        lax.psum(row_grads[0].astype(jnp.bfloat16), "seq").astype(jnp.float32),
        lax.psum(row_grads[1].astype(jnp.bfloat16), "seq").astype(jnp.float32),
        lax.psum(row_grads[2].astype(jnp.bfloat16), "seq").astype(jnp.float32),
        lax.psum(row_grads[3].astype(jnp.bfloat16), "seq").astype(jnp.float32),
        lax.psum(row_grads[4].astype(jnp.bfloat16), "seq").astype(jnp.float32),
        lax.psum(row_grads[5].astype(jnp.bfloat16), "seq").astype(jnp.float32),
    )
    small_sums = lax.psum((g_attn_gain, g_ffn_gain, g_table), ("dp", "seq"))
    layer_out = output_rows.astype(jnp.bfloat16).reshape(n_pass, local_rows, width)
    return (
        layer_out,
        pooled,
        grad_input,
        small_sums[0],
        row_grads[0],
        row_grads[1],
        row_grads[2],
        row_grads[3],
        small_sums[2],
        small_sums[1],
        row_grads[4],
        row_grads[5],
    )


DP, SEQ = 8, 4
FAR, EVENTS = 4, 7
BF, F32 = jnp.bfloat16, jnp.float32
MESH_ID = pl.DeviceIdType.MESH
TOKENS, WIDTH, HIDDEN, HEAD_N = 512, 768, 3072, 12
PAIRS = HEAD_N // 2
GELU_A, GELU_B = math.sqrt(2 / math.pi), 0.044715


AG, CR, BEGIN, RS, HALF, GO, XC, SHARE_A, FIN_B, FSUM, HOP, LEAVE = range(12)
(
    AT_A1, AT_NORM, AT_ATT, AT_WO, AT_IN, AT_COTW, AT_MFF, AT_FF, AT_FNORM, AT_PREWO, AT_GWO, AT_GMIX, AT_LAY,
    AT_GX, AT_TAIL, AT_PROJECT, AT_ATTEND, AT_RESIDUAL, AT_WIDEN, AT_GFF, AT_GUP, AT_GIN, AT_GNF, AT_NARROW, AT_AB,
    AT_GN,
) = range(26)
PLAN = {
    AT_A1: (
        (AG, 2, 0), (AG, 2, 4), (AG, 1, 0), (AG, 1, 4), (AG, 0, 0), (AG, 0, 4), (AG, 2, 1), (AG, 2, 5), (AG, 1, 1),
        (AG, 1, 5), (AG, 0, 1), (AG, 0, 5), (AG, 2, 2),
    ),
    AT_NORM: (
        (AG, 2, 6),
    ),
    AT_ATT: (
        (CR, 2, 0), (AG, 1, 2), (CR, 2, 4), (AG, 1, 6), (CR, 2, 1), (AG, 0, 2), (BEGIN, 3), (BEGIN, 1), (CR, 2, 5),
        (AG, 0, 6), (AG, 2, 3), (CR, 2, 2), (AG, 1, 3), (CR, 2, 6), (AG, 0, 3), (AG, 7, 0), (CR, 2, 3), (AG, 7, 4),
    ),
    (AT_PROJECT, 0): (
        (AG, 4, 0), (AG, 4, 4),
    ),
    (AT_PROJECT, 2): (
        (AG, 3, 0),
    ),
    (AT_ATTEND, 0): (
        (AG, 3, 4), (AG, 7, 1),
    ),
    (AT_ATTEND, 1): (
        (AG, 7, 5), (AG, 4, 1),
    ),
    (AT_ATTEND, 2): (
        (AG, 4, 5), (AG, 3, 1),
    ),
    (AT_ATTEND, 3): (
        (AG, 3, 5), (AG, 7, 2),
    ),
    (AT_ATTEND, 4): (
        (AG, 7, 6), (AG, 4, 2), (CR, 4, 0),
    ),
    (AT_ATTEND, 5): (
        (AG, 4, 6), (CR, 4, 4), (AG, 3, 2), (BEGIN, 2),
    ),
    AT_WO: (
        (CR, 4, 1), (AG, 3, 6), (AG, 7, 3), (CR, 4, 5), (AG, 4, 3),
    ),
    (AT_RESIDUAL, 0): (
        (CR, 4, 2),
    ),
    (AT_RESIDUAL, 1): (
        (AG, 3, 3),
    ),
    AT_IN: (
        (AG, 6, 0), (CR, 4, 6), (AG, 6, 4), (CR, 4, 3), (AG, 5, 0),
    ),
    (AT_WIDEN, 0): (
        (AG, 5, 4), (AG, 6, 1), (CR, 6, 0),
    ),
    (AT_WIDEN, 1): (
        (AG, 6, 5),
    ),
    (AT_WIDEN, 2): (
        (AG, 5, 1), (CR, 6, 4),
    ),
    (AT_WIDEN, 3): (
        (AG, 5, 5),
    ),
    (AT_GFF, 0): (
        (AG, 6, 2), (CR, 6, 1),
    ),
    (AT_GFF, 1): (
        (AG, 6, 6),
    ),
    (AT_GFF, 2): (
        (AG, 5, 2), (CR, 6, 5),
    ),
    (AT_GFF, 3): (
        (AG, 5, 6), (HALF, 0, 0), (LEAVE, 0),
    ),
    AT_MFF: (
        (AG, 6, 3), (HALF, 0, 1), (CR, 6, 2), (HALF, 0, 2), (LEAVE, 4), (AG, 5, 3), (CR, 6, 6), (HALF, 0, 3), (GO, 0),
        (RS, 0, 0),
    ),
    AT_FF: (
        (RS, 1, 0), (CR, 6, 3), (RS, 0, 4),
    ),
    (AT_GUP, 0): (
        (RS, 1, 4), (RS, 0, 1),
    ),
    (AT_GUP, 2): (
        (RS, 1, 1),
    ),
    (AT_GUP, 3): (
        (RS, 0, 5),
    ),
    (AT_GIN, 1): (
        (RS, 1, 5),
    ),
    (AT_GIN, 2): (
        (RS, 0, 2),
    ),
    (AT_GIN, 3): (
        (RS, 1, 2),
    ),
    (AT_GNF, 0): (
        (XC, 0), (RS, 0, 6), (HALF, 1, 0),
    ),
    (AT_GNF, 1): (
        (RS, 1, 6), (HALF, 1, 1),
    ),
    (AT_GNF, 2): (
        (RS, 0, 3), (HALF, 1, 2),
    ),
    (AT_GNF, 3): (
        (RS, 1, 3), (SHARE_A, 0), (HALF, 1, 3), (GO, 1), (RS, 2, 0), (RS, 2, 4),
    ),
    (AT_NARROW, 0): (
        (RS, 3, 0),
    ),
    (AT_NARROW, 1): (
        (RS, 3, 4), (HALF, 2, 3), (GO, 5),
    ),
    (AT_NARROW, 2): (
        (RS, 4, 0),
    ),
    (AT_NARROW, 3): (
        (FSUM, 0), (RS, 4, 4),
    ),
    AT_LAY: (
        (RS, 2, 1),
    ),
    (AT_AB, 0): (
        (RS, 2, 5), (RS, 3, 1), (RS, 3, 5),
    ),
    (AT_AB, 1): (
        (RS, 9, 0), (RS, 9, 4), (RS, 4, 1), (RS, 4, 5), (RS, 2, 2),
    ),
    (AT_AB, 2): (
        (RS, 2, 6), (XC, 1), (RS, 3, 2), (RS, 3, 6), (HALF, 2, 0), (GO, 2), (RS, 9, 1),
    ),
    (AT_AB, 3): (
        (RS, 9, 5), (RS, 4, 2), (RS, 4, 6), (RS, 2, 3), (FIN_B, 0), (RS, 5, 0),
    ),
    (AT_AB, 4): (
        (RS, 5, 4), (RS, 3, 3), (RS, 6, 0), (HALF, 2, 1), (GO, 3), (RS, 6, 4),
    ),
    (AT_AB, 5): (
        (RS, 9, 2), (RS, 9, 6), (RS, 4, 3), (SHARE_A, 1), (RS, 5, 1), (RS, 5, 5),
    ),
    (AT_GN, 0): (
        (RS, 6, 1), (RS, 7, 0),
    ),
    (AT_GN, 1): (
        (RS, 7, 4), (RS, 6, 5), (HALF, 2, 2), (GO, 4),
    ),
    AT_GX: (
        (RS, 9, 3), (SHARE_A, 5), (RS, 5, 2),
    ),
    AT_TAIL: (
        (RS, 5, 6), (RS, 6, 2), (RS, 7, 1), (RS, 7, 5), (FSUM, 1), (RS, 6, 6), (RS, 8, 0), (HOP, 0), (RS, 8, 4),
        (RS, 5, 3), (FIN_B, 1), (RS, 6, 3), (SHARE_A, 2), (RS, 7, 2), (RS, 7, 6), (RS, 8, 1), (HOP, 1), (RS, 8, 5),
        (RS, 7, 3), (SHARE_A, 3), (RS, 8, 2), (RS, 8, 6), (FSUM, 5), (HOP, 2), (RS, 8, 3), (SHARE_A, 4), (FSUM, 2),
        (FSUM, 3), (FSUM, 4),
    ),
}

def dg(left, right, on_left, on_right):
    return lax.dot_general(
        left, right, (((on_left,), (on_right,)), ((), ())), preferred_element_type=F32
    )


def exact(left, right, on_left, on_right):
    return lax.dot_general(
        left, right, (((on_left,), (on_right,)), ((), ())), precision=HIGH, preferred_element_type=F32
    )


def ring_dp(place):
    high = place // 4
    return 2 * (place * (1 - high) + (7 - place) * high) + high


def times(start, size, step):
    return pl.ds(pl.multiple_of(start, step), size)


def band_bucket(n_buckets):
    lane = lax.broadcasted_iota(jnp.int32, (n_buckets, 512), 1)
    relative = jnp.where(lane < 384, lane - 128, lane - 640)
    row = lax.broadcasted_iota(jnp.int32, (n_buckets, 512), 0)
    return (bucket_index(relative, n_buckets, MAXDIST) == row).astype(F32)


def layer_kernel(
    x_hbm, cot_hbm, wq_hbm, wk_hbm, wv_hbm, wo_hbm, win_hbm, wff_hbm, lengths, attn_gain, ffn_gain, table,
    out_hbm, gx_hbm, gatt_hbm, gin_hbm, gff_hbm, pool_hbm, small_out,
    watt, win, wff, gin, gff, big, probs, xs, cot, normed, qkv, mixed, nf, hid, acc, band, diag, d_both,
    sib_ff, sib_in, y_ff, y_in, r_ffa, r_ffb, r_ina, r_inb, r_att, f_ff, f_in, f_att, sums, sums_in, spread, pool,
    ag_s, ag_r, sb_s, sb_r, yf_s, yf_r, yb_s, yb_r, rr_s, loc, a2_s, a2_r, hs_s, hs_r, yx_s, yx_r,
    fa_s, fa_r, fb_s, fb_r, fo_s, fo_r, fl, bf_s, bf_r,
):
    dp, sq = lax.axis_index("dp"), lax.axis_index("seq")
    z, x, y, c = dp // 2, dp % 2, sq // 2, sq % 2
    place = x * (7 - z) + (1 - x) * z
    turn = 1 - 2 * c

    def owner(steps):
        return ring_dp((place + steps * turn + 16) % 8)

    sib, yp, ysib = (dp, 2 * y + 1 - c), (dp, 2 * (1 - y) + c), (dp, 2 * (1 - y) + 1 - c)
    peers = (sib, yp, ysib)
    others = [((dp + k) % DP, sq) for k in range(1, DP)]

    def send(src, dst, ss, rs, dev):
        return pltpu.make_async_remote_copy(
            src_ref=src, dst_ref=dst, send_sem=ss, recv_sem=rs, device_id=dev, device_id_type=MESH_ID
        )

    def when(condition, body):
        if isinstance(condition, bool):
            if condition:
                body()
        else:
            pl.when(condition)(body)

    def loop(count, body):
        def step(i, _):
            body(i)
            return 0

        lax.fori_loop(0, count, step, 0)

    barrier = pltpu.get_barrier_semaphore()
    for dev in (*peers, *others):
        pl.semaphore_signal(barrier, inc=1, device_id=dev, device_id_type=MESH_ID)

    r96 = times(96 * dp, 96, 96)
    own = [pltpu.make_async_copy(w, watt.at[i, r96], loc.at[i]) for i, w in enumerate((wq_hbm, wk_hbm, wv_hbm, wo_hbm))]
    for i in range(2):
        own.append(pltpu.make_async_copy(win_hbm.at[pl.ds(48 * i, 48)], win.at[dp, i], loc.at[4 + i]))
    own.append(pltpu.make_async_copy(wff_hbm, wff.at[times(384 * dp, 384, 384)], loc.at[6]))
    mine = times(128 * sq, 128, 128)
    own.append(pltpu.make_async_copy(x_hbm.at[sq], xs.at[mine], loc.at[7]))
    own.append(pltpu.make_async_copy(cot_hbm.at[sq], cot.at[mine], loc.at[8]))
    for copy in own:
        copy.start()
    pl.semaphore_wait(barrier, len(peers) + len(others))

    def swap(k, src_hbm, dst, at):
        dev = peers[k]
        return send(src_hbm.at[dev[1]], dst.at[mine], a2_s.at[at], a2_r.at[at], dev)

    def three(ref, at):
        return send(ref, ref, a2_s.at[at], a2_r.at[at], sib)

    def swap_wait(dst, at):
        three(dst.at[pl.ds(0, 384)], at).wait_recv()

    for k in range(3):
        swap(k, x_hbm, xs, 0).start()

    def piece(ch, d, cc, yy):
        if ch < 3:
            cols = pl.ds(128 + 256 * ch, 256) if ch < 2 else times(640 * yy, 128, 128)
            return watt.at[0:3, times(96 * d + 48 * cc, 48, 48), cols]
        if ch < 5:
            cols = pl.ds(768, 1536) if ch == 3 else times(2304 * yy, 768, 768)
            return win.at[d, cc, :, cols]
        if ch == 7:
            return watt.at[3, times(96 * d + 48 * cc, 48, 48)]
        cols = pl.ds(256, 256) if ch == 5 else times(512 * yy, 256, 256)
        return wff.at[times(384 * d + 192 * cc, 192, 192), cols]

    crossing = (2, 4, 6)
    groups = ((0, 1, 2), (3, 4), (5, 6), (7,))

    def came_from(e):
        ahead = e // FAR
        return (1 - ahead) * (-e - 1) + ahead * (e - 3)

    def side(e):
        return (owner(1 - 2 * (e // FAR)), sq)

    def ring_send(ch, e):
        ahead = e // FAR
        part = piece(ch, owner((1 - ahead) * -e + ahead * (e - FAR)), c, y)
        return send(part, part, ag_s.at[ch], ag_r.at[ch, e], side(e))

    def hand_on(ch, e):
        part = piece(ch, owner(came_from(e)), c, y)
        return send(part, part, sb_s.at[ch], sb_r.at[ch], sib)

    def cross(ch, e):
        part = piece(ch, owner(came_from(e)), c, y)
        return send(part, part, yf_s.at[ch // 2 - 1], yf_r.at[ch // 2 - 1, e], yp)

    def cross_on(ch, e):
        part = piece(ch, owner(came_from(e)), c, 1 - y)
        return send(part, part, yb_s.at[ch // 2 - 1], yb_r.at[ch // 2 - 1], sib)

    def arrive(ch, e):
        part = piece(ch, owner(came_from(e)), c, y)
        send(part, part, ag_s.at[ch], ag_r.at[ch, e], side(e)).wait_recv()
        if e not in (FAR - 1, EVENTS - 1):
            ring_send(ch, e + 1).start()
        if ch in crossing:
            cross(ch, e).start()
        hand_on(ch, e).start()

    def arrive_cross(ch, e):
        part = piece(ch, owner(came_from(e)), c, 1 - y)
        send(part, part, yf_s.at[ch // 2 - 1], yf_r.at[ch // 2 - 1, e], yp).wait_recv()
        cross_on(ch, e).start()

    def seven(ch):
        if ch < 3:
            return watt.at[0:3, pl.ds(0, 336), pl.ds(0, 256 if ch < 2 else 128)]
        if ch < 5:
            return win.at[pl.ds(0, 7), 0, :, pl.ds(0, 1536 if ch == 3 else 768)]
        return watt.at[3, pl.ds(0, 336)] if ch == 7 else wff.at[pl.ds(0, 1344), pl.ds(0, 256)]

    def all_seven(ch, ss, rs, dev):
        return send(seven(ch), seven(ch), ss, rs, dev)

    def settled(group):
        for ch in groups[group]:
            all_seven(ch, sb_s.at[ch], sb_r.at[ch], sib).wait_recv()
            if ch in crossing:
                all_seven(ch, yb_s.at[group], yb_r.at[group], sib).wait_recv()

    def gather_sent(group):
        for ch in groups[group]:
            all_seven(ch, ag_s.at[ch], ag_r.at[ch, 0], sib).wait_send()
            all_seven(ch, sb_s.at[ch], sb_r.at[ch], sib).wait_send()
            if ch in crossing:
                all_seven(ch, yf_s.at[group], yf_r.at[group, 0], yp).wait_send()
                all_seven(ch, yb_s.at[group], yb_r.at[group], sib).wait_send()

    def begin(group):
        for ch in reversed(groups[group]):
            ring_send(ch, 0).start()
            ring_send(ch, FAR).start()

    acts = {AG: arrive, CR: arrive_cross, BEGIN: begin}

    def serve(slot):
        for name, *place in PLAN.get(slot, ()):
            acts[name](*place)

    def serve_at(slot, count, i):
        for k in range(count):
            if (slot, k) in PLAN:

                @pl.when(i == k)
                def _(k=k):
                    serve((slot, k))

    for i in range(4):
        own[i].wait()
    begin(0)

    band[pl.ds(0, HEAD_N), :] = exact(table[...], band_bucket(32), 1, 0)
    gain_a = attn_gain[...].reshape(1, WIDTH)
    gain_f = ffn_gain[...].reshape(1, WIDTH)

    serve(AT_A1)
    own[7].wait()
    swap_wait(xs, 0)
    for i in range(4, 7):
        own[i].wait()

    def norm_rows(b):
        rows = times(128 * b, 128, 128)
        v = xs[rows, :].astype(F32)
        s = lax.rsqrt(jnp.mean(v * v, axis=-1, keepdims=True) + EPS)
        normed[rows, :] = (v * s * gain_a).astype(BF)

    loop(4, norm_rows)

    serve(AT_NORM)
    serve(AT_ATT)
    settled(0)
    for k in range(3):
        swap(k, cot_hbm, cot, 1).start()

    def project(m):
        qkv[m] = dg(normed[...], watt[m], 1, 0).astype(BF)
        serve_at(AT_PROJECT, 3, m)

    loop(3, project)

    count = lengths[sq]
    valid = lax.broadcasted_iota(jnp.int32, (1, TOKENS), 1) < count
    lane = lax.broadcasted_iota(jnp.int32, (1, 128), 1)
    keep = (lane < 64, lane >= 64)

    def only(h, v):
        return jnp.where(keep[h], v, jnp.zeros_like(v))

    def attend(hp):
        cols = times(128 * hp, 128, 128)
        key, value = qkv[1, :, cols], qkv[2, :, cols]
        total = [None] * 4
        for h in range(2):
            row = band[pl.ds(2 * hp + h, 1), :]
            tilted = pltpu.roll(jnp.broadcast_to(row, (128, 512)), 0, 1, stride=1, stride_axis=0)
            before = jnp.broadcast_to(row[:, 384:], (128, 128))
            after = jnp.broadcast_to(row[:, 256:384], (128, 128))
            value_h = only(h, value)
            for ib in range(4):
                rows = pl.ds(128 * ib, 128)
                blocks = []
                for jb in range(4):
                    off = jb - ib
                    if off < -1:
                        blocks.append(before)
                    elif off > 1:
                        blocks.append(after)
                    else:
                        blocks.append(tilted[:, 128 * (off + 1) : 128 * (off + 2)])
                scores = dg(only(h, qkv[0, rows, cols]), key, 1, 1) + jnp.concatenate(blocks, axis=1)
                scores = jnp.where(valid, scores, FLOOR)
                top = jnp.max(scores, axis=-1, keepdims=True)
                expo = jnp.exp(scores - top)
                part = jnp.sum(expo, axis=-1, keepdims=True)
                low = (expo * (1.0 / part)).astype(BF)
                probs[2 * hp + h, rows, :] = low
                one = dg(low, value_h, 1, 0)
                total[ib] = one if h == 0 else total[ib] + one
        for ib in range(4):
            mixed[pl.ds(128 * ib, 128), cols] = total[ib].astype(BF)
        serve_at(AT_ATTEND, PAIRS, hp)

    loop(PAIRS, attend)
    serve(AT_WO)
    settled(3)

    def residual(b):
        rows = times(256 * b, 256, 256)
        v = xs[rows, :].astype(F32) + dg(mixed[rows, :], watt[3], 1, 0)
        hid[rows, :] = v
        s = lax.rsqrt(jnp.mean(v * v, axis=-1, keepdims=True) + EPS)
        nf[rows, :] = (v * s * gain_f).astype(BF)
        serve_at(AT_RESIDUAL, 2, b)

    loop(2, residual)

    serve(AT_IN)
    settled(1)
    up_rows, down_rows = pl.ds(0, TOKENS), pl.ds(TOKENS, TOKENS)

    def block(j):
        return times(768 * j, 768, 768)

    def win_block(j):
        return win[:, :, :, block(j)].reshape(768, 768)

    def widen(j):
        v = dg(nf[...], win_block(j), 1, 0)
        sq_v = v * v
        t = jnp.tanh(v * (GELU_A + (GELU_A * GELU_B) * sq_v))
        half = 0.5 + 0.5 * t
        big[j, up_rows, :] = (v * half).astype(BF)
        slope = half + (v * half) * (1.0 - t) * (GELU_A + (3 * GELU_A * GELU_B) * sq_v)
        big[j, down_rows, :] = slope.astype(BF)
        serve_at(AT_WIDEN, 4, j)

    loop(4, widen)
    serve(AT_COTW)
    own[8].wait()
    swap_wait(cot, 1)

    def chunk(i):
        return (3 - z + (i + 1) // 2 + 2 * (i % 2) * (1 - i // 2)) % 4

    def half_ff(i):
        two = pl.ds(2 * chunk(i), 2)
        src = gff.at[two, times(192 * (1 - c), 192, 192)]
        return send(src, sib_ff.at[two], hs_s.at[0], hs_r.at[0, i], sib)

    def grad_ff(i):
        j = chunk(i)
        v = dg(big[j, up_rows, :], cot[...], 0, 0).astype(BF)
        gff[pl.ds(2 * j, 2)] = v.reshape(2, 384, 768)
        half_ff(i).start()
        serve_at(AT_GFF, 4, i)


    def merge_ff(i):
        j = chunk(i)
        half_ff(i).wait_recv()
        rows = times(192 * c, 192, 192)
        for i in range(2):
            gff[2 * j + i, rows] = (gff[2 * j + i, rows].astype(F32) + sib_ff[2 * j + i].astype(F32)).astype(BF)

    def cross_src(g, yy):
        if g == 0:
            return gff.at[:, times(192 * c + 160 * yy, 32, 32)]
        return gin.at[:, times(1536 * c + 1280 * yy, 256, 256)]

    cross_dst = (y_ff, y_in)

    def cross_sum(g):
        return send(cross_src(g, 1 - y), cross_dst[g], yx_s.at[g], yx_r.at[g], yp)

    def add_cross(g):
        cross_sum(g).wait()
        here, came = cross_src(g, y), cross_dst[g]
        here[...] = (here[...].astype(F32) + came[...].astype(F32)).astype(BF)

    def rs_piece(ch, d, yy):
        if ch < 3:
            rows = times(192 * c + 32 + 64 * ch, 64, 32) if ch < 2 else times(192 * c + 160 * yy, 32, 32)
            return gff.at[d, rows]
        if ch < 5:
            return gin.at[times(96 * d, 96, 96), times(1536 * c + 256 + 512 * (ch - 3), 512, 256)]
        if ch == 5:
            return gin.at[times(96 * d, 96, 96), times(1536 * c + 1280 * yy, 256, 256)]
        return win.at[d, c, :, pl.ds(768 * (ch - 6), 768)]

    landing = [r_ffa.at[0], r_ffa.at[1], r_ffb, r_ina.at[0], r_ina.at[1], r_inb, r_att.at[0]]
    landing += [r_ffa.at[0, :, pl.ds(0, 48)], r_ffa.at[1, :, pl.ds(0, 48)], r_att.at[1]]

    def rs_send(ch, e):
        ahead = e // FAR
        part = rs_piece(ch, owner((1 - ahead) * (FAR - e) + ahead * (e - EVENTS)), y)
        return send(part, landing[ch].at[e], rr_s.at[ch], ag_r.at[ch, e], side(e))

    def rs_begin(ch):
        rs_send(ch, 0).start()
        rs_send(ch, FAR).start()

    def rs_event(ch, e):
        rs_send(ch, e).wait_recv()
        here = rs_piece(ch, owner(FAR - 1 - e if e < FAR else e - EVENTS + 1), y)
        here[...] = (here[...].astype(F32) + landing[ch][e].astype(F32)).astype(BF)
        if e not in (FAR - 1, EVENTS - 1):
            rs_send(ch, e + 1).start()

    def half_in(k):
        src = gin.at[:, times(1536 * (1 - c) + 384 * k, 384, 384)]
        return send(src, sib_in.at[k], hs_s.at[1], hs_r.at[1, k], sib)

    def merge_in(k):
        half_in(k).wait_recv()
        cols = times(1536 * c + 384 * k, 384, 384)
        gin[:, cols] = (gin[:, cols].astype(F32) + sib_in[k].astype(F32)).astype(BF)

    def sib_rows(t):
        return sib_ff.at[:, times(48 * t, 48, 48)]

    def half_att(t):
        return send(win.at[:, 1 - c, :, block(t)], sib_rows(t), hs_s.at[2], hs_r.at[2, t], sib)

    def merge_att(t):
        half_att(t).wait_recv()
        win[:, c, :, block(t)] = (win[:, c, :, block(t)].astype(F32) + sib_rows(t)[...].astype(F32)).astype(BF)

    final = [f_ff, f_in] + [f_att.at[t] for t in range(4)]

    def own_piece(g):
        if g == 0:
            return gff.at[dp, times(192 * c + 32, 128, 32)]
        if g == 1:
            return gin.at[r96, times(1536 * c + 256, 1024, 256)]
        return rs_piece(4 + g, dp, y)

    def out_piece(g, cc, yy):
        if g == 0:
            return gff_hbm.at[times(192 * cc + 32, 128, 32) if yy is None else times(192 * cc + 160 * yy, 32, 32)]
        if g == 1:
            if yy is None:
                return gin_hbm.at[:, times(1536 * cc + 256, 1024, 256)]
            return gin_hbm.at[:, times(1536 * cc + 1280 * yy, 256, 256)]
        return gatt_hbm.at[g - 2, times(48 * cc, 48, 48)]

    def share_a(g):
        return send(own_piece(g), final[g], fa_s.at[g], fa_r.at[g], yp)

    def share_b(g, k):
        return send(rs_piece(3 * g + 2, dp, y), out_piece(g, c, y), fb_s.at[g], fb_r.at[g], peers[k])

    def share_sum(g):
        return send(final[g], out_piece(g, c, None), fo_s.at[g], fo_r.at[g], sib)

    def keep_b(g):
        return pltpu.make_async_copy(rs_piece(3 * g + 2, dp, y), out_piece(g, c, y), fl.at[g, 0])

    def keep_sum(g):
        return pltpu.make_async_copy(final[g], out_piece(g, c, None), fl.at[g, 1])

    def finish_b(g):
        for k in range(3):
            share_b(g, k).start()
        keep_b(g).start()

    def finish_sum(g):
        share_a(g).wait()
        final[g][...] = (final[g][...].astype(F32) + own_piece(g)[...].astype(F32)).astype(BF)
        share_sum(g).start()
        keep_sum(g).start()

    def hop(k):
        return send(sums.at[k], sums_in.at[k], bf_s.at[k], bf_r.at[k], (yp, sib)[k])

    def hop_on(k):
        if k < 2:
            hop(k).wait()
            sums[k + 1] = sums[k] + sums_in[k]
        if k == 0:
            hop(1).start()
        elif k == 1:
            for dev in others:
                send(sums.at[2], spread.at[dp], bf_s.at[2], bf_r.at[2], dev).start()
            spread[dp] = sums[2]
        else:
            send(spread.at[pl.ds(0, 7)], spread.at[pl.ds(0, 7)], bf_s.at[2], bf_r.at[2], sib).wait()
            total = spread[0]
            for k in range(1, DP):
                total = total + spread[k]
            small_out[...] = total

    def merge(g, k):
        (merge_ff, merge_in, merge_att)[g](k)

    def go(g):
        if g == 0:
            cross_sum(0).start()
        elif g == 1:
            cross_sum(1).start()
            rs_begin(3)
            rs_begin(4)
        else:
            rs_begin(4 + g)

    def leave(e):
        for ch in range(2):
            rs_send(ch, e).start()

    def cross_in(g):
        add_cross(g)
        rs_begin(3 * g + 2)

    acts |= {
        RS: rs_event, HALF: merge, GO: go, LEAVE: leave, XC: cross_in, SHARE_A: lambda g: share_a(g).start(), FIN_B: finish_b,
        FSUM: finish_sum, HOP: hop_on,
    }

    loop(4, grad_ff)
    serve(AT_MFF)
    serve(AT_FF)
    settled(2)

    def grad_up(j):
        v = dg(cot[...], wff[block(j), :], 1, 1) * big[j, down_rows, :].astype(F32)
        big[j, down_rows, :] = v.astype(BF)
        serve_at(AT_GUP, 4, j)

    loop(4, grad_up)

    def grad_in(i):
        j = (2 * (1 - c) + i) % 4
        gin[:, block(j)] = dg(nf[...], big[j, down_rows, :], 0, 0).astype(BF)

        @pl.when(i == 1)
        def _():
            for k in range(4):
                half_in(k).start()

        serve_at(AT_GIN, 4, i)

    loop(4, grad_in)

    acc[...] = jnp.zeros_like(acc)

    def grad_nf(j):
        acc[...] += dg(big[j, down_rows, :], win_block(j), 1, 1)
        serve_at(AT_GNF, 4, j)

    loop(4, grad_nf)

    def norm_back(v, gain, grad):
        s = lax.rsqrt(jnp.mean(v * v, axis=-1, keepdims=True) + EPS)
        scaled = grad * gain
        back = s * scaled - v * (s * s * s) * jnp.mean(v * scaled, axis=-1, keepdims=True)
        return back, jnp.sum(grad * v * s, axis=0, keepdims=True)

    def ffn_norm_back(b, total):
        rows = times(128 * b, 128, 128)
        v = hid[rows, :]
        back, part = norm_back(v, gain_f, acc[rows, :])
        grad = cot[rows, :].astype(F32) + back
        acc[rows, :] = grad
        cot[rows, :] = grad.astype(BF)
        return total + part

    g_ffn_gain = lax.fori_loop(0, 4, ffn_norm_back, jnp.zeros((1, WIDTH), F32))

    serve(AT_FNORM)
    serve(AT_PREWO)
    gather_sent(1)
    win[:, :, :, block(3)] = dg(mixed[...], cot[...], 0, 0).astype(BF).reshape(8, 2, 48, 768)

    half_att(3).start()
    serve(AT_GWO)
    nf[...] = dg(cot[...], watt[3], 1, 1).astype(BF)
    serve(AT_GMIX)


    def give(src, dst_hbm, at, k):
        dev = peers[k]
        return send(src.at[times(128 * dev[1], 128, 128)], dst_hbm.at[sq], a2_s.at[at], a2_r.at[at], dev)

    def pool_send(k):
        return send(pool, pool_hbm.at[sq], a2_s.at[4], a2_r.at[4], peers[k])

    pool_own = pltpu.make_async_copy(pool, pool_hbm.at[sq], loc.at[2])
    lay = big.at[0, up_rows]
    lay_own = pltpu.make_async_copy(lay.at[mine], out_hbm.at[sq], loc.at[1])
    def narrow(j):
        part = dg(big[j, up_rows, :], wff[block(j), :], 1, 0)
        hid[...] += part
        serve_at(AT_NARROW, 4, j)

    loop(4, narrow)
    lay[...] = hid[...].astype(BF)
    for k in range(3):
        give(lay, out_hbm, 2, k).start()
    lay_own.start()
    here_t = lax.broadcasted_iota(jnp.int32, (TOKENS, 1), 0) < count
    mean = jnp.sum(jnp.where(here_t, hid[...], 0.0), axis=0, keepdims=True) / count.astype(F32)
    pool[...] = jnp.broadcast_to(mean, (8, WIDTH))
    pool_own.start()
    for k in range(3):
        pool_send(k).start()
    serve(AT_LAY)

    flip_sum = lax.broadcasted_iota(jnp.int32, (128, 128), 0) + lax.broadcasted_iota(jnp.int32, (128, 128), 1)
    flip = (flip_sum == 127).astype(F32).astype(BF)

    def flipped(v):
        high = v.astype(BF)
        return dg(flip, high, 1, 0) + dg(flip, (v - high.astype(F32)).astype(BF), 1, 0)

    def attend_back(hp):
        cols = times(128 * hp, 128, 128)
        key, value = qkv[1, :, cols], qkv[2, :, cols]
        query, grad = qkv[0, :, cols], nf[:, cols]
        g_query = [None] * 4
        for h in range(2):
            key_h = only(h, key)
            before = after = jnp.zeros((128, 128), F32)
            near = [jnp.zeros((128, 128), F32) for _ in range(3)]
            for ib in range(4):
                rows = pl.ds(128 * ib, 128)
                wide = probs[2 * hp + h, rows, :].astype(F32)
                d_probs = dg(only(h, nf[rows, cols]), value, 1, 1)
                mean_d = jnp.sum(wide * d_probs, axis=-1, keepdims=True)
                d_score = wide * (d_probs - mean_d)
                for jb in range(4):
                    off, part = jb - ib, d_score[:, 128 * jb : 128 * (jb + 1)]
                    if off < -1:
                        before = before + part
                    elif off > 1:
                        after = after + part
                    else:
                        near[off + 1] = near[off + 1] + part
                d_low = d_score.astype(BF)
                d_both[pl.ds(512 * h + 128 * ib, 128), :] = d_low
                one = dg(d_low, key_h, 1, 0)
                g_query[ib] = one if h == 0 else g_query[ib] + one
            tilted = flipped(jnp.concatenate(near, axis=1))
            tilted = jnp.concatenate([tilted, jnp.zeros((128, 128), F32)], axis=1)
            flat = jnp.sum(pltpu.roll(tilted, 385, 1, stride=1, stride_axis=0), axis=0, keepdims=True)
            far = jnp.concatenate(
                [
                    jnp.zeros((1, 256), F32),
                    jnp.sum(after, axis=0, keepdims=True),
                    jnp.sum(before, axis=0, keepdims=True),
                ],
                axis=1,
            )
            diag[pl.ds(2 * hp + h, 1), :] = flat + far
        both_query = jnp.concatenate([only(0, query), only(1, query)], axis=0)
        both_grad = jnp.concatenate([only(0, grad), only(1, grad)], axis=0)
        qkv[1, :, cols] = dg(d_both[...], both_query, 0, 0).astype(BF)
        qkv[2, :, cols] = dg(probs[pl.ds(2 * hp, 2)].reshape(1024, 512), both_grad, 0, 0).astype(BF)
        for ib in range(4):
            qkv[0, pl.ds(128 * ib, 128), cols] = g_query[ib].astype(BF)

        @pl.when(hp % 2 == 1)
        def _():
            t = hp // 2
            three = times(256 * t, 256, 256)
            grads = jnp.concatenate([qkv[0, :, three], qkv[1, :, three], qkv[2, :, three]], axis=1)
            win[:, :, :, block(t)] = dg(normed[...], grads, 0, 0).astype(BF).reshape(8, 2, 48, 768)
            half_att(t).start()

        serve_at(AT_AB, PAIRS, hp)

    loop(PAIRS, attend_back)
    def attn_norm_back(b, total):
        rows = times(256 * b, 256, 256)
        grad = dg(qkv[0, rows, :], watt[0], 1, 1) + dg(qkv[1, rows, :], watt[1], 1, 1) + dg(qkv[2, rows, :], watt[2], 1, 1)
        back, part = norm_back(xs[rows, :].astype(F32), gain_a, grad)
        mixed[rows, :] = (acc[rows, :] + back).astype(BF)
        serve_at(AT_GN, 2, b)
        return total + part

    g_attn_gain = lax.fori_loop(0, 2, attn_norm_back, jnp.zeros((1, WIDTH), F32))

    sums[0] = jnp.zeros((32, 128), F32)
    sums[0, 0:16, 0:32] = exact(diag[...], band_bucket(32), 1, 1)
    for k in range(6):
        sums[0, 16 + k : 17 + k, :] = g_attn_gain[:, 128 * k : 128 * (k + 1)]
        sums[0, 22 + k : 23 + k, :] = g_ffn_gain[:, 128 * k : 128 * (k + 1)]

    hop(0).start()
    for k in range(3):
        give(mixed, gx_hbm, 3, k).start()
    gx_own = pltpu.make_async_copy(mixed.at[mine], gx_hbm.at[sq], loc.at[0])
    gx_own.start()
    serve(AT_GX)
    serve(AT_TAIL)

    for g in range(6):
        if g < 2:
            keep_b(g).wait()
            same = (sib_ff.at[pl.ds(0, 3), pl.ds(0, 32)], gin.at[pl.ds(0, 288), pl.ds(0, 256)])[g]
            send(same, same, fb_s.at[g], fb_r.at[g], sib).wait()
        keep_sum(g).wait()
        share_sum(g).wait_send()
        came = out_piece(g, 1 - c, None)
        send(came, came, fo_s.at[g], fo_r.at[g], sib).wait_recv()
    for ch in range(10):
        send(landing[ch], landing[ch], rr_s.at[ch], ag_r.at[ch, 0], sib).wait_send()
    for g, same in enumerate((sib_ff, sib_in, sib_ff)):
        send(same, same, hs_s.at[g], hs_r.at[g, 0], sib).wait_send()
    gather_sent(0)
    gather_sent(2)
    gather_sent(3)
    three(out_hbm.at[pl.ds(0, 3)], 2).wait()
    three(gx_hbm.at[pl.ds(0, 3)], 3).wait()
    three(pool_hbm.at[pl.ds(0, 3)], 4).wait()
    three(xs.at[pl.ds(0, 384)], 0).wait_send()
    three(cot.at[pl.ds(0, 384)], 1).wait_send()
    lay_own.wait()
    gx_own.wait()
    pool_own.wait()


def finish_kernel(
    out_in, gx_in, att_in, in_in, ff_in, pool_in, small_in,
    out, gx, pool_out, gain_a, gq, gk, gv, go, g_table, gain_f, gin_out, gff_out,
    v_out, v_gx, v_att, v_in, v_ff, v_pool, w_att, w_in, w_ff, w_pool, sem_in, sem_out,
):
    sources = (in_in, ff_in, att_in, pool_in, out_in, gx_in)
    held = (v_in, v_ff, v_att, v_pool, v_out, v_gx)
    reads = [pltpu.make_async_copy(a, b, sem_in.at[k]) for k, (a, b) in enumerate(zip(sources, held))]
    for read in reads:
        read.start()
    g_table[...] = small_in[0:HEAD_N, 0:32]
    for k in range(6):
        gain_a[128 * k : 128 * (k + 1)] = small_in[16 + k : 17 + k, :].reshape(128)
        gain_f[128 * k : 128 * (k + 1)] = small_in[22 + k : 23 + k, :].reshape(128)
    writes = []

    def write(src, dst):
        writes.append(pltpu.make_async_copy(src, dst, sem_out.at[len(writes)]))
        writes[-1].start()

    reads[0].wait()
    w_in[...] = v_in[...].astype(F32)
    write(w_in, gin_out)
    reads[1].wait()
    w_ff[...] = v_ff[...].astype(F32)
    write(w_ff, gff_out)
    reads[2].wait()
    w_att[3] = v_att[3].astype(F32)
    for t in range(3):
        for i in range(3):
            w_att[i, :, 256 * t : 256 * (t + 1)] = v_att[t, :, 256 * i : 256 * (i + 1)].astype(F32)
    for i, ref in enumerate((gq, gk, gv, go)):
        write(w_att.at[i], ref)
    reads[3].wait()
    for p in range(SEQ):
        w_pool[p : p + 1, :] = v_pool[p, 0:1, :]
    write(w_pool, pool_out)
    reads[4].wait()
    write(v_out, out)
    reads[5].wait()
    write(v_gx, gx)
    for copy in writes:
        copy.wait()


def passage_shards(
    passages, lengths, attn_gain, w_query, w_key, w_value, w_attn_out, bias_table, ffn_gain, w_in, w_ff_out, cotangent
):
    any_space = pl.BlockSpec(memory_space=pl.ANY)
    vmem = pl.BlockSpec(memory_space=pltpu.VMEM)
    dma = pltpu.SemaphoreType.DMA
    scratch = [
        pltpu.VMEM(shape, BF)
        for shape in (
            (4, 768, 768), (8, 2, 48, 3072), (3072, 768), (768, 3072), (8, 384, 768), (4, 1024, 768), (12, 512, 512),
            (512, 768), (512, 768), (512, 768), (3, 512, 768), (512, 768), (512, 768),
        )
    ]
    scratch += [pltpu.VMEM(shape, F32) for shape in ((512, 768), (512, 768), (16, 512), (16, 512))]
    scratch += [
        pltpu.VMEM(shape, BF)
        for shape in (
            (1024, 512), (8, 192, 768), (4, 768, 384), (8, 32, 768), (768, 256),
            (2, 7, 64, 768), (7, 32, 768), (2, 7, 96, 512), (7, 96, 256), (2, 7, 48, 768),
            (128, 768), (96, 1024), (4, 48, 768),
        )
    ]
    scratch += [pltpu.VMEM((n, 32, 128), F32) for n in (3, 2, DP)]
    scratch.append(pltpu.VMEM((8, 768), F32))
    scratch += [
        dma(shape)
        for shape in (
            (8,), (10, 7), (8,), (8,), (3,), (3, 7), (3,), (3,), (10,), (9,), (5,), (5,), (3,), (3, 4), (2,), (2,),
            (6,), (6,), (2,), (2,), (6,), (6,), (6, 2), (3,), (3,),
        )
    ]
    sums = pl.pallas_call(
        layer_kernel,
        out_shape=(
            jax.ShapeDtypeStruct((4, 128, 768), BF),
            jax.ShapeDtypeStruct((4, 128, 768), BF),
            jax.ShapeDtypeStruct((4, 96, 768), BF),
            jax.ShapeDtypeStruct((96, 3072), BF),
            jax.ShapeDtypeStruct((384, 768), BF),
            jax.ShapeDtypeStruct((4, 8, 768), F32),
            jax.ShapeDtypeStruct((32, 128), F32),
        ),
        in_specs=[any_space] * 8 + [pl.BlockSpec(memory_space=pltpu.SMEM)] + [vmem] * 3,
        out_specs=(any_space,) * 6 + (vmem,),
        scratch_shapes=scratch,
        compiler_params=pltpu.CompilerParams(collective_id=0, has_side_effects=True, vmem_limit_bytes=64 * 2**20),
        name="layer",
    )(
        passages, cotangent, w_query, w_key, w_value, w_attn_out, w_in, w_ff_out, lengths,
        attn_gain, ffn_gain, bias_table.T,
    )
    square = jax.ShapeDtypeStruct((96, 768), F32)
    gain = jax.ShapeDtypeStruct((WIDTH,), F32)
    outs = pl.pallas_call(
        finish_kernel,
        out_shape=(
            jax.ShapeDtypeStruct((4, 128, 768), BF),
            jax.ShapeDtypeStruct((4, 128, 768), BF),
            jax.ShapeDtypeStruct((4, 768), F32),
            gain,
            square,
            square,
            square,
            square,
            jax.ShapeDtypeStruct((HEAD_N, 32), F32),
            gain,
            jax.ShapeDtypeStruct((96, 3072), F32),
            jax.ShapeDtypeStruct((384, 768), F32),
        ),
        in_specs=[any_space] * 6 + [vmem],
        out_specs=(any_space,) * 3 + (vmem,) + (any_space,) * 4 + (vmem,) * 2 + (any_space,) * 2,
        scratch_shapes=[
            pltpu.VMEM((4, 128, 768), BF),
            pltpu.VMEM((4, 128, 768), BF),
            pltpu.VMEM((4, 96, 768), BF),
            pltpu.VMEM((96, 3072), BF),
            pltpu.VMEM((384, 768), BF),
            pltpu.VMEM((4, 8, 768), F32),
            pltpu.VMEM((4, 96, 768), F32),
            pltpu.VMEM((96, 3072), F32),
            pltpu.VMEM((384, 768), F32),
            pltpu.VMEM((4, 768), F32),
            dma((6,)),
            dma((9,)),
        ],
        compiler_params=pltpu.CompilerParams(vmem_limit_bytes=64 * 2**20),
        name="finish",
    )(*sums)
    return (outs[0], outs[2], outs[1], *outs[3:8], outs[8].T, *outs[9:])


def solution(mesh):
    ring = (mesh.shape["dp"], mesh.shape["seq"]) == (DP, SEQ)
    return jax.shard_map(
        passage_shards if ring else shards,
        mesh=mesh,
        in_specs=(
            P("dp", "seq", None),
            P("dp"),
            P(),
            P("dp", None),
            P("dp", None),
            P("dp", None),
            P("dp", None),
            P(),
            P(),
            P("dp", None),
            P("dp", None),
            P("dp", "seq", None),
        ),
        out_specs=(
            P("dp", "seq", None),
            P("dp", None),
            P("dp", "seq", None),
            P(),
            P("dp", None),
            P("dp", None),
            P("dp", None),
            P("dp", None),
            P(),
            P(),
            P("dp", None),
            P("dp", None),
        ),
        check_vma=False,
    )
```

```python
import math

import jax
import jax.numpy as jnp
from jax import lax
from jax.experimental import pallas as pl
from jax.experimental.pallas import tpu as pltpu
from jax.sharding import PartitionSpec as P

MAXDIST = 128


EPS = 1e-06
HIGH = lax.Precision.HIGHEST
FLOOR = -1e30


def bucket_index(relative, buckets, reach):
    half_count = buckets // 2
    exact_count = half_count // 2
    distance = jnp.abs(relative)
    result = jnp.minimum(distance, exact_count)
    for power in range(1, half_count - exact_count):
        bound_at = math.ceil(
            exact_count * (reach / exact_count) ** (power / (half_count - exact_count)) - 1e-06
        )
        result = result + (distance >= bound_at).astype(jnp.int32)
    return result + (relative > 0).astype(jnp.int32) * half_count


def rms_norm(values, gain_vec):
    return values * lax.rsqrt(jnp.mean(values * values, axis=-1, keepdims=True) + EPS) * gain_vec


def attend_forward(query_four, key_four, value_four, bias_rows, key_valid):
    scores = (
        jnp.einsum("pqhe,pkhe->phqk", query_four, key_four, preferred_element_type=jnp.float32)
        + bias_rows[None]
    )
    scores = jnp.where(key_valid[:, None, None, :], scores, FLOOR)
    row_top = jnp.max(scores, axis=-1, keepdims=True)
    expo = jnp.exp(scores - row_top)
    row_total = jnp.sum(expo, axis=-1, keepdims=True)
    log_total = row_top + jnp.log(row_total)
    attn_probs = (expo / row_total).astype(jnp.bfloat16)
    mixed_rows = jnp.einsum(
        "phqk,pkhe->pqhe", attn_probs, value_four, preferred_element_type=jnp.float32
    )
    return (mixed_rows.astype(jnp.bfloat16), log_total)


def attend_backward(query_four, key_four, value_four, grad_mixed, log_total, key_valid, bias_rows):

    def one_passage(score_sum, pieces):
        query_p, key_p, value_p, grad_p, log_p, valid_p = pieces
        score_p = (
            jnp.einsum("qhe,khe->hqk", query_p, key_p, preferred_element_type=jnp.float32)
            + bias_rows
        )
        score_p = jnp.where(valid_p[None, None, :], score_p, FLOOR)
        prob_p = jnp.exp(score_p - log_p)
        grad_prob = jnp.einsum("qhe,khe->hqk", grad_p, value_p, preferred_element_type=jnp.float32)
        grad_score = (
            prob_p * (grad_prob - jnp.sum(prob_p * grad_prob, axis=-1, keepdims=True))
        ).astype(jnp.bfloat16)
        grad_query_p = jnp.einsum(
            "hqk,khe->qhe", grad_score, key_p, preferred_element_type=jnp.float32
        ).astype(jnp.bfloat16)
        grad_key_p = jnp.einsum(
            "hqk,qhe->khe", grad_score, query_p, preferred_element_type=jnp.float32
        )
        grad_value_p = jnp.einsum(
            "hqk,qhe->khe", prob_p.astype(jnp.bfloat16), grad_p, preferred_element_type=jnp.float32
        )
        return (
            score_sum + grad_score.astype(jnp.float32),
            (grad_query_p, grad_key_p, grad_value_p),
        )

    start_sum = jnp.zeros(bias_rows.shape, jnp.float32)
    return lax.scan(
        one_passage, start_sum, (query_four, key_four, value_four, grad_mixed, log_total, key_valid)
    )


def shards(
    passages,
    lengths,
    attn_gain,
    w_query,
    w_key,
    w_value,
    w_attn_out,
    bias_table,
    ffn_gain,
    w_in,
    w_ff_out,
    cotangent,
):
    n_pass, local_rows, width = passages.shape
    n_buckets, n_heads = bias_table.shape
    head_dim = width // n_heads
    seq_count = lax.axis_size("seq")
    full_len = local_rows * seq_count
    row_count = n_pass * local_rows
    first_row = lax.axis_index("seq") * local_rows
    gathered = (
        lax.all_gather(w_query, "dp", axis=0, tiled=True),
        lax.all_gather(w_key, "dp", axis=0, tiled=True),
        lax.all_gather(w_value, "dp", axis=0, tiled=True),
        lax.all_gather(w_attn_out, "dp", axis=0, tiled=True),
        lax.all_gather(w_in, "dp", axis=0, tiled=True),
        lax.all_gather(w_ff_out, "dp", axis=0, tiled=True),
    )
    wq_full, wk_full, wv_full, wo_full, win_full, wff_full = gathered
    key_pos = jnp.arange(full_len, dtype=jnp.int32)
    query_pos = first_row + jnp.arange(local_rows, dtype=jnp.int32)
    key_valid = key_pos[None, :] < lengths[:, None]
    query_valid = query_pos[None, :] < lengths[:, None]
    inputs = passages.astype(jnp.float32).reshape(row_count, width)
    normed = rms_norm(inputs, attn_gain).astype(jnp.bfloat16)
    query_rows = jnp.dot(normed, wq_full, preferred_element_type=jnp.float32).astype(jnp.bfloat16)
    key_rows = jnp.dot(normed, wk_full, preferred_element_type=jnp.float32).astype(jnp.bfloat16)
    value_rows = jnp.dot(normed, wv_full, preferred_element_type=jnp.float32).astype(jnp.bfloat16)
    query_local = query_rows.reshape(n_pass, local_rows, n_heads, head_dim)
    relative = key_pos[None, :] - query_pos[:, None]
    one_hot = (
        bucket_index(relative, n_buckets, MAXDIST)[:, :, None]
        == jnp.arange(n_buckets, dtype=jnp.int32)
    ).astype(jnp.float32)
    bias_rows = jnp.einsum("qkb,bh->hqk", one_hot, bias_table, precision=HIGH)
    key_all, value_all = (
        lax.all_gather(key_rows.reshape(n_pass, local_rows, width), "seq", axis=1, tiled=True),
        lax.all_gather(value_rows.reshape(n_pass, local_rows, width), "seq", axis=1, tiled=True),
    )
    key_four = key_all.reshape(n_pass, full_len, n_heads, head_dim)
    value_four = value_all.reshape(n_pass, full_len, n_heads, head_dim)
    mixed_four, log_total = attend_forward(query_local, key_four, value_four, bias_rows, key_valid)
    mixed_rows = mixed_four.reshape(row_count, width)
    hidden = inputs + jnp.dot(mixed_rows, wo_full, preferred_element_type=jnp.float32)
    normed_ffn = rms_norm(hidden, ffn_gain).astype(jnp.bfloat16)
    up_rows = jnp.dot(normed_ffn, win_full, preferred_element_type=jnp.float32)
    activated = jax.nn.gelu(up_rows).astype(jnp.bfloat16)
    output_rows = hidden + jnp.dot(activated, wff_full, preferred_element_type=jnp.float32)
    pool_part = jnp.sum(
        output_rows.reshape(n_pass, local_rows, width)
        * query_valid[:, :, None].astype(jnp.float32),
        axis=1,
    )
    pooled = lax.psum(pool_part, "seq") / lengths[:, None].astype(jnp.float32)
    gathered = (
        lax.all_gather(w_query, "dp", axis=0, tiled=True),
        lax.all_gather(w_key, "dp", axis=0, tiled=True),
        lax.all_gather(w_value, "dp", axis=0, tiled=True),
        lax.all_gather(w_attn_out, "dp", axis=0, tiled=True),
        lax.all_gather(w_in, "dp", axis=0, tiled=True),
        lax.all_gather(w_ff_out, "dp", axis=0, tiled=True),
    )
    wq_full, wk_full, wv_full, wo_full, win_full, wff_full = gathered
    grad_out = cotangent.astype(jnp.float32).reshape(row_count, width)
    grad_branch = grad_out.astype(jnp.bfloat16)
    g_ff_out = jnp.einsum("rf,rd->fd", activated, grad_branch, preferred_element_type=jnp.float32)
    grad_act = jnp.einsum("rd,fd->rf", grad_branch, wff_full, preferred_element_type=jnp.float32)
    _, gelu_pull = jax.vjp(jax.nn.gelu, up_rows)
    grad_up = gelu_pull(grad_act)[0].astype(jnp.bfloat16)
    g_in = jnp.einsum("rd,rf->df", normed_ffn, grad_up, preferred_element_type=jnp.float32)
    grad_normed_ffn = jnp.einsum("rf,df->rd", grad_up, win_full, preferred_element_type=jnp.float32)
    _, ffn_pull = jax.vjp(rms_norm, hidden, ffn_gain)
    grad_hidden_norm, g_ffn_gain = ffn_pull(grad_normed_ffn)
    grad_hidden = grad_out + grad_hidden_norm
    grad_attn = grad_hidden.astype(jnp.bfloat16)
    g_attn_out = jnp.einsum("rd,re->de", mixed_rows, grad_attn, preferred_element_type=jnp.float32)
    grad_mixed = jnp.einsum("re,de->rd", grad_attn, wo_full, preferred_element_type=jnp.float32)
    grad_mixed = grad_mixed.astype(jnp.bfloat16).reshape(n_pass, local_rows, n_heads, head_dim)
    score_sum, (grad_query, grad_key, grad_value) = attend_backward(
        query_local, key_four, value_four, grad_mixed, log_total, key_valid, bias_rows
    )
    grad_key, grad_value = (
        lax.psum_scatter(
            grad_key.reshape(n_pass, full_len, width).astype(jnp.bfloat16),
            "seq",
            scatter_dimension=1,
            tiled=True,
        ).astype(jnp.float32),
        lax.psum_scatter(
            grad_value.reshape(n_pass, full_len, width).astype(jnp.bfloat16),
            "seq",
            scatter_dimension=1,
            tiled=True,
        ).astype(jnp.float32),
    )
    grad_query = grad_query.reshape(row_count, width)
    grad_key = grad_key.astype(jnp.bfloat16).reshape(row_count, width)
    grad_value = grad_value.astype(jnp.bfloat16).reshape(row_count, width)
    g_table = jnp.einsum("qkb,hqk->bh", one_hot, score_sum, precision=HIGH)
    g_query = jnp.einsum("rd,re->de", normed, grad_query, preferred_element_type=jnp.float32)
    g_key = jnp.einsum("rd,re->de", normed, grad_key, preferred_element_type=jnp.float32)
    g_value = jnp.einsum("rd,re->de", normed, grad_value, preferred_element_type=jnp.float32)
    grad_normed = jnp.einsum("re,de->rd", grad_query, wq_full, preferred_element_type=jnp.float32)
    grad_normed = grad_normed + jnp.einsum(
        "re,de->rd", grad_key, wk_full, preferred_element_type=jnp.float32
    )
    grad_normed = grad_normed + jnp.einsum(
        "re,de->rd", grad_value, wv_full, preferred_element_type=jnp.float32
    )
    _, attn_pull = jax.vjp(rms_norm, inputs, attn_gain)
    grad_inputs_norm, g_attn_gain = attn_pull(grad_normed)
    grad_input = (
        (grad_hidden + grad_inputs_norm).astype(jnp.bfloat16).reshape(n_pass, local_rows, width)
    )
    row_grads = (
        lax.psum_scatter(g_query, "dp", scatter_dimension=0, tiled=True),
        lax.psum_scatter(g_key, "dp", scatter_dimension=0, tiled=True),
        lax.psum_scatter(g_value, "dp", scatter_dimension=0, tiled=True),
        lax.psum_scatter(g_attn_out, "dp", scatter_dimension=0, tiled=True),
        lax.psum_scatter(g_in, "dp", scatter_dimension=0, tiled=True),
        lax.psum_scatter(g_ff_out, "dp", scatter_dimension=0, tiled=True),
    )
    row_grads = (
        lax.psum(row_grads[0].astype(jnp.bfloat16), "seq").astype(jnp.float32),
        lax.psum(row_grads[1].astype(jnp.bfloat16), "seq").astype(jnp.float32),
        lax.psum(row_grads[2].astype(jnp.bfloat16), "seq").astype(jnp.float32),
        lax.psum(row_grads[3].astype(jnp.bfloat16), "seq").astype(jnp.float32),
        lax.psum(row_grads[4].astype(jnp.bfloat16), "seq").astype(jnp.float32),
        lax.psum(row_grads[5].astype(jnp.bfloat16), "seq").astype(jnp.float32),
    )
    small_sums = lax.psum((g_attn_gain, g_ffn_gain, g_table), ("dp", "seq"))
    layer_out = output_rows.astype(jnp.bfloat16).reshape(n_pass, local_rows, width)
    return (
        layer_out,
        pooled,
        grad_input,
        small_sums[0],
        row_grads[0],
        row_grads[1],
        row_grads[2],
        row_grads[3],
        small_sums[2],
        small_sums[1],
        row_grads[4],
        row_grads[5],
    )


DP, SEQ = 8, 4
FAR, EVENTS = 4, 7
BF, F32 = jnp.bfloat16, jnp.float32
MESH_ID = pl.DeviceIdType.MESH
TOKENS, WIDTH, HIDDEN, HEAD_N = 512, 768, 3072, 12
PAIRS = HEAD_N // 2
GELU_A, GELU_B = math.sqrt(2 / math.pi), 0.044715


AG, CR, BEGIN, RS, HALF, GO, XC, SHARE_A, FIN_B, FSUM, HOP, LEAVE = range(12)
(
    AT_A1, AT_NORM, AT_ATT, AT_WO, AT_IN, AT_COTW, AT_MFF, AT_FF, AT_FNORM, AT_PREWO, AT_GWO, AT_GMIX, AT_LAY,
    AT_GX, AT_TAIL, AT_PROJECT, AT_ATTEND, AT_RESIDUAL, AT_WIDEN, AT_GFF, AT_GUP, AT_GIN, AT_GNF, AT_NARROW, AT_AB,
    AT_GN,
) = range(26)
PLAN = {
    AT_A1: (
        (AG, 2, 0), (AG, 2, 4), (AG, 1, 0), (AG, 1, 4), (AG, 0, 0), (AG, 0, 4), (AG, 2, 1), (AG, 2, 5), (AG, 1, 1),
        (AG, 1, 5), (AG, 0, 1), (AG, 0, 5), (AG, 2, 2),
    ),
    AT_NORM: (
        (AG, 2, 6),
    ),
    AT_ATT: (
        (CR, 2, 0), (AG, 1, 2), (CR, 2, 4), (AG, 1, 6), (CR, 2, 1), (AG, 0, 2), (BEGIN, 3), (BEGIN, 1), (CR, 2, 5),
        (AG, 0, 6), (AG, 2, 3), (CR, 2, 2), (AG, 1, 3), (CR, 2, 6), (AG, 0, 3), (AG, 7, 0), (CR, 2, 3), (AG, 7, 4),
    ),
    (AT_PROJECT, 0): (
        (AG, 4, 0), (AG, 4, 4),
    ),
    (AT_PROJECT, 2): (
        (AG, 3, 0),
    ),
    (AT_ATTEND, 0): (
        (AG, 3, 4), (AG, 7, 1),
    ),
    (AT_ATTEND, 1): (
        (AG, 7, 5), (AG, 4, 1),
    ),
    (AT_ATTEND, 2): (
        (AG, 4, 5), (AG, 3, 1),
    ),
    (AT_ATTEND, 3): (
        (AG, 3, 5), (AG, 7, 2),
    ),
    (AT_ATTEND, 4): (
        (AG, 7, 6), (AG, 4, 2), (CR, 4, 0),
    ),
    (AT_ATTEND, 5): (
        (AG, 4, 6), (CR, 4, 4), (AG, 3, 2), (BEGIN, 2),
    ),
    AT_WO: (
        (CR, 4, 1), (AG, 3, 6), (AG, 7, 3), (CR, 4, 5), (AG, 4, 3),
    ),
    (AT_RESIDUAL, 0): (
        (CR, 4, 2),
    ),
    (AT_RESIDUAL, 1): (
        (AG, 3, 3),
    ),
    AT_IN: (
        (AG, 6, 0), (CR, 4, 6), (AG, 6, 4), (CR, 4, 3), (AG, 5, 0),
    ),
    (AT_WIDEN, 0): (
        (AG, 5, 4), (AG, 6, 1), (CR, 6, 0),
    ),
    (AT_WIDEN, 1): (
        (AG, 6, 5),
    ),
    (AT_WIDEN, 2): (
        (AG, 5, 1), (CR, 6, 4),
    ),
    (AT_WIDEN, 3): (
        (AG, 5, 5),
    ),
    (AT_GFF, 0): (
        (AG, 6, 2), (CR, 6, 1),
    ),
    (AT_GFF, 1): (
        (AG, 6, 6),
    ),
    (AT_GFF, 2): (
        (AG, 5, 2), (CR, 6, 5),
    ),
    (AT_GFF, 3): (
        (AG, 5, 6), (HALF, 0, 0), (LEAVE, 0),
    ),
    AT_MFF: (
        (AG, 6, 3), (HALF, 0, 1), (CR, 6, 2), (HALF, 0, 2), (LEAVE, 4), (AG, 5, 3), (CR, 6, 6), (HALF, 0, 3), (GO, 0),
        (RS, 0, 0),
    ),
    AT_FF: (
        (RS, 1, 0), (CR, 6, 3), (RS, 0, 4),
    ),
    (AT_GUP, 0): (
        (RS, 1, 4), (RS, 0, 1),
    ),
    (AT_GUP, 2): (
        (RS, 1, 1),
    ),
    (AT_GUP, 3): (
        (RS, 0, 5),
    ),
    (AT_GIN, 1): (
        (RS, 1, 5),
    ),
    (AT_GIN, 2): (
        (RS, 0, 2),
    ),
    (AT_GIN, 3): (
        (RS, 1, 2),
    ),
    (AT_GNF, 0): (
        (XC, 0), (RS, 0, 6), (HALF, 1, 0),
    ),
    (AT_GNF, 1): (
        (RS, 1, 6), (HALF, 1, 1),
    ),
    (AT_GNF, 2): (
        (RS, 0, 3), (HALF, 1, 2),
    ),
    (AT_GNF, 3): (
        (RS, 1, 3), (SHARE_A, 0), (HALF, 1, 3), (GO, 1), (RS, 2, 0), (RS, 2, 4),
    ),
    (AT_NARROW, 0): (
        (RS, 3, 0),
    ),
    (AT_NARROW, 1): (
        (RS, 3, 4), (HALF, 2, 3), (GO, 5),
    ),
    (AT_NARROW, 2): (
        (RS, 4, 0),
    ),
    (AT_NARROW, 3): (
        (FSUM, 0), (RS, 4, 4),
    ),
    AT_LAY: (
        (RS, 2, 1),
    ),
    (AT_AB, 0): (
        (RS, 2, 5), (RS, 3, 1), (RS, 3, 5),
    ),
    (AT_AB, 1): (
        (RS, 9, 0), (RS, 9, 4), (RS, 4, 1), (RS, 4, 5), (RS, 2, 2),
    ),
    (AT_AB, 2): (
        (RS, 2, 6), (XC, 1), (RS, 3, 2), (RS, 3, 6), (HALF, 2, 0), (GO, 2), (RS, 9, 1),
    ),
    (AT_AB, 3): (
        (RS, 9, 5), (RS, 4, 2), (RS, 4, 6), (RS, 2, 3), (FIN_B, 0), (RS, 5, 0),
    ),
    (AT_AB, 4): (
        (RS, 5, 4), (RS, 3, 3), (RS, 6, 0), (HALF, 2, 1), (GO, 3), (RS, 6, 4),
    ),
    (AT_AB, 5): (
        (RS, 9, 2), (RS, 9, 6), (RS, 4, 3), (SHARE_A, 1), (RS, 5, 1), (RS, 5, 5),
    ),
    (AT_GN, 0): (
        (RS, 6, 1), (RS, 7, 0),
    ),
    (AT_GN, 1): (
        (RS, 7, 4), (RS, 6, 5), (HALF, 2, 2), (GO, 4),
    ),
    AT_GX: (
        (RS, 9, 3), (SHARE_A, 5), (RS, 5, 2),
    ),
    AT_TAIL: (
        (RS, 5, 6), (RS, 6, 2), (RS, 7, 1), (RS, 7, 5), (FSUM, 1), (RS, 6, 6), (RS, 8, 0), (HOP, 0), (RS, 8, 4),
        (RS, 5, 3), (FIN_B, 1), (RS, 6, 3), (SHARE_A, 2), (RS, 7, 2), (RS, 7, 6), (RS, 8, 1), (HOP, 1), (RS, 8, 5),
        (RS, 7, 3), (SHARE_A, 3), (RS, 8, 2), (RS, 8, 6), (FSUM, 5), (HOP, 2), (RS, 8, 3), (SHARE_A, 4), (FSUM, 2),
        (FSUM, 3), (FSUM, 4),
    ),
}

def dg(left, right, on_left, on_right):
    return lax.dot_general(
        left, right, (((on_left,), (on_right,)), ((), ())), preferred_element_type=F32
    )


def exact(left, right, on_left, on_right):
    return lax.dot_general(
        left, right, (((on_left,), (on_right,)), ((), ())), precision=HIGH, preferred_element_type=F32
    )


def ring_dp(place):
    high = place // 4
    return 2 * (place * (1 - high) + (7 - place) * high) + high


def times(start, size, step):
    return pl.ds(pl.multiple_of(start, step), size)


def band_bucket(n_buckets):
    lane = lax.broadcasted_iota(jnp.int32, (n_buckets, 512), 1)
    relative = jnp.where(lane < 384, lane - 128, lane - 640)
    row = lax.broadcasted_iota(jnp.int32, (n_buckets, 512), 0)
    return (bucket_index(relative, n_buckets, MAXDIST) == row).astype(F32)


def layer_kernel(
    x_hbm, cot_hbm, wq_hbm, wk_hbm, wv_hbm, wo_hbm, win_hbm, wff_hbm, lengths, attn_gain, ffn_gain, table,
    out_hbm, gx_hbm, gatt_hbm, gin_hbm, gff_hbm, pool_hbm, small_out,
    watt, win, wff, gin, gff, big, probs, xs, cot, normed, qkv, mixed, nf, hid, acc, band, diag, d_both,
    sib_ff, sib_in, y_ff, y_in, r_ffa, r_ffb, r_ina, r_inb, r_att, f_ff, f_in, f_att, sums, sums_in, spread, pool,
    ag_s, ag_r, sb_s, sb_r, yf_s, yf_r, yb_s, yb_r, rr_s, loc, a2_s, a2_r, hs_s, hs_r, yx_s, yx_r,
    fa_s, fa_r, fb_s, fb_r, fo_s, fo_r, fl, bf_s, bf_r,
):
    dp, sq = lax.axis_index("dp"), lax.axis_index("seq")
    z, x, y, c = dp // 2, dp % 2, sq // 2, sq % 2
    place = x * (7 - z) + (1 - x) * z
    turn = 1 - 2 * c

    def owner(steps):
        return ring_dp((place + steps * turn + 16) % 8)

    sib, yp, ysib = (dp, 2 * y + 1 - c), (dp, 2 * (1 - y) + c), (dp, 2 * (1 - y) + 1 - c)
    peers = (sib, yp, ysib)
    others = [((dp + k) % DP, sq) for k in range(1, DP)]

    def send(src, dst, ss, rs, dev):
        return pltpu.make_async_remote_copy(
            src_ref=src, dst_ref=dst, send_sem=ss, recv_sem=rs, device_id=dev, device_id_type=MESH_ID
        )

    def when(condition, body):
        if isinstance(condition, bool):
            if condition:
                body()
        else:
            pl.when(condition)(body)

    def loop(count, body):
        def step(i, _):
            body(i)
            return 0

        lax.fori_loop(0, count, step, 0)

    barrier = pltpu.get_barrier_semaphore()
    for dev in (*peers, *others):
        pl.semaphore_signal(barrier, inc=1, device_id=dev, device_id_type=MESH_ID)

    r96 = times(96 * dp, 96, 96)
    own = [pltpu.make_async_copy(w, watt.at[i, r96], loc.at[i]) for i, w in enumerate((wq_hbm, wk_hbm, wv_hbm, wo_hbm))]
    for i in range(2):
        own.append(pltpu.make_async_copy(win_hbm.at[pl.ds(48 * i, 48)], win.at[dp, i], loc.at[4 + i]))
    own.append(pltpu.make_async_copy(wff_hbm, wff.at[times(384 * dp, 384, 384)], loc.at[6]))
    mine = times(128 * sq, 128, 128)
    own.append(pltpu.make_async_copy(x_hbm.at[sq], xs.at[mine], loc.at[7]))
    own.append(pltpu.make_async_copy(cot_hbm.at[sq], cot.at[mine], loc.at[8]))
    for copy in own:
        copy.start()
    pl.semaphore_wait(barrier, len(peers) + len(others))

    def swap(k, src_hbm, dst, at):
        dev = peers[k]
        return send(src_hbm.at[dev[1]], dst.at[mine], a2_s.at[at], a2_r.at[at], dev)

    def three(ref, at):
        return send(ref, ref, a2_s.at[at], a2_r.at[at], sib)

    def swap_wait(dst, at):
        three(dst.at[pl.ds(0, 384)], at).wait_recv()

    for k in range(3):
        swap(k, x_hbm, xs, 0).start()

    def piece(ch, d, cc, yy):
        if ch < 3:
            cols = pl.ds(128 + 256 * ch, 256) if ch < 2 else times(640 * yy, 128, 128)
            return watt.at[0:3, times(96 * d + 48 * cc, 48, 48), cols]
        if ch < 5:
            cols = pl.ds(768, 1536) if ch == 3 else times(2304 * yy, 768, 768)
            return win.at[d, cc, :, cols]
        if ch == 7:
            return watt.at[3, times(96 * d + 48 * cc, 48, 48)]
        cols = pl.ds(256, 256) if ch == 5 else times(512 * yy, 256, 256)
        return wff.at[times(384 * d + 192 * cc, 192, 192), cols]

    crossing = (2, 4, 6)
    groups = ((0, 1, 2), (3, 4), (5, 6), (7,))

    def came_from(e):
        ahead = e // FAR
        return (1 - ahead) * (-e - 1) + ahead * (e - 3)

    def side(e):
        return (owner(1 - 2 * (e // FAR)), sq)

    def ring_send(ch, e):
        ahead = e // FAR
        part = piece(ch, owner((1 - ahead) * -e + ahead * (e - FAR)), c, y)
        return send(part, part, ag_s.at[ch], ag_r.at[ch, e], side(e))

    def hand_on(ch, e):
        part = piece(ch, owner(came_from(e)), c, y)
        return send(part, part, sb_s.at[ch], sb_r.at[ch], sib)

    def cross(ch, e):
        part = piece(ch, owner(came_from(e)), c, y)
        return send(part, part, yf_s.at[ch // 2 - 1], yf_r.at[ch // 2 - 1, e], yp)

    def cross_on(ch, e):
        part = piece(ch, owner(came_from(e)), c, 1 - y)
        return send(part, part, yb_s.at[ch // 2 - 1], yb_r.at[ch // 2 - 1], sib)

    def arrive(ch, e):
        part = piece(ch, owner(came_from(e)), c, y)
        send(part, part, ag_s.at[ch], ag_r.at[ch, e], side(e)).wait_recv()
        if e not in (FAR - 1, EVENTS - 1):
            ring_send(ch, e + 1).start()
        if ch in crossing:
            cross(ch, e).start()
        hand_on(ch, e).start()

    def arrive_cross(ch, e):
        part = piece(ch, owner(came_from(e)), c, 1 - y)
        send(part, part, yf_s.at[ch // 2 - 1], yf_r.at[ch // 2 - 1, e], yp).wait_recv()
        cross_on(ch, e).start()

    def seven(ch):
        if ch < 3:
            return watt.at[0:3, pl.ds(0, 336), pl.ds(0, 256 if ch < 2 else 128)]
        if ch < 5:
            return win.at[pl.ds(0, 7), 0, :, pl.ds(0, 1536 if ch == 3 else 768)]
        return watt.at[3, pl.ds(0, 336)] if ch == 7 else wff.at[pl.ds(0, 1344), pl.ds(0, 256)]

    def all_seven(ch, ss, rs, dev):
        return send(seven(ch), seven(ch), ss, rs, dev)

    def settled(group):
        for ch in groups[group]:
            all_seven(ch, sb_s.at[ch], sb_r.at[ch], sib).wait_recv()
            if ch in crossing:
                all_seven(ch, yb_s.at[group], yb_r.at[group], sib).wait_recv()

    def gather_sent(group):
        for ch in groups[group]:
            all_seven(ch, ag_s.at[ch], ag_r.at[ch, 0], sib).wait_send()
            all_seven(ch, sb_s.at[ch], sb_r.at[ch], sib).wait_send()
            if ch in crossing:
                all_seven(ch, yf_s.at[group], yf_r.at[group, 0], yp).wait_send()
                all_seven(ch, yb_s.at[group], yb_r.at[group], sib).wait_send()

    def begin(group):
        for ch in reversed(groups[group]):
            ring_send(ch, 0).start()
            ring_send(ch, FAR).start()

    acts = {AG: arrive, CR: arrive_cross, BEGIN: begin}

    def serve(slot):
        for name, *place in PLAN.get(slot, ()):
            acts[name](*place)

    def serve_at(slot, count, i):
        for k in range(count):
            if (slot, k) in PLAN:

                @pl.when(i == k)
                def _(k=k):
                    serve((slot, k))

    for i in range(4):
        own[i].wait()
    begin(0)

    band[pl.ds(0, HEAD_N), :] = exact(table[...], band_bucket(32), 1, 0)
    gain_a = attn_gain[...].reshape(1, WIDTH)
    gain_f = ffn_gain[...].reshape(1, WIDTH)

    serve(AT_A1)
    own[7].wait()
    swap_wait(xs, 0)
    for i in range(4, 7):
        own[i].wait()

    def norm_rows(b):
        rows = times(128 * b, 128, 128)
        v = xs[rows, :].astype(F32)
        s = lax.rsqrt(jnp.mean(v * v, axis=-1, keepdims=True) + EPS)
        normed[rows, :] = (v * s * gain_a).astype(BF)

    loop(4, norm_rows)

    serve(AT_NORM)
    serve(AT_ATT)
    settled(0)
    for k in range(3):
        swap(k, cot_hbm, cot, 1).start()

    def project(m):
        qkv[m] = dg(normed[...], watt[m], 1, 0).astype(BF)
        serve_at(AT_PROJECT, 3, m)

    loop(3, project)

    count = lengths[sq]
    valid = lax.broadcasted_iota(jnp.int32, (1, TOKENS), 1) < count
    lane = lax.broadcasted_iota(jnp.int32, (1, 128), 1)
    keep = (lane < 64, lane >= 64)

    def only(h, v):
        return jnp.where(keep[h], v, jnp.zeros_like(v))

    def attend(hp):
        cols = times(128 * hp, 128, 128)
        key, value = qkv[1, :, cols], qkv[2, :, cols]
        total = [None] * 4
        for h in range(2):
            row = band[pl.ds(2 * hp + h, 1), :]
            tilted = pltpu.roll(jnp.broadcast_to(row, (128, 512)), 0, 1, stride=1, stride_axis=0)
            before = jnp.broadcast_to(row[:, 384:], (128, 128))
            after = jnp.broadcast_to(row[:, 256:384], (128, 128))
            value_h = only(h, value)
            for ib in range(4):
                rows = pl.ds(128 * ib, 128)
                blocks = []
                for jb in range(4):
                    off = jb - ib
                    if off < -1:
                        blocks.append(before)
                    elif off > 1:
                        blocks.append(after)
                    else:
                        blocks.append(tilted[:, 128 * (off + 1) : 128 * (off + 2)])
                scores = dg(only(h, qkv[0, rows, cols]), key, 1, 1) + jnp.concatenate(blocks, axis=1)
                scores = jnp.where(valid, scores, FLOOR)
                top = jnp.max(scores, axis=-1, keepdims=True)
                expo = jnp.exp(scores - top)
                part = jnp.sum(expo, axis=-1, keepdims=True)
                low = (expo * (1.0 / part)).astype(BF)
                probs[2 * hp + h, rows, :] = low
                one = dg(low, value_h, 1, 0)
                total[ib] = one if h == 0 else total[ib] + one
        for ib in range(4):
            mixed[pl.ds(128 * ib, 128), cols] = total[ib].astype(BF)
        serve_at(AT_ATTEND, PAIRS, hp)

    loop(PAIRS, attend)
    serve(AT_WO)
    settled(3)

    def residual(b):
        rows = times(256 * b, 256, 256)
        v = xs[rows, :].astype(F32) + dg(mixed[rows, :], watt[3], 1, 0)
        hid[rows, :] = v
        s = lax.rsqrt(jnp.mean(v * v, axis=-1, keepdims=True) + EPS)
        nf[rows, :] = (v * s * gain_f).astype(BF)
        serve_at(AT_RESIDUAL, 2, b)

    loop(2, residual)

    serve(AT_IN)
    settled(1)
    up_rows, down_rows = pl.ds(0, TOKENS), pl.ds(TOKENS, TOKENS)

    def block(j):
        return times(768 * j, 768, 768)

    def win_block(j):
        return win[:, :, :, block(j)].reshape(768, 768)

    def widen(j):
        v = dg(nf[...], win_block(j), 1, 0)
        sq_v = v * v
        t = jnp.tanh(v * (GELU_A + (GELU_A * GELU_B) * sq_v))
        half = 0.5 + 0.5 * t
        big[j, up_rows, :] = (v * half).astype(BF)
        slope = half + (v * half) * (1.0 - t) * (GELU_A + (3 * GELU_A * GELU_B) * sq_v)
        big[j, down_rows, :] = slope.astype(BF)
        serve_at(AT_WIDEN, 4, j)

    loop(4, widen)
    serve(AT_COTW)
    own[8].wait()
    swap_wait(cot, 1)

    def chunk(i):
        return (3 - z + (i + 1) // 2 + 2 * (i % 2) * (1 - i // 2)) % 4

    def half_ff(i):
        two = pl.ds(2 * chunk(i), 2)
        src = gff.at[two, times(192 * (1 - c), 192, 192)]
        return send(src, sib_ff.at[two], hs_s.at[0], hs_r.at[0, i], sib)

    def grad_ff(i):
        j = chunk(i)
        v = dg(big[j, up_rows, :], cot[...], 0, 0).astype(BF)
        gff[pl.ds(2 * j, 2)] = v.reshape(2, 384, 768)
        half_ff(i).start()
        serve_at(AT_GFF, 4, i)


    def merge_ff(i):
        j = chunk(i)
        half_ff(i).wait_recv()
        rows = times(192 * c, 192, 192)
        for i in range(2):
            gff[2 * j + i, rows] = (gff[2 * j + i, rows].astype(F32) + sib_ff[2 * j + i].astype(F32)).astype(BF)

    def cross_src(g, yy):
        if g == 0:
            return gff.at[:, times(192 * c + 160 * yy, 32, 32)]
        return gin.at[:, times(1536 * c + 1280 * yy, 256, 256)]

    cross_dst = (y_ff, y_in)

    def cross_sum(g):
        return send(cross_src(g, 1 - y), cross_dst[g], yx_s.at[g], yx_r.at[g], yp)

    def add_cross(g):
        cross_sum(g).wait()
        here, came = cross_src(g, y), cross_dst[g]
        here[...] = (here[...].astype(F32) + came[...].astype(F32)).astype(BF)

    def rs_piece(ch, d, yy):
        if ch < 3:
            rows = times(192 * c + 32 + 64 * ch, 64, 32) if ch < 2 else times(192 * c + 160 * yy, 32, 32)
            return gff.at[d, rows]
        if ch < 5:
            return gin.at[times(96 * d, 96, 96), times(1536 * c + 256 + 512 * (ch - 3), 512, 256)]
        if ch == 5:
            return gin.at[times(96 * d, 96, 96), times(1536 * c + 1280 * yy, 256, 256)]
        return win.at[d, c, :, pl.ds(768 * (ch - 6), 768)]

    landing = [r_ffa.at[0], r_ffa.at[1], r_ffb, r_ina.at[0], r_ina.at[1], r_inb, r_att.at[0]]
    landing += [r_ffa.at[0, :, pl.ds(0, 48)], r_ffa.at[1, :, pl.ds(0, 48)], r_att.at[1]]

    def rs_send(ch, e):
        ahead = e // FAR
        part = rs_piece(ch, owner((1 - ahead) * (FAR - e) + ahead * (e - EVENTS)), y)
        return send(part, landing[ch].at[e], rr_s.at[ch], ag_r.at[ch, e], side(e))

    def rs_begin(ch):
        rs_send(ch, 0).start()
        rs_send(ch, FAR).start()

    def rs_event(ch, e):
        rs_send(ch, e).wait_recv()
        here = rs_piece(ch, owner(FAR - 1 - e if e < FAR else e - EVENTS + 1), y)
        here[...] = (here[...].astype(F32) + landing[ch][e].astype(F32)).astype(BF)
        if e not in (FAR - 1, EVENTS - 1):
            rs_send(ch, e + 1).start()

    def half_in(k):
        src = gin.at[:, times(1536 * (1 - c) + 384 * k, 384, 384)]
        return send(src, sib_in.at[k], hs_s.at[1], hs_r.at[1, k], sib)

    def merge_in(k):
        half_in(k).wait_recv()
        cols = times(1536 * c + 384 * k, 384, 384)
        gin[:, cols] = (gin[:, cols].astype(F32) + sib_in[k].astype(F32)).astype(BF)

    def sib_rows(t):
        return sib_ff.at[:, times(48 * t, 48, 48)]

    def half_att(t):
        return send(win.at[:, 1 - c, :, block(t)], sib_rows(t), hs_s.at[2], hs_r.at[2, t], sib)

    def merge_att(t):
        half_att(t).wait_recv()
        win[:, c, :, block(t)] = (win[:, c, :, block(t)].astype(F32) + sib_rows(t)[...].astype(F32)).astype(BF)

    final = [f_ff, f_in] + [f_att.at[t] for t in range(4)]

    def own_piece(g):
        if g == 0:
            return gff.at[dp, times(192 * c + 32, 128, 32)]
        if g == 1:
            return gin.at[r96, times(1536 * c + 256, 1024, 256)]
        return rs_piece(4 + g, dp, y)

    def out_piece(g, cc, yy):
        if g == 0:
            return gff_hbm.at[times(192 * cc + 32, 128, 32) if yy is None else times(192 * cc + 160 * yy, 32, 32)]
        if g == 1:
            if yy is None:
                return gin_hbm.at[:, times(1536 * cc + 256, 1024, 256)]
            return gin_hbm.at[:, times(1536 * cc + 1280 * yy, 256, 256)]
        return gatt_hbm.at[g - 2, times(48 * cc, 48, 48)]

    def share_a(g):
        return send(own_piece(g), final[g], fa_s.at[g], fa_r.at[g], yp)

    def share_b(g, k):
        return send(rs_piece(3 * g + 2, dp, y), out_piece(g, c, y), fb_s.at[g], fb_r.at[g], peers[k])

    def share_sum(g):
        return send(final[g], out_piece(g, c, None), fo_s.at[g], fo_r.at[g], sib)

    def keep_b(g):
        return pltpu.make_async_copy(rs_piece(3 * g + 2, dp, y), out_piece(g, c, y), fl.at[g, 0])

    def keep_sum(g):
        return pltpu.make_async_copy(final[g], out_piece(g, c, None), fl.at[g, 1])

    def finish_b(g):
        for k in range(3):
            share_b(g, k).start()
        keep_b(g).start()

    def finish_sum(g):
        share_a(g).wait()
        final[g][...] = (final[g][...].astype(F32) + own_piece(g)[...].astype(F32)).astype(BF)
        share_sum(g).start()
        keep_sum(g).start()

    def hop(k):
        return send(sums.at[k], sums_in.at[k], bf_s.at[k], bf_r.at[k], (yp, sib)[k])

    def hop_on(k):
        if k < 2:
            hop(k).wait()
            sums[k + 1] = sums[k] + sums_in[k]
        if k == 0:
            hop(1).start()
        elif k == 1:
            for dev in others:
                send(sums.at[2], spread.at[dp], bf_s.at[2], bf_r.at[2], dev).start()
            spread[dp] = sums[2]
        else:
            send(spread.at[pl.ds(0, 7)], spread.at[pl.ds(0, 7)], bf_s.at[2], bf_r.at[2], sib).wait()
            total = spread[0]
            for k in range(1, DP):
                total = total + spread[k]
            small_out[...] = total

    def merge(g, k):
        (merge_ff, merge_in, merge_att)[g](k)

    def go(g):
        if g == 0:
            cross_sum(0).start()
        elif g == 1:
            cross_sum(1).start()
            rs_begin(3)
            rs_begin(4)
        else:
            rs_begin(4 + g)

    def leave(e):
        for ch in range(2):
            rs_send(ch, e).start()

    def cross_in(g):
        add_cross(g)
        rs_begin(3 * g + 2)

    acts |= {
        RS: rs_event, HALF: merge, GO: go, LEAVE: leave, XC: cross_in, SHARE_A: lambda g: share_a(g).start(), FIN_B: finish_b,
        FSUM: finish_sum, HOP: hop_on,
    }

    loop(4, grad_ff)
    serve(AT_MFF)
    serve(AT_FF)
    settled(2)

    def grad_up(j):
        v = dg(cot[...], wff[block(j), :], 1, 1) * big[j, down_rows, :].astype(F32)
        big[j, down_rows, :] = v.astype(BF)
        serve_at(AT_GUP, 4, j)

    loop(4, grad_up)

    def grad_in(i):
        j = (2 * (1 - c) + i) % 4
        gin[:, block(j)] = dg(nf[...], big[j, down_rows, :], 0, 0).astype(BF)

        @pl.when(i == 1)
        def _():
            for k in range(4):
                half_in(k).start()

        serve_at(AT_GIN, 4, i)

    loop(4, grad_in)

    def norm_back(v, gain, grad):
        s = lax.rsqrt(jnp.mean(v * v, axis=-1, keepdims=True) + EPS)
        scaled = grad * gain
        back = s * scaled - v * (s * s * s) * jnp.mean(v * scaled, axis=-1, keepdims=True)
        return back, jnp.sum(grad * v * s, axis=0, keepdims=True)

    def ffn_norm_back(b, total):
        rows, down = times(256 * b, 256, 256), times(TOKENS + 256 * b, 256, 256)
        grad = dg(big[0, down, :], win_block(0), 1, 1)
        for j in range(1, 4):
            grad = grad + dg(big[j, down, :], win_block(j), 1, 1)
        back, part = norm_back(hid[rows, :], gain_f, grad)
        grad = cot[rows, :].astype(F32) + back
        acc[rows, :] = grad
        cot[rows, :] = grad.astype(BF)
        serve_at(AT_GNF, 4, 2 * b)
        serve_at(AT_GNF, 4, 2 * b + 1)
        return total + part

    g_ffn_gain = lax.fori_loop(0, 2, ffn_norm_back, jnp.zeros((1, WIDTH), F32))

    serve(AT_FNORM)
    serve(AT_PREWO)
    gather_sent(1)
    win[:, :, :, block(3)] = dg(mixed[...], cot[...], 0, 0).astype(BF).reshape(8, 2, 48, 768)

    half_att(3).start()
    serve(AT_GWO)
    nf[...] = dg(cot[...], watt[3], 1, 1).astype(BF)
    serve(AT_GMIX)


    def give(src, dst_hbm, at, k):
        dev = peers[k]
        return send(src.at[times(128 * dev[1], 128, 128)], dst_hbm.at[sq], a2_s.at[at], a2_r.at[at], dev)

    def pool_send(k):
        return send(pool, pool_hbm.at[sq], a2_s.at[4], a2_r.at[4], peers[k])

    pool_own = pltpu.make_async_copy(pool, pool_hbm.at[sq], loc.at[2])
    lay = big.at[0, up_rows]
    lay_own = pltpu.make_async_copy(lay.at[mine], out_hbm.at[sq], loc.at[1])
    def narrow(j):
        part = dg(big[j, up_rows, :], wff[block(j), :], 1, 0)
        hid[...] += part
        serve_at(AT_NARROW, 4, j)

    loop(4, narrow)
    lay[...] = hid[...].astype(BF)
    for k in range(3):
        give(lay, out_hbm, 2, k).start()
    lay_own.start()
    here_t = lax.broadcasted_iota(jnp.int32, (TOKENS, 1), 0) < count
    mean = jnp.sum(jnp.where(here_t, hid[...], 0.0), axis=0, keepdims=True) / count.astype(F32)
    pool[...] = jnp.broadcast_to(mean, (8, WIDTH))
    pool_own.start()
    for k in range(3):
        pool_send(k).start()
    serve(AT_LAY)

    flip_sum = lax.broadcasted_iota(jnp.int32, (128, 128), 0) + lax.broadcasted_iota(jnp.int32, (128, 128), 1)
    flip = (flip_sum == 127).astype(F32).astype(BF)

    def flipped(v):
        high = v.astype(BF)
        return dg(flip, high, 1, 0) + dg(flip, (v - high.astype(F32)).astype(BF), 1, 0)

    def attend_back(hp):
        cols = times(128 * hp, 128, 128)
        key, value = qkv[1, :, cols], qkv[2, :, cols]
        query, grad = qkv[0, :, cols], nf[:, cols]
        g_query = [None] * 4
        for h in range(2):
            key_h = only(h, key)
            before = after = jnp.zeros((128, 128), F32)
            near = [jnp.zeros((128, 128), F32) for _ in range(3)]
            for ib in range(4):
                rows = pl.ds(128 * ib, 128)
                wide = probs[2 * hp + h, rows, :].astype(F32)
                d_probs = dg(only(h, nf[rows, cols]), value, 1, 1)
                mean_d = jnp.sum(wide * d_probs, axis=-1, keepdims=True)
                d_score = wide * (d_probs - mean_d)
                for jb in range(4):
                    off, part = jb - ib, d_score[:, 128 * jb : 128 * (jb + 1)]
                    if off < -1:
                        before = before + part
                    elif off > 1:
                        after = after + part
                    else:
                        near[off + 1] = near[off + 1] + part
                d_low = d_score.astype(BF)
                d_both[pl.ds(512 * h + 128 * ib, 128), :] = d_low
                one = dg(d_low, key_h, 1, 0)
                g_query[ib] = one if h == 0 else g_query[ib] + one
            tilted = flipped(jnp.concatenate(near, axis=1))
            tilted = jnp.concatenate([tilted, jnp.zeros((128, 128), F32)], axis=1)
            flat = jnp.sum(pltpu.roll(tilted, 385, 1, stride=1, stride_axis=0), axis=0, keepdims=True)
            far = jnp.concatenate(
                [
                    jnp.zeros((1, 256), F32),
                    jnp.sum(after, axis=0, keepdims=True),
                    jnp.sum(before, axis=0, keepdims=True),
                ],
                axis=1,
            )
            diag[pl.ds(2 * hp + h, 1), :] = flat + far
        both_query = jnp.concatenate([only(0, query), only(1, query)], axis=0)
        both_grad = jnp.concatenate([only(0, grad), only(1, grad)], axis=0)
        qkv[1, :, cols] = dg(d_both[...], both_query, 0, 0).astype(BF)
        qkv[2, :, cols] = dg(probs[pl.ds(2 * hp, 2)].reshape(1024, 512), both_grad, 0, 0).astype(BF)
        for ib in range(4):
            qkv[0, pl.ds(128 * ib, 128), cols] = g_query[ib].astype(BF)

        @pl.when(hp % 2 == 1)
        def _():
            t = hp // 2
            three = times(256 * t, 256, 256)
            grads = jnp.concatenate([qkv[0, :, three], qkv[1, :, three], qkv[2, :, three]], axis=1)
            win[:, :, :, block(t)] = dg(normed[...], grads, 0, 0).astype(BF).reshape(8, 2, 48, 768)
            half_att(t).start()

        serve_at(AT_AB, PAIRS, hp)

    loop(PAIRS, attend_back)
    def attn_norm_back(b, total):
        rows = times(256 * b, 256, 256)
        grad = dg(qkv[0, rows, :], watt[0], 1, 1) + dg(qkv[1, rows, :], watt[1], 1, 1) + dg(qkv[2, rows, :], watt[2], 1, 1)
        back, part = norm_back(xs[rows, :].astype(F32), gain_a, grad)
        mixed[rows, :] = (acc[rows, :] + back).astype(BF)
        serve_at(AT_GN, 2, b)
        return total + part

    g_attn_gain = lax.fori_loop(0, 2, attn_norm_back, jnp.zeros((1, WIDTH), F32))

    sums[0] = jnp.zeros((32, 128), F32)
    sums[0, 0:16, 0:32] = exact(diag[...], band_bucket(32), 1, 1)
    for k in range(6):
        sums[0, 16 + k : 17 + k, :] = g_attn_gain[:, 128 * k : 128 * (k + 1)]
        sums[0, 22 + k : 23 + k, :] = g_ffn_gain[:, 128 * k : 128 * (k + 1)]

    hop(0).start()
    for k in range(3):
        give(mixed, gx_hbm, 3, k).start()
    gx_own = pltpu.make_async_copy(mixed.at[mine], gx_hbm.at[sq], loc.at[0])
    gx_own.start()
    serve(AT_GX)
    serve(AT_TAIL)

    for g in range(6):
        if g < 2:
            keep_b(g).wait()
            same = (sib_ff.at[pl.ds(0, 3), pl.ds(0, 32)], gin.at[pl.ds(0, 288), pl.ds(0, 256)])[g]
            send(same, same, fb_s.at[g], fb_r.at[g], sib).wait()
        keep_sum(g).wait()
        share_sum(g).wait_send()
        came = out_piece(g, 1 - c, None)
        send(came, came, fo_s.at[g], fo_r.at[g], sib).wait_recv()
    for ch in range(10):
        send(landing[ch], landing[ch], rr_s.at[ch], ag_r.at[ch, 0], sib).wait_send()
    for g, same in enumerate((sib_ff, sib_in, sib_ff)):
        send(same, same, hs_s.at[g], hs_r.at[g, 0], sib).wait_send()
    gather_sent(0)
    gather_sent(2)
    gather_sent(3)
    three(out_hbm.at[pl.ds(0, 3)], 2).wait()
    three(gx_hbm.at[pl.ds(0, 3)], 3).wait()
    three(pool_hbm.at[pl.ds(0, 3)], 4).wait()
    three(xs.at[pl.ds(0, 384)], 0).wait_send()
    three(cot.at[pl.ds(0, 384)], 1).wait_send()
    lay_own.wait()
    gx_own.wait()
    pool_own.wait()


def finish_kernel(
    out_in, gx_in, att_in, in_in, ff_in, pool_in, small_in,
    out, gx, pool_out, gain_a, gq, gk, gv, go, g_table, gain_f, gin_out, gff_out,
    v_out, v_gx, v_att, v_in, v_ff, v_pool, w_att, w_in, w_ff, w_pool, sem_in, sem_out,
):
    sources = (in_in, ff_in, att_in, pool_in, out_in, gx_in)
    held = (v_in, v_ff, v_att, v_pool, v_out, v_gx)
    reads = [pltpu.make_async_copy(a, b, sem_in.at[k]) for k, (a, b) in enumerate(zip(sources, held))]
    for read in reads:
        read.start()
    g_table[...] = small_in[0:HEAD_N, 0:32]
    for k in range(6):
        gain_a[128 * k : 128 * (k + 1)] = small_in[16 + k : 17 + k, :].reshape(128)
        gain_f[128 * k : 128 * (k + 1)] = small_in[22 + k : 23 + k, :].reshape(128)
    writes = []

    def write(src, dst):
        writes.append(pltpu.make_async_copy(src, dst, sem_out.at[len(writes)]))
        writes[-1].start()

    reads[0].wait()
    w_in[...] = v_in[...].astype(F32)
    write(w_in, gin_out)
    reads[1].wait()
    w_ff[...] = v_ff[...].astype(F32)
    write(w_ff, gff_out)
    reads[2].wait()
    w_att[3] = v_att[3].astype(F32)
    for t in range(3):
        for i in range(3):
            w_att[i, :, 256 * t : 256 * (t + 1)] = v_att[t, :, 256 * i : 256 * (i + 1)].astype(F32)
    for i, ref in enumerate((gq, gk, gv, go)):
        write(w_att.at[i], ref)
    reads[3].wait()
    for p in range(SEQ):
        w_pool[p : p + 1, :] = v_pool[p, 0:1, :]
    write(w_pool, pool_out)
    reads[4].wait()
    write(v_out, out)
    reads[5].wait()
    write(v_gx, gx)
    for copy in writes:
        copy.wait()


def passage_shards(
    passages, lengths, attn_gain, w_query, w_key, w_value, w_attn_out, bias_table, ffn_gain, w_in, w_ff_out, cotangent
):
    any_space = pl.BlockSpec(memory_space=pl.ANY)
    vmem = pl.BlockSpec(memory_space=pltpu.VMEM)
    dma = pltpu.SemaphoreType.DMA
    scratch = [
        pltpu.VMEM(shape, BF)
        for shape in (
            (4, 768, 768), (8, 2, 48, 3072), (3072, 768), (768, 3072), (8, 384, 768), (4, 1024, 768), (12, 512, 512),
            (512, 768), (512, 768), (512, 768), (3, 512, 768), (512, 768), (512, 768),
        )
    ]
    scratch += [pltpu.VMEM(shape, F32) for shape in ((512, 768), (512, 768), (16, 512), (16, 512))]
    scratch += [
        pltpu.VMEM(shape, BF)
        for shape in (
            (1024, 512), (8, 192, 768), (4, 768, 384), (8, 32, 768), (768, 256),
            (2, 7, 64, 768), (7, 32, 768), (2, 7, 96, 512), (7, 96, 256), (2, 7, 48, 768),
            (128, 768), (96, 1024), (4, 48, 768),
        )
    ]
    scratch += [pltpu.VMEM((n, 32, 128), F32) for n in (3, 2, DP)]
    scratch.append(pltpu.VMEM((8, 768), F32))
    scratch += [
        dma(shape)
        for shape in (
            (8,), (10, 7), (8,), (8,), (3,), (3, 7), (3,), (3,), (10,), (9,), (5,), (5,), (3,), (3, 4), (2,), (2,),
            (6,), (6,), (2,), (2,), (6,), (6,), (6, 2), (3,), (3,),
        )
    ]
    sums = pl.pallas_call(
        layer_kernel,
        out_shape=(
            jax.ShapeDtypeStruct((4, 128, 768), BF),
            jax.ShapeDtypeStruct((4, 128, 768), BF),
            jax.ShapeDtypeStruct((4, 96, 768), BF),
            jax.ShapeDtypeStruct((96, 3072), BF),
            jax.ShapeDtypeStruct((384, 768), BF),
            jax.ShapeDtypeStruct((4, 8, 768), F32),
            jax.ShapeDtypeStruct((32, 128), F32),
        ),
        in_specs=[any_space] * 8 + [pl.BlockSpec(memory_space=pltpu.SMEM)] + [vmem] * 3,
        out_specs=(any_space,) * 6 + (vmem,),
        scratch_shapes=scratch,
        compiler_params=pltpu.CompilerParams(collective_id=0, has_side_effects=True, vmem_limit_bytes=64 * 2**20),
        name="layer",
    )(
        passages, cotangent, w_query, w_key, w_value, w_attn_out, w_in, w_ff_out, lengths,
        attn_gain, ffn_gain, bias_table.T,
    )
    square = jax.ShapeDtypeStruct((96, 768), F32)
    gain = jax.ShapeDtypeStruct((WIDTH,), F32)
    outs = pl.pallas_call(
        finish_kernel,
        out_shape=(
            jax.ShapeDtypeStruct((4, 128, 768), BF),
            jax.ShapeDtypeStruct((4, 128, 768), BF),
            jax.ShapeDtypeStruct((4, 768), F32),
            gain,
            square,
            square,
            square,
            square,
            jax.ShapeDtypeStruct((HEAD_N, 32), F32),
            gain,
            jax.ShapeDtypeStruct((96, 3072), F32),
            jax.ShapeDtypeStruct((384, 768), F32),
        ),
        in_specs=[any_space] * 6 + [vmem],
        out_specs=(any_space,) * 3 + (vmem,) + (any_space,) * 4 + (vmem,) * 2 + (any_space,) * 2,
        scratch_shapes=[
            pltpu.VMEM((4, 128, 768), BF),
            pltpu.VMEM((4, 128, 768), BF),
            pltpu.VMEM((4, 96, 768), BF),
            pltpu.VMEM((96, 3072), BF),
            pltpu.VMEM((384, 768), BF),
            pltpu.VMEM((4, 8, 768), F32),
            pltpu.VMEM((4, 96, 768), F32),
            pltpu.VMEM((96, 3072), F32),
            pltpu.VMEM((384, 768), F32),
            pltpu.VMEM((4, 768), F32),
            dma((6,)),
            dma((9,)),
        ],
        compiler_params=pltpu.CompilerParams(vmem_limit_bytes=64 * 2**20),
        name="finish",
    )(*sums)
    return (outs[0], outs[2], outs[1], *outs[3:8], outs[8].T, *outs[9:])


def solution(mesh):
    ring = (mesh.shape["dp"], mesh.shape["seq"]) == (DP, SEQ)
    return jax.shard_map(
        passage_shards if ring else shards,
        mesh=mesh,
        in_specs=(
            P("dp", "seq", None),
            P("dp"),
            P(),
            P("dp", None),
            P("dp", None),
            P("dp", None),
            P("dp", None),
            P(),
            P(),
            P("dp", None),
            P("dp", None),
            P("dp", "seq", None),
        ),
        out_specs=(
            P("dp", "seq", None),
            P("dp", None),
            P("dp", "seq", None),
            P(),
            P("dp", None),
            P("dp", None),
            P("dp", None),
            P("dp", None),
            P(),
            P(),
            P("dp", None),
            P("dp", None),
        ),
        check_vma=False,
    )
```
